128 devices in a mesh: seq: 8 (over x_lo, z), ctx: 16 (over y, x_hi, core).
Axes of the slice: x: 4 (x_hi: 2, x_lo: 2; x = x_hi * 2 + x_lo), y: 4, z: 4, core: 2. Of those that a mesh axis runs over, the one named last changes fastest.
Arguments:
- block_in: bfloat16 [8, 2048, 1536], P('seq', 'ctx'), may hold values from -6 to 6
- routes: int32 [8, 2048, 8], P('seq', 'ctx'), may hold values from 0 to 31, all different within a row; in each aligned block of 128 rows (0 to 127, 128 to 255, ..., all dimensions but the last counted through in order) at most 48 rows name the same one
- cotangent: bfloat16 [8, 2048, 1536], P('seq', 'ctx'), may hold values from -6 to 6
- gain_attn: bfloat16 [1536], P(('seq', 'ctx')), may hold values from 0.099609375 to 1.8984375
- w_query: bfloat16 [1536, 1536], P(('seq', 'ctx')), may hold values from -0.21875 to 0.21875
- key_weight: bfloat16 [1536, 512], P(('seq', 'ctx')), may hold values from -0.21875 to 0.21875
- value_weight: bfloat16 [1536, 512], P(('seq', 'ctx')), may hold values from -0.15625 to 0.15625
- w_out: bfloat16 [1536, 1536], P(('seq', 'ctx')), may hold values from -1.75 to 1.75
- gain_ffn: bfloat16 [1536], P(('seq', 'ctx')), may hold values from 0.099609375 to 1.8984375
- w_router: bfloat16 [1536, 32], P(('seq', 'ctx')), may hold values from -0.078125 to 0.078125
- w_gate: bfloat16 [32, 1536, 512], P('ctx', 'seq'), may hold values from -0.15625 to 0.15625
- w_up: bfloat16 [32, 1536, 512], P('ctx', 'seq'), may hold values from -0.15625 to 0.15625
- w_down: bfloat16 [32, 512, 1536], P('ctx', 'seq'), may hold values from -1 to 1
Outputs:
- block_out: bfloat16 [8, 2048, 1536], P('seq', 'ctx')
- grad_in: float32 [8, 2048, 1536], P('seq', 'ctx')
- grad_gain_attn: float32 [1536], P(('seq', 'ctx'))
- grad_query: float32 [1536, 1536], P(('seq', 'ctx'))
- key_weight_gradient: float32 [1536, 512], P(('seq', 'ctx'))
- value_weight_gradient: float32 [1536, 512], P(('seq', 'ctx'))
- grad_out: float32 [1536, 1536], P(('seq', 'ctx'))
- grad_gain_ffn: float32 [1536], P(('seq', 'ctx'))
- grad_router: float32 [1536, 32], P(('seq', 'ctx'))
- grad_gate: float32 [32, 1536, 512], P('ctx', 'seq')
- grad_up: float32 [32, 1536, 512], P('ctx', 'seq')
- grad_down: float32 [32, 512, 1536], P('ctx', 'seq')
The draws below stay inside these ranges and needn't reach their ends.
Inputs may be any that keep to these rules, and one draw needn't show every extreme that they name: `routes`: each token names 8 different experts. Within the rows of one device (aligned blocks of 128 tokens) no expert is named by more than 48 tokens, a bound that some block reaches of one device in every draw.
All inputs are finite; a program needn't handle non-finite values.
Results may differ from the reference program's by a relative error of at most 0.02.
The reference program's roundings to bfloat16 on the way count: a program that leaves them out, or rounds other values in their place, can miss the bound.
Values may be sent and summed in bfloat16 or wider, within the bound.
A program may use at most 192 MiB of HBM per device.

```python
import math
import jax
import jax.numpy as jnp
import numpy as np
from jax import lax

MODEL_WIDTH = 1536
QUERY_HEADS = 24
KEY_VALUE_HEADS = 8
HEAD_WIDTH = 64
FF = 512
TOPK = 8
TOK_DEV = 128
EXPERTS = 32
SEQS = 8
LEN = 2048
CAP = 48


def block_levels(stream_key, shape, split, low, high):
    level = 1.0
    for axis_at, parts in split:
        heights = jax.random.uniform(jax.random.fold_in(jax.random.fold_in(stream_key, 6), axis_at), (parts,), jnp.float32, low / len(split), high / len(split))
        level = level * jnp.repeat(jnp.exp(heights), shape[axis_at] // parts).reshape((-1,) + (1,) * (len(shape) - 1 - axis_at))
    return level


def shared_out(own_key, own, number, rows, number_of, top, bound, lean):
    ranking = jax.random.permutation(own_key, number_of)
    packed, common = load_shares(number_of, rows * top, bound, lean, True), load_shares(number_of, rows * top, bound, lean, False)
    places = jnp.arange(number_of)

    def named(tallies, offset_by):
        used = int((tallies > 0).sum())
        fixed = max(1, used // 4)
        shifted = fixed + (places - fixed + offset_by * (used - fixed)) % max(1, number_of - fixed)
        return jnp.zeros((number_of,), jnp.int32).at[ranking[jnp.where(places < fixed, places, shifted)]].set(jnp.asarray(tallies, jnp.int32))

    tallies = jnp.where(number % 4 == 0, named(packed, number // 4), named(common, number - number // 4 - 1))
    mixed = jax.random.permutation(jax.random.fold_in(own, 3), number_of)
    donor, sink = mixed[0:number_of // 2 * 2:2], mixed[1:number_of // 2 * 2:2]
    room = jnp.minimum(tallies[donor] - 1, bound - tallies[sink]) // 2
    room = jnp.where((donor == ranking[0]) | (sink == ranking[0]) | (tallies[sink] == 0), 0, jnp.maximum(room, 0))
    shifted = jax.random.randint(jax.random.fold_in(own, 4), (number_of // 2,), 0, 1 << 20) % (room + 1)
    tallies = tallies.at[donor].add(-shifted).at[sink].add(shifted)
    items = jnp.searchsorted(jnp.cumsum(tallies), jnp.arange(rows * top), side="right").astype(jnp.int32)
    table = items.reshape(top, rows).T
    table = table[jax.random.permutation(jax.random.fold_in(own, 1), rows)]
    offset_by = jax.random.randint(jax.random.fold_in(own, 2), (rows, 1), 0, top)
    return jnp.take_along_axis(table, (jnp.arange(top)[None, :] + offset_by) % top, axis=1)


def load_shares(number_of, total, reach, skew, full):
    weights = [(1 << 20) // math.isqrt(rank ** skew) + 1 for rank in range(1, number_of + 1)]
    largest = reach if full else min(reach, max(-(-total // number_of), total * weights[0] // sum(weights)))
    least = 1 if total - largest >= number_of - 1 else 0
    counts, spare = [largest] + [least] * (number_of - 1), total - largest - least * (number_of - 1)
    while spare > 0:
        candidates = [i for i in range(1, number_of) if counts[i] < largest] or [i for i in range(1, number_of) if counts[i] < reach]
        pool, left = sum([weights[i] for i in candidates]), spare
        for i in candidates:
            addition = min(reach - counts[i], max(1, left * weights[i] // pool), spare)
            counts[i] = counts[i] + addition
            spare = spare - addition
    return np.array(counts)


def normal_values(own_key, dims, width, most, shards=(), held_as=jnp.bfloat16):
    array = jax.random.normal(own_key, dims, jnp.float32) * width
    if len(shards) > 0:
        array = block_levels(own_key, dims, shards, -0.22, 0.18) * array
    return jnp.clip(array, min=-most, max=most).astype(held_as)


def setup_inputs(seed: int = 0) -> dict:
    key_list = jax.random.split(jax.random.key(seed), 14)
    block_in = normal_values(key_list[0], (SEQS, LEN, MODEL_WIDTH), 1.0, 6.0, ((0, 8), (1, 16)))
    routes_keys = jax.random.split(jax.random.fold_in(key_list[1], 1), SEQS * LEN // TOK_DEV)
    routes_turns = jax.random.permutation(jax.random.fold_in(key_list[1], 3), SEQS * LEN // TOK_DEV)
    routes = jax.vmap(lambda own, number: shared_out(jax.random.fold_in(key_list[1], 2), own, number, TOK_DEV, EXPERTS, TOPK, CAP, 2))(routes_keys, routes_turns).reshape((SEQS, LEN, TOPK))
    cotangent = normal_values(key_list[2], (SEQS, LEN, MODEL_WIDTH), 1.0, 6.0, ((0, 8), (1, 16)))
    gain_attn = jnp.clip(1.0 + 0.18 * jax.random.normal(key_list[3], (MODEL_WIDTH,), jnp.float32), 0.099609375, 1.8984375).astype(jnp.bfloat16)
    w_query = normal_values(key_list[4], (MODEL_WIDTH, QUERY_HEADS * HEAD_WIDTH), (MODEL_WIDTH // 2) ** -0.5, 0.21875, ((0, 128),))
    key_weight = normal_values(key_list[5], (MODEL_WIDTH, KEY_VALUE_HEADS * HEAD_WIDTH), (MODEL_WIDTH // 2) ** -0.5, 0.21875, ((0, 128),))
    value_weight = normal_values(key_list[6], (MODEL_WIDTH, KEY_VALUE_HEADS * HEAD_WIDTH), MODEL_WIDTH ** -0.5, 0.15625, ((0, 128),))
    w_out = normal_values(key_list[7], (QUERY_HEADS * HEAD_WIDTH, MODEL_WIDTH), (max(1, QUERY_HEADS * HEAD_WIDTH * 16 // LEN)) ** -0.5, 1.75, ((0, 128),))
    gain_ffn = jnp.clip(1.0 + 0.18 * jax.random.normal(key_list[8], (MODEL_WIDTH,), jnp.float32), 0.099609375, 1.8984375).astype(jnp.bfloat16)
    w_router = normal_values(key_list[9], (MODEL_WIDTH, EXPERTS), (4 * MODEL_WIDTH) ** -0.5, 0.078125, ((0, 128),))
    w_gate = normal_values(key_list[10], (EXPERTS, MODEL_WIDTH, FF), MODEL_WIDTH ** -0.5, 0.15625, ((0, 16), (1, 8)))
    w_up = normal_values(key_list[11], (EXPERTS, MODEL_WIDTH, FF), MODEL_WIDTH ** -0.5, 0.15625, ((0, 16), (1, 8)))
    w_down = normal_values(key_list[12], (EXPERTS, FF, MODEL_WIDTH), (FF // 16) ** -0.5, 1.0, ((0, 16), (1, 8)))
    return dict(block_in=block_in, routes=routes, cotangent=cotangent, gain_attn=gain_attn, w_query=w_query, key_weight=key_weight, value_weight=value_weight, w_out=w_out, gain_ffn=gain_ffn, w_router=w_router, w_gate=w_gate, w_up=w_up, w_down=w_down)


@jax.custom_vjp
def reduced_precision(v):
    return lax.optimization_barrier(v.astype(jnp.bfloat16)).astype(jnp.float32)

@jax.custom_vjp
def reduced_backward(v):
    return v

def low_keep(v):
    return (reduced_precision(v), None)

def low_pass(kept, grad):
    return (grad,)

def back_keep(v):
    return (v, None)

def back_low(kept, grad):
    return (reduced_precision(grad),)
reduced_precision.defvjp(low_keep, low_pass)
reduced_backward.defvjp(back_keep, back_low)
EPSILON = 1e-06
HIGHEST = lax.Precision.HIGHEST

def matrix_product(left_side, right_side):
    return jnp.dot(left_side, right_side, precision=HIGHEST, preferred_element_type=jnp.float32)

def rope_tables(positions, head_size):
    half_size = head_size // 2
    frequency = jnp.exp(jnp.arange(half_size, dtype=jnp.float32) * (-2.0 * math.log(10000.0) / head_size))
    angles = positions.astype(jnp.float32)[:, None] * frequency[None, :]
    return (jnp.cos(angles)[:, None, :], jnp.sin(angles)[:, None, :])

def apply_rotary(vector, cosine_lookup, sine_lookup):
    half_size = vector.shape[-1] // 2
    first_half = vector[..., :half_size]
    second_half = vector[..., half_size:]
    return jnp.concatenate([first_half * cosine_lookup - second_half * sine_lookup, second_half * cosine_lookup + first_half * sine_lookup], -1)

def rms_norm(values, gain_vec):
    inverse = lax.rsqrt(lax.optimization_barrier(jnp.mean(values * values, -1, keepdims=True)) + EPSILON)
    return values * inverse * gain_vec

def attention(query_rows, rows_of_key, rows_of_value):
    sequence_length = query_rows.shape[0]
    rows_per_block = min(512, sequence_length)
    head_groups = QUERY_HEADS // KEY_VALUE_HEADS
    blocks_of_query = query_rows.reshape(sequence_length // rows_per_block, rows_per_block, KEY_VALUE_HEADS, head_groups, HEAD_WIDTH)
    block_starts = jnp.arange(sequence_length // rows_per_block, dtype=jnp.int32) * rows_per_block
    key_pos = jnp.arange(sequence_length, dtype=jnp.int32)
    heads_of_key = rows_of_key.reshape(sequence_length, KEY_VALUE_HEADS, HEAD_WIDTH)
    heads_of_value = rows_of_value.reshape(sequence_length, KEY_VALUE_HEADS, HEAD_WIDTH)

    def one_block(operand):
        query_block, block_start = operand
        scores = reduced_backward(jnp.einsum('tkgd,skd->kgts', query_block, heads_of_key, precision=HIGHEST) * HEAD_WIDTH ** (-0.5))
        query_pos = block_start + jnp.arange(rows_per_block, dtype=jnp.int32)
        allowed = key_pos[None, :] <= query_pos[:, None]
        scores = jnp.where(allowed[None, None], scores, -1e+30)
        top_score = lax.optimization_barrier(jnp.max(scores, -1, keepdims=True))
        raised = jnp.exp(scores - top_score)
        shares = raised / lax.optimization_barrier(jnp.sum(raised, -1, keepdims=True))
        return jnp.einsum('kgts,skd->tkgd', reduced_precision(shares), heads_of_value, precision=HIGHEST).reshape(rows_per_block, QUERY_HEADS * HEAD_WIDTH)
    return lax.map(jax.checkpoint(one_block), (blocks_of_query, block_starts)).reshape(sequence_length, QUERY_HEADS * HEAD_WIDTH)

def expert_slots(routes):
    sequence_length = routes.shape[0]
    blocks = sequence_length // TOK_DEV
    flat_routes = routes.reshape(blocks, TOK_DEV * TOPK)
    onehot = (flat_routes[:, :, None] == jnp.arange(EXPERTS, dtype=jnp.int32)[None, None, :]).astype(jnp.int32)
    earlier = jnp.cumsum(onehot, 1) - onehot
    slot_rank = lax.optimization_barrier(jnp.sum(earlier * onehot, -1))
    block_index = jnp.arange(blocks, dtype=jnp.int32)[:, None]
    slot_index = flat_routes * (blocks * CAP) + block_index * CAP + slot_rank
    return slot_index.reshape(-1)

def forward(tokens, routes, gain_attn, w_query, key_weight, value_weight, w_out, gain_ffn, w_router, w_gate, w_up, w_down):
    sequence_length = tokens.shape[0]
    cosine_lookup, sine_lookup = rope_tables(jnp.arange(sequence_length, dtype=jnp.int32), HEAD_WIDTH)
    first_hidden = reduced_precision(rms_norm(tokens, gain_attn))
    query_rows = reduced_backward(matrix_product(first_hidden, w_query)).reshape(sequence_length, QUERY_HEADS, HEAD_WIDTH)
    rows_of_key = reduced_backward(matrix_product(first_hidden, key_weight)).reshape(sequence_length, KEY_VALUE_HEADS, HEAD_WIDTH)
    rows_of_value = reduced_precision(reduced_backward(matrix_product(first_hidden, value_weight)))
    query_rows = reduced_precision(apply_rotary(query_rows, cosine_lookup, sine_lookup)).reshape(sequence_length, QUERY_HEADS * HEAD_WIDTH)
    rows_of_key = reduced_precision(apply_rotary(rows_of_key, cosine_lookup, sine_lookup)).reshape(sequence_length, KEY_VALUE_HEADS * HEAD_WIDTH)
    mixed_heads = reduced_precision(reduced_backward(attention(query_rows, rows_of_key, rows_of_value)))
    middle = tokens + reduced_backward(matrix_product(mixed_heads, w_out))
    hidden_two = reduced_precision(rms_norm(middle, gain_ffn))
    logits = matrix_product(hidden_two, w_router)
    picked = jnp.take_along_axis(logits, routes, axis=1)
    top_logit = lax.optimization_barrier(jnp.max(picked, -1, keepdims=True))
    raised = jnp.exp(picked - top_logit)
    gate_share = raised / lax.optimization_barrier(jnp.sum(raised, -1, keepdims=True))
    slot_index = expert_slots(routes)
    copies = reduced_backward(jnp.broadcast_to(hidden_two[:, None, :], (sequence_length, TOPK, MODEL_WIDTH))).reshape(sequence_length * TOPK, MODEL_WIDTH)
    buffer = jnp.zeros((EXPERTS * (sequence_length // TOK_DEV) * CAP, MODEL_WIDTH), jnp.float32).at[slot_index].set(copies)
    buffer = buffer.reshape(EXPERTS, sequence_length // TOK_DEV * CAP, MODEL_WIDTH)
    gate_act = reduced_backward(jnp.einsum('esd,edf->esf', buffer, w_gate, precision=HIGHEST))
    up_act = reduced_backward(jnp.einsum('esd,edf->esf', buffer, w_up, precision=HIGHEST))
    inner_act = reduced_precision(jax.nn.silu(gate_act) * up_act)
    result = reduced_backward(reduced_precision(jnp.einsum('esf,efd->esd', inner_act, w_down, precision=HIGHEST)))
    returned = result.reshape(-1, MODEL_WIDTH)[slot_index].reshape(sequence_length, TOPK, MODEL_WIDTH)
    return middle + lax.optimization_barrier(jnp.sum(gate_share[:, :, None] * returned, 1))

def reference(block_in, routes, cotangent, gain_attn, w_query, key_weight, value_weight, w_out, gain_ffn, w_router, w_gate, w_up, w_down):
    weights = tuple((weight.astype(jnp.float32) for weight in (gain_attn, w_query, key_weight, value_weight, w_out, gain_ffn, w_router, w_gate, w_up, w_down)))

    def one_sequence(running, sequence):
        tokens, route_rows, grad_rows = sequence

        def local_forward(token_rows, gain_one, query_w, key_w, value_w, out_w, gain_two, router_w, gate_w, up_w, down_w):
            return forward(token_rows, route_rows, gain_one, query_w, key_w, value_w, out_w, gain_two, router_w, gate_w, up_w, down_w)
        output, pullback = jax.vjp(local_forward, tokens.astype(jnp.float32), *weights)
        gradients = pullback(grad_rows.astype(jnp.float32))
        running = tuple((total + update for total, update in zip(running, gradients[1:])))
        return (running, (output.astype(jnp.bfloat16), gradients[0]))
    zero_grads = tuple((jnp.zeros_like(weight) for weight in weights))
    totals, (outputs, input_grads) = lax.scan(one_sequence, zero_grads, (block_in, routes, cotangent))
    return (outputs, input_grads, totals[0], totals[1], totals[2], totals[3], totals[4], totals[5], totals[6], totals[7], totals[8], totals[9])
```

```python
import functools
import math

import jax
import jax.numpy as jnp
import numpy as np
from jax import lax
from jax.experimental import pallas as pl
from jax.experimental.pallas import tpu as pltpu
from jax.sharding import PartitionSpec as P

WIDTH = 1536
HEADS = 24
KV_HEADS = 8
HEAD = 64
TOPK = 8
ROWS = 128
LENGTH = 2048
EXPERTS = 32
FF = 512
CAP = 48
EPSILON = 1e-06

BF = jnp.bfloat16
F32 = jnp.float32
MESH = pl.DeviceIdType.MESH
VMEM_BYTES = 60 << 20

QUARTER = 1152
HALF = 2 * QUARTER
COL_K, COL_V, COL_O, COL_M, COL_END = 768, 1024, 1280, 2048, 2176
TALL = WIDTH + 128


def vm():
    return pl.BlockSpec(memory_space=pltpu.VMEM)


def hbm():
    return pl.BlockSpec(memory_space=pl.ANY)


def shape(dims, dtype=BF):
    return jax.ShapeDtypeStruct(dims, dtype)


def place():
    seq, ctx = lax.axis_index("seq"), lax.axis_index("ctx")
    return (ctx // 2 % 2 * 2 + seq // 4, ctx // 4, seq % 4, ctx % 2)


def device(x, y, z, core):
    return (x % 2 * 4 + z, (y * 2 + x // 2) * 2 + core)


def ring(at, dim, step):
    x, y, z, core = at
    if dim == 0:
        return ((x + step) % 4, y, z, core)
    if dim == 1:
        return (x, (y + step) % 4, z, core)
    return (x, y, (z + step) % 4, core)


def sibling(at):
    return (at[0], at[1], at[2], 1 - at[3])


def greet(peers):
    barrier = pltpu.get_barrier_semaphore()
    for peer in peers:
        pl.semaphore_signal(barrier, inc=1, device_id=device(*peer), device_id_type=MESH)
    pl.semaphore_wait(barrier, len(peers))


class Wires:
    def __init__(self, send, recv):
        self.send, self.recv, self.used, self.open = send, recv, 0, []

    def go(self, src, dst, peer):
        n = self.used
        self.used += 1
        copy = pltpu.make_async_remote_copy(
            src_ref=src,
            dst_ref=dst,
            send_sem=self.send.at[n],
            recv_sem=self.recv.at[n],
            device_id=device(*peer),
            device_id_type=MESH,
        )
        copy.start()
        self.open.append(copy)
        return copy

    def close(self):
        for copy in self.open:
            copy.wait_send()


def wire_sems(n):
    return [pltpu.SemaphoreType.DMA((n,)), pltpu.SemaphoreType.DMA((n,))]


def got(copies):
    for copy in copies:
        copy.wait_recv()


def dot(a, b):
    return jnp.dot(a, b, preferred_element_type=F32)


def dot_t(a, b):
    return lax.dot_general(a, b, (((1,), (1,)), ((), ())), preferred_element_type=F32)


def t_dot(a, b):
    return lax.dot_general(a, b, (((0,), (0,)), ((), ())), preferred_element_type=F32)


def iota(dims, axis):
    return lax.broadcasted_iota(jnp.int32, dims, axis)


def turn(block, cosine, sine):
    low = iota((block.shape[0], 128), 1) % HEAD < HEAD // 2
    parts = []
    for i in range(block.shape[1] // 128):
        unit = block[:, 128 * i : 128 * i + 128]
        other = jnp.where(low, pltpu.roll(unit, 96, 1), pltpu.roll(unit, 32, 1))
        parts.append(unit * cosine + other * sine)
    return jnp.concatenate(parts, 1)


def regroup():
    r, c = iota((48, 64), 0), iota((48, 64), 1)
    owner = c // 16 % 2 * 2 + c // 32
    hit = (r == owner * 12 + c % 16) & (c % 16 < 12)
    return hit.astype(F32).astype(BF)


def regroup_back():
    r, c = iota((64, 48), 0), iota((64, 48), 1)
    hit = (c == r // 16 * 12 + r % 16) & (r % 16 < 12)
    return hit.astype(F32).astype(BF)


ORDERS = ((0, 1, 2), (1, 2, 0), (2, 0, 1))


def block_of(ref, part, fixed, at):
    x, y, z, _ = at
    whole = slice(None)
    columns = (
        pl.ds(pl.multiple_of(x // 2 * QUARTER, 128), QUARTER) if 0 in fixed else pl.ds(0, HALF)
    )
    return (
        x % 2 if 0 in fixed else whole,
        z if 2 in fixed else whole,
        y if 1 in fixed else whole,
        part,
        whole,
        columns,
    )


def spread(ref, wires, at):
    waits = [[], [], []]
    for phase in range(3):
        for part in range(3):
            got(waits[part])
            waits[part] = []
            fixed = ORDERS[part][phase:]
            spot = ref.at[block_of(ref, part, fixed, at)]
            for step in (1, 2, 3):
                waits[part].append(wires.go(spot, spot, ring(at, fixed[0], step)))
    for part in range(3):
        got(waits[part])


def ctx_peers(at):
    return [ring(at, 1, 1), ring(at, 1, 2), ring(at, 1, 3), ring(at, 0, 2)]


def all_peers(at):
    return [ring(at, d, s) for d in range(3) for s in (1, 2, 3)]


def first_kernel(
    stage, x, cosine, sine,
    weights, wo, rows, router, q, kv, h1t,
    both, slots, cos_v, sin_v, ssem, rsem, lsem,
):
    at = place()
    xx, y, z, core = at
    xh, chip = xx // 2, y * 2 + xx // 2
    diagonal = sibling(ring(at, 0, 2))
    greet(all_peers(at) + [sibling(at), diagonal])
    wires = Wires(ssem, rsem)
    tables = [
        pltpu.make_async_copy(src.at[pl.ds(pl.multiple_of(chip * 256, 256), 256)], dst, lsem.at[i])
        for i, (src, dst) in enumerate(((cosine, cos_v), (sine, sin_v)))
    ]
    for copy in tables:
        copy.start()
    mine = core * 2 + xh
    first = [
        wires.go(stage.at[peer[3] * 2 + peer[0] // 2], slots.at[mine], peer)
        for peer in (sibling(at), ring(at, 0, 2), diagonal)
    ]
    tokens = wires.go(x, both.at[core], sibling(at))
    slots[mine] = stage[mine]
    both[core] = x[...]
    got(first)
    unit = dot(regroup(), slots[...].reshape(64, QUARTER)).astype(BF)
    lanes = pl.ds(pl.multiple_of(xh * QUARTER, 128), QUARTER)
    for part in range(3):
        weights[xx % 2, z, y, part, :, lanes] = unit[16 * part : 16 * part + 16]
    spread(weights, wires, at)

    out_columns = slice(COL_O, COL_M)
    swap = wires.go(
        weights.at[1 - core, :, :, :, :, out_columns],
        wo.at[:, :, :, :, pl.ds(pl.multiple_of(core * 768, 128), 768)],
        sibling(at),
    )
    for i in range(4):
        wo[i, :, :, :, pl.ds(pl.multiple_of(core * 768, 128), 768)] = weights[core, i, :, :, :, out_columns]
    small = weights[:, :, :, :, :, COL_M:COL_END].reshape(WIDTH, 128)
    router[...] = small
    turned = jnp.transpose(small.astype(F32))
    rows[...] = turned[32:40]
    got([tokens])
    values = both[...].reshape(256, WIDTH).astype(F32)
    inverse = lax.rsqrt(jnp.mean(values * values, -1, keepdims=True) + EPSILON)
    hidden = (values * inverse * turned[32:33]).astype(BF)
    made = dot(hidden, weights[:, :, :, :, :, 0:COL_O].reshape(WIDTH, COL_O))
    for copy in tables:
        copy.wait()
    cos, sin = cos_v[...], sin_v[...]
    key = turn(made[:, COL_K:COL_V], cos, sin).astype(BF)
    value = made[:, COL_V:COL_O].astype(BF)
    for part in range(2):
        kv[y, xh, part, :, 0:256] = key[128 * part : 128 * part + 128]
        kv[y, xh, part, :, 256:512] = value[128 * part : 128 * part + 128]
    own = [kv.at[y, xh, 0], kv.at[y, xh, 1]]
    a = [wires.go(own[0], own[0], ring(at, 1, s)) for s in (1, 2, 3)]
    b = [wires.go(own[1], own[1], ring(at, 0, 2))]
    q[...] = turn(made[:, 0:COL_K], cos, sin).astype(BF)
    got(a)
    column = kv.at[:, xh, 0]
    a = [wires.go(column, column, ring(at, 0, 2))]
    got(b)
    pair = kv.at[y, :, 1]
    b = [wires.go(pair, pair, ring(at, 1, s)) for s in (1, 2, 3)]
    h1t[...] = jnp.transpose(hidden.astype(F32)).astype(BF)
    got(a)
    got(b)
    got([swap])
    wires.close()


def first_call(stage, x, cosine, sine):
    return pl.pallas_call(
        first_kernel,
        out_shape=[
            shape((2, 4, 4, 3, 16, HALF)),
            shape((4, 4, 3, 16, WIDTH)),
            shape((8, WIDTH), F32),
            shape((WIDTH, 128)),
            shape((256, 768)),
            shape((4, 2, 2, 128, 512)),
            shape((WIDTH, 256)),
        ],
        in_specs=[vm(), vm(), hbm(), hbm()],
        out_specs=[vm()] * 7,
        scratch_shapes=[
            pltpu.VMEM((2, 128, WIDTH), BF),
            pltpu.VMEM((4, 16, QUARTER), BF),
            pltpu.VMEM((256, 128), F32),
            pltpu.VMEM((256, 128), F32),
            *wire_sems(48),
            pltpu.SemaphoreType.DMA((2,)),
        ],
        compiler_params=pltpu.CompilerParams(
            collective_id=1, has_side_effects=True, vmem_limit_bytes=VMEM_BYTES
        ),
        name="weights_qkv",
    )(stage, x, cosine, sine)


def attend_kernel(q, kv, o, ot, lse, scores, vt, qt, qz, out_t):
    at = place()
    chip = at[1] * 2 + at[0] // 2
    qt[...] = jnp.transpose(q[...].astype(F32) * 0.125).astype(BF)
    for kb in range(8):
        vt[kb] = jnp.transpose(kv[256 * kb : 256 * kb + 256, 256:512].astype(F32)).astype(BF)
    allowed = iota((256, 768), 0) <= iota((256, 768), 1) % 256
    for j in range(4):
        u, half = j // 2, j % 2
        qz[...] = jnp.zeros_like(qz)
        for g in range(3):
            h = 3 * j + g
            qz[64 * half : 64 * half + 64, 256 * g : 256 * g + 256] = qt[64 * h : 64 * h + 64]

        def score(kb):
            rows = pl.ds(pl.multiple_of(kb * 256, 256), 256)
            return rows, dot(kv[rows, 128 * u : 128 * u + 128], qz[...])

        def top(kb, most):
            rows, s = score(kb)
            scores[rows] = s
            return jnp.maximum(most, jnp.max(s.reshape(32, 8, 768), 0))

        most = lax.fori_loop(0, chip, top, jnp.full((8, 768), -1e30, F32))
        rows, s = score(chip)
        s = jnp.where(allowed, s, -1e30)
        scores[rows] = s
        most = jnp.maximum(most, jnp.max(s.reshape(32, 8, 768), 0))
        most = jnp.max(most, 0, keepdims=True)

        def raise_(kb, total):
            rows = pl.ds(pl.multiple_of(kb * 256, 256), 256)
            e = jnp.exp(scores[rows] - most)
            scores[rows] = e
            return total + jnp.sum(e.reshape(32, 8, 768), 0)

        total = lax.fori_loop(0, chip + 1, raise_, jnp.zeros((8, 768), F32))
        total = jnp.sum(total, 0, keepdims=True)
        lse[j] = jnp.broadcast_to(most + jnp.log(total), (8, 768))
        inverse = 1.0 / total

        def mix(kb, acc):
            rows = pl.ds(pl.multiple_of(kb * 256, 256), 256)
            p = (scores[rows] * inverse).astype(BF)
            return acc + dot(vt[kb, 64 * j : 64 * j + 64], p)

        acc = lax.fori_loop(0, chip + 1, mix, jnp.zeros((64, 768), F32))
        for g in range(3):
            h = 3 * j + g
            out_t[64 * h : 64 * h + 64] = acc[:, 256 * g : 256 * g + 256]
    ot[...] = out_t[...].astype(BF)
    o[...] = jnp.transpose(out_t[...]).astype(BF)


def attend_call(q, kv):
    return pl.pallas_call(
        attend_kernel,
        out_shape=[shape((256, 768)), shape((768, 256)), shape((4, 8, 768), F32)],
        in_specs=[vm(), vm()],
        out_specs=[vm()] * 3,
        scratch_shapes=[
            pltpu.VMEM((LENGTH, 768), F32),
            pltpu.VMEM((8, 256, 256), BF),
            pltpu.VMEM((768, 256), BF),
            pltpu.VMEM((128, 768), BF),
            pltpu.VMEM((768, 256), F32),
        ],
        compiler_params=pltpu.CompilerParams(vmem_limit_bytes=VMEM_BYTES),
        name="attend",
    )(q, kv)


def attend_back_kernel(
    q, kv, d_o, lse, cosine, sine,
    dq, dkv,
    probs, grads, kt, qt, dot_, qz, oz, acc, dqt, cos_v, sin_v, lsem,
):
    at = place()
    chip = at[1] * 2 + at[0] // 2
    tables = [
        pltpu.make_async_copy(src.at[pl.ds(pl.multiple_of(chip * 256, 256), 256)], dst, lsem.at[i])
        for i, (src, dst) in enumerate(((cosine, cos_v), (sine, sin_v)))
    ]
    for copy in tables:
        copy.start()
    qt[...] = jnp.transpose(q[...].astype(F32) * 0.125).astype(BF)
    dot_[...] = jnp.transpose(d_o[...].astype(F32)).astype(BF)
    for kb in range(8):
        kt[kb] = jnp.transpose(kv[256 * kb : 256 * kb + 256, 0:256].astype(F32)).astype(BF)
    acc[...] = jnp.zeros_like(acc)
    allowed = iota((256, 768), 0) <= iota((256, 768), 1) % 256
    for j in range(4):
        u, half = j // 2, j % 2
        qz[...] = jnp.zeros_like(qz)
        oz[...] = jnp.zeros_like(oz)
        for g in range(3):
            h = 3 * j + g
            qz[64 * half : 64 * half + 64, 256 * g : 256 * g + 256] = qt[64 * h : 64 * h + 64]
            oz[64 * half : 64 * half + 64, 256 * g : 256 * g + 256] = dot_[64 * h : 64 * h + 64]
        level = lse[j, 0:1]

        def share(kb, centre, masked):
            rows = pl.ds(pl.multiple_of(kb * 256, 256), 256)
            p = jnp.exp(dot(kv[rows, 128 * u : 128 * u + 128], qz[...]) - level)
            if masked:
                p = jnp.where(allowed, p, 0.0)
            probs[rows] = p
            dp = dot(kv[rows, 256 + 128 * u : 384 + 128 * u], oz[...])
            grads[rows] = dp
            acc[rows, 256 + 128 * u : 384 + 128 * u] += dot_t(p.astype(BF), oz[...])
            return centre + jnp.sum((p * dp).reshape(32, 8, 768), 0)

        centre = lax.fori_loop(
            0, chip, functools.partial(share, masked=False), jnp.zeros((8, 768), F32)
        )
        centre = share(chip, centre, True)
        centre = jnp.sum(centre, 0, keepdims=True)

        def back(kb, total):
            rows = pl.ds(pl.multiple_of(kb * 256, 256), 256)
            ds = (probs[rows] * (grads[rows] - centre)).astype(BF)
            acc[rows, 128 * u : 128 * u + 128] += dot_t(ds, qz[...])
            return total + dot(kt[kb, 64 * j : 64 * j + 64], ds)

        total = lax.fori_loop(0, chip + 1, back, jnp.zeros((64, 768), F32))
        for g in range(3):
            h = 3 * j + g
            dqt[64 * h : 64 * h + 64] = total[:, 256 * g : 256 * g + 256] * 0.125
    for kb in range(8):
        for part in range(2):
            at_row = 256 * kb + 128 * part
            dkv[part, kb] = acc[at_row : at_row + 128].astype(BF)
    for copy in tables:
        copy.wait()
    dq[...] = turn(jnp.transpose(dqt[...]), cos_v[...], -sin_v[...]).astype(BF)


def attend_back_call(q, kv, d_o, lse, cosine, sine):
    return pl.pallas_call(
        attend_back_kernel,
        out_shape=[shape((256, 768)), shape((2, 8, 128, 512))],
        in_specs=[vm()] * 4 + [hbm()] * 2,
        out_specs=[vm()] * 2,
        scratch_shapes=[
            pltpu.VMEM((LENGTH, 768), F32),
            pltpu.VMEM((LENGTH, 768), F32),
            pltpu.VMEM((8, 256, 256), BF),
            pltpu.VMEM((768, 256), BF),
            pltpu.VMEM((768, 256), BF),
            pltpu.VMEM((128, 768), BF),
            pltpu.VMEM((128, 768), BF),
            pltpu.VMEM((LENGTH, 512), F32),
            pltpu.VMEM((768, 256), F32),
            pltpu.VMEM((256, 128), F32),
            pltpu.VMEM((256, 128), F32),
            pltpu.SemaphoreType.DMA((2,)),
        ],
        compiler_params=pltpu.CompilerParams(vmem_limit_bytes=VMEM_BYTES),
        name="attend_back",
    )(q, kv, d_o, lse, cosine, sine)


def share_rows(ref, wires, at):
    x, y, _, core = at
    xh = x // 2
    near, far = sibling(at), ring(at, 0, 2)

    def pass_on(spot, peer):
        return wires.go(spot, spot, peer)

    inner = [pass_on(ref.at[y, xh, core], near)]
    a = [pass_on(ref.at[y, xh, core, 0], ring(at, 1, s)) for s in (1, 2, 3)]
    b = [pass_on(ref.at[y, xh, core, 1], far)]
    yield
    got(b)
    b = [pass_on(ref.at[y, :, core, 1], ring(at, 1, s)) for s in (1, 2, 3)]
    got(a)
    a = [pass_on(ref.at[:, xh, core, 0], far)]
    inner.append(pass_on(ref.at[y, 1 - xh, core, 1], near))
    for s in (1, 2, 3):
        inner.append(pass_on(ref.at[(y + s) % 4, xh, core, 0], near))
    yield
    got(a)
    inner.append(pass_on(ref.at[:, 1 - xh, core, 0], near))
    got(b)
    for s in (1, 2, 3):
        inner.append(pass_on(ref.at[(y + s) % 4, :, core, 1], near))
    yield
    got(inner)


def ctx_and_sibling(at):
    return ctx_peers(at) + [sibling(at)]


def share_kernel(rows, all_rows, ssem, rsem, lsem):
    at = place()
    x, y, _, core = at
    greet(ctx_and_sibling(at))
    wires = Wires(ssem, rsem)
    own = pltpu.make_async_copy(rows, all_rows.at[y, x // 2, core], lsem)
    own.start()
    own.wait()
    for _ in share_rows(all_rows, wires, at):
        pass
    wires.close()


def share_call(rows):
    return pl.pallas_call(
        share_kernel,
        out_shape=shape((4, 2, 2, 2, 64, WIDTH)),
        in_specs=[hbm()],
        out_specs=hbm(),
        scratch_shapes=[*wire_sems(24), pltpu.SemaphoreType.DMA],
        compiler_params=pltpu.CompilerParams(collective_id=2, has_side_effects=True),
        name="share_cotangent",
    )(rows)


def normed(values):
    inverse = lax.rsqrt(jnp.mean(values * values, -1, keepdims=True) + EPSILON)
    return values * inverse, inverse


def middle_kernel(
    o, wo, x, routes, rows, router,
    middle, gates, tall,
    product, arrived, ssem, rsem,
):
    at = place()
    xx, y, _, core = at
    near = sibling(at)
    greet(ctx_and_sibling(at))
    wires = Wires(ssem, rsem)
    full = wo[...].reshape(768, WIDTH)
    product[0] = dot(o[1 - core], full)
    swap = wires.go(product.at[0], arrived, near)
    product[1] = dot(o[core], full)
    lane = iota((ROWS, 128), 1)
    named = routes[:, 0:1] == lane
    for i in range(1, TOPK):
        named = named | (routes[:, i : i + 1] == lane)
    got([swap])
    mid = x[...].astype(F32) + product[1] + arrived[...]
    middle[...] = mid
    hidden = (normed(mid)[0] * rows[1:2]).astype(BF)
    logits = jnp.where(named, dot(hidden, router[...]), -jnp.inf)
    raised = jnp.exp(logits - jnp.max(logits, -1, keepdims=True))
    gate = raised / jnp.sum(raised, -1, keepdims=True)
    gates[...] = gate
    high = gate.astype(BF).astype(F32)
    both = high + pltpu.roll(gate - high, EXPERTS, 1)
    for part in range(2):
        cut = slice(64 * part, 64 * part + 64)
        tall[y, xx // 2, core, part, :, 0:WIDTH] = hidden[cut]
        tall[y, xx // 2, core, part, :, WIDTH:TALL] = both[cut].astype(BF)
    for _ in share_rows(tall, wires, at):
        pass
    wires.close()


def middle_call(o, wo, x, routes, rows, router):
    return pl.pallas_call(
        middle_kernel,
        out_shape=[
            shape((ROWS, WIDTH), F32),
            shape((ROWS, 128), F32),
            shape((4, 2, 2, 2, 64, TALL)),
        ],
        in_specs=[vm()] * 6,
        out_specs=[vm()] * 3,
        scratch_shapes=[
            pltpu.VMEM((2, ROWS, WIDTH), F32),
            pltpu.VMEM((ROWS, WIDTH), F32),
            *wire_sems(24),
        ],
        compiler_params=pltpu.CompilerParams(
            collective_id=3, has_side_effects=True, vmem_limit_bytes=VMEM_BYTES
        ),
        name="middle",
    )(o.reshape(2, ROWS, 768), wo, x, routes, rows, router)


def expert_kernel(
    tall, dy, w_gate, w_up, w_down,
    out_rows, d_rows, g_gate, g_up, g_down,
    big, wide, a_rows, y_rows, r_rows, back, wg, wu, wd, gg, gu, gd, m_s, dg_s, du_s, slot_t, sem,
):
    ctx = lax.axis_index("ctx")
    loads = [
        pltpu.make_async_copy(src, dst, sem.at[i])
        for i, (src, dst) in enumerate(
            ((tall, big), (dy, wide), (w_gate, wg), (w_up, wu), (w_down, wd))
        )
    ]
    for copy in loads:
        copy.start()
    lane = iota((128, 128), 1)
    earlier = (iota((128, 128), 1) < iota((128, 128), 0)).astype(F32).astype(BF)
    slots = iota((CAP, 128), 0).astype(F32)
    loads[0].wait()
    loads[1].wait()

    def collect(b, _):
        rows = pl.ds(pl.multiple_of(b * 128, 128), 128)
        packed = pl.ds(pl.multiple_of(b * CAP, CAP), CAP)
        both = big[rows, WIDTH:TALL].astype(F32)
        gate = both + pltpu.roll(both, 128 - EXPERTS, 1)
        hot = (gate > 0.0) & (lane < EXPERTS)
        rank = dot(earlier, hot.astype(F32).astype(BF))
        slot = jnp.where(hot, rank, -1.0)
        slot_t[...] = jnp.transpose(slot)
        picks = [
            (slot_t[pl.ds(2 * ctx + i, 1), :] == slots).astype(F32).astype(BF) for i in range(2)
        ]
        pick = jnp.concatenate(picks, 0)
        found = dot(pick, big[rows, :]).astype(BF)
        grads = dot(pick, wide[rows, :]).astype(BF)
        for i in range(2):
            a_rows[i, packed] = found[CAP * i : CAP * i + CAP]
            y_rows[i, packed] = grads[CAP * i : CAP * i + CAP]
        column = [
            jnp.sum(jnp.where(lane == 2 * ctx + i, slot, 0.0), 1, keepdims=True) for i in range(2)
        ]
        spot = lane.astype(F32)
        put = jnp.where(lane < CAP, column[0], column[1] + CAP) == spot
        back[b] = put.astype(F32).astype(BF)
        return 0

    lax.fori_loop(0, 16, collect, 0)
    for copy in loads[2:]:
        copy.wait()
    stores = []
    for e in range(2):
        number = 2 * ctx + e

        def forward(c, _):
            rows = pl.ds(pl.multiple_of(c * 384, 384), 384)
            a = a_rows[e, rows, 0:WIDTH]
            ag, au = dot(a, wg[e]), dot(a, wu[e])
            sg = jax.nn.sigmoid(ag)
            act = ag * sg
            m = (act * au).astype(BF)
            r = dot(m, wd[e]).astype(BF).astype(F32)
            lanes = iota((384, 128), 1)
            hits = (lanes == number) | (lanes == number + EXPERTS)
            gate = jnp.sum(
                jnp.where(hits, a_rows[e, rows, WIDTH:TALL].astype(F32), 0.0), 1, keepdims=True
            )
            y = y_rows[e, rows].astype(F32)
            d_gate = jnp.sum(y * r, 1, keepdims=True)
            r_rows[e, rows] = (gate * r).astype(BF)
            gr = (gate * y).astype(BF)
            y_rows[e, rows] = gr
            dm = dot_t(gr, wd[e])
            m_s[rows] = m
            dg_s[rows] = (dm * au * (sg * (1.0 + ag * (1.0 - sg)))).astype(BF)
            du_s[rows] = (dm * act).astype(BF)
            high = d_gate.astype(BF).astype(F32)
            d_both = jnp.where(
                lanes == number, high, jnp.where(lanes == number + EXPERTS, d_gate - high, 0.0)
            )
            a_rows[e, rows, WIDTH:TALL] = d_both.astype(BF)
            return 0

        lax.fori_loop(0, 2, forward, 0)
        gd[e] = t_dot(m_s[...], y_rows[e]).astype(BF)
        gg[e] = t_dot(a_rows[e, :, 0:WIDTH], dg_s[...]).astype(BF)
        gu[e] = t_dot(a_rows[e, :, 0:WIDTH], du_s[...]).astype(BF)
        for i, (src, dst) in enumerate(((gd, g_down), (gg, g_gate), (gu, g_up))):
            copy = pltpu.make_async_copy(src.at[e], dst.at[e], sem.at[5 + 3 * e + i])
            copy.start()
            stores.append(copy)

        def to_tokens(c, _):
            rows = pl.ds(pl.multiple_of(c * 384, 384), 384)
            back_rows = dot_t(dg_s[rows], wg[e]) + dot_t(du_s[rows], wu[e])
            a_rows[e, rows, 0:WIDTH] = back_rows.astype(BF)
            return 0

        lax.fori_loop(0, 2, to_tokens, 0)

    def hand_back(b, _):
        rows = pl.ds(pl.multiple_of(b * 128, 128), 128)
        packed = pl.ds(pl.multiple_of(b * CAP, CAP), CAP)
        put = back[b][:, 0 : 2 * CAP]
        big[rows, :] = dot(put, jnp.concatenate([a_rows[0, packed], a_rows[1, packed]], 0)).astype(BF)
        wide[rows, :] = dot(put, jnp.concatenate([r_rows[0, packed], r_rows[1, packed]], 0)).astype(BF)
        return 0

    lax.fori_loop(0, 16, hand_back, 0)
    for i, (src, dst) in enumerate(((big, d_rows), (wide, out_rows))):
        copy = pltpu.make_async_copy(src, dst, sem.at[i])
        copy.start()
        stores.append(copy)
    for copy in stores:
        copy.wait()


def expert_call(tall, dy, w_gate, w_up, w_down):
    slots = 16 * CAP
    return pl.pallas_call(
        expert_kernel,
        out_shape=[
            shape((LENGTH, WIDTH)),
            shape((LENGTH, TALL)),
            shape((2, WIDTH, FF)),
            shape((2, WIDTH, FF)),
            shape((2, FF, WIDTH)),
        ],
        in_specs=[hbm()] * 5,
        out_specs=[hbm()] * 5,
        scratch_shapes=[
            pltpu.VMEM((LENGTH, TALL), BF),
            pltpu.VMEM((LENGTH, WIDTH), BF),
            pltpu.VMEM((2, slots, TALL), BF),
            pltpu.VMEM((2, slots, WIDTH), BF),
            pltpu.VMEM((2, slots, WIDTH), BF),
            pltpu.VMEM((16, 128, 128), BF),
            pltpu.VMEM((2, WIDTH, FF), BF),
            pltpu.VMEM((2, WIDTH, FF), BF),
            pltpu.VMEM((2, FF, WIDTH), BF),
            pltpu.VMEM((2, WIDTH, FF), BF),
            pltpu.VMEM((2, WIDTH, FF), BF),
            pltpu.VMEM((2, FF, WIDTH), BF),
            pltpu.VMEM((slots, FF), BF),
            pltpu.VMEM((slots, FF), BF),
            pltpu.VMEM((slots, FF), BF),
            pltpu.VMEM((128, 128), F32),
            pltpu.SemaphoreType.DMA((11,)),
        ],
        compiler_params=pltpu.CompilerParams(vmem_limit_bytes=VMEM_BYTES),
        name="experts",
    )(tall.reshape(LENGTH, TALL), dy.reshape(LENGTH, WIDTH), w_gate, w_up, w_down)


def sum_scratch(rows, columns):
    return [
        pltpu.VMEM((4, rows, columns), BF),
        pltpu.VMEM((3, 2, rows, columns), BF),
        pltpu.VMEM((4, rows, columns), BF),
        pltpu.VMEM((2, rows, columns), BF),
        pltpu.VMEM((3, rows, columns), BF),
        pltpu.VMEM((1, rows, columns), BF),
    ]


def sum_chips(source, scratch, wires, at):
    e0, e1, t0, t1, f0, f1 = scratch
    x, y, _, _ = at
    xh = x // 2
    far = ring(at, 0, 2)
    a = [wires.go(source.at[0, :, 1 - xh], e0, far)]
    b = [
        wires.go(source.at[1, (y + s) % 4], e1.at[s - 1], ring(at, 1, s)) for s in (1, 2, 3)
    ]
    yield None
    got(a)
    for i in range(4):
        t0[i] = (source[0, i, xh].astype(F32) + e0[i].astype(F32)).astype(BF)
    a = [wires.go(t0.at[(y + s) % 4], f0.at[s - 1], ring(at, 1, s)) for s in (1, 2, 3)]
    got(b)
    for i in range(2):
        total = source[1, y, i].astype(F32)
        for s in range(3):
            total += e1[s, i].astype(F32)
        t1[i] = total.astype(BF)
    b = [wires.go(t1.at[1 - xh], f1.at[0], far)]
    yield None
    got(a)
    first = t0[y].astype(F32)
    for s in range(3):
        first += f0[s].astype(F32)
    got(b)
    yield first, t1[xh].astype(F32) + f1[0].astype(F32)


def sum_rows_scratch(columns):
    return [
        pltpu.VMEM((2, 4, 2, 64, columns), BF),
        pltpu.VMEM((2, 4, 2, 64, columns), BF),
        *sum_scratch(64, columns),
    ]


def sum_rows(rows, scratch, wires, at):
    landed, own, rest = scratch[0], scratch[1], scratch[2:]
    core = at[3]
    copies = [
        wires.go(rows.at[:, :, 1 - core, part], landed.at[part], sibling(at)) for part in range(2)
    ]
    yield None
    for part in range(2):
        got([copies[part]])
        for i in range(4):
            for h in range(2):
                own[part, i, h] = (
                    rows[i, h, core, part].astype(F32) + landed[part, i, h].astype(F32)
                ).astype(BF)
    for result in sum_chips(own, rest, wires, at):
        yield result


def final(steps):
    result = None
    for result in steps:
        pass
    return result


def block_out_kernel(rows, middle, out, *rest):
    scratch, (ssem, rsem) = rest[:-2], rest[-2:]
    at = place()
    greet(ctx_and_sibling(at))
    wires = Wires(ssem, rsem)
    parts = final(sum_rows(rows, scratch, wires, at))
    for part in range(2):
        cut = slice(64 * part, 64 * part + 64)
        out[cut] = (middle[cut] + parts[part]).astype(BF)
    wires.close()


def block_out_call(rows, middle):
    return pl.pallas_call(
        block_out_kernel,
        out_shape=shape((ROWS, WIDTH)),
        in_specs=[vm()] * 2,
        out_specs=vm(),
        scratch_shapes=[*sum_rows_scratch(WIDTH), *wire_sems(16)],
        compiler_params=pltpu.CompilerParams(
            collective_id=5, has_side_effects=True, vmem_limit_bytes=VMEM_BYTES
        ),
        name="block_out",
    )(rows.reshape(4, 2, 2, 2, 64, WIDTH), middle)


def split_dot(left, right, form):
    high = left.astype(BF)
    low = (left - high.astype(F32)).astype(BF)
    return form(high, right) + form(low, right)


def norm_back(grad, gain, n, inverse):
    scaled = grad * gain
    return inverse * (scaled - n * jnp.mean(scaled * n, -1, keepdims=True))


def token_grad_kernel(
    d_rows, middle, gates, dy, rows, router, wo, ot,
    d_mid, d_o, small, g_out,
    low, product, *rest,
):
    scratch, (ssem, rsem) = rest[:-2], rest[-2:]
    at = place()
    core = at[3]
    near = sibling(at)
    greet(ctx_and_sibling(at))
    wires = Wires(ssem, rsem)
    steps = sum_rows(d_rows, scratch, wires, at)
    next(steps)
    next(steps)
    n, inverse = normed(middle[...])
    hidden = (n * rows[1:2]).astype(BF)
    parts = final(steps)
    total = jnp.concatenate(parts, 0)
    d_hidden = total[:, 0:WIDTH]
    both = total[:, WIDTH:TALL]
    gate = gates[...]
    lane = iota((ROWS, 128), 1)
    d_gate = jnp.where(lane < EXPERTS, both + pltpu.roll(both, 128 - EXPERTS, 1), 0.0)
    centre = jnp.sum(gate * d_gate, -1, keepdims=True)
    d_logits = gate * (d_gate - centre)
    d_hidden += split_dot(d_logits, router[...], dot_t)
    d_middle = norm_back(d_hidden, rows[1:2], n, inverse) + dy[...].astype(F32)
    d_low = d_middle.astype(BF)
    low[core] = d_low
    swap = wires.go(low.at[core], low.at[core], near)
    d_mid[...] = d_middle
    grads = split_dot(jnp.transpose(d_logits), hidden, dot)
    line = jnp.sum(d_hidden * n, 0, keepdims=True)
    small[...] = grads + jnp.where(iota((128, WIDTH), 0) == EXPERTS + 1, line, 0.0)
    got([swap])
    chip_rows = low[...].reshape(256, WIDTH)
    d_o[...] = dot_t(chip_rows, wo[...].reshape(768, WIDTH)).astype(BF)
    product[...] = dot(ot[...], chip_rows).astype(BF).reshape(4, 4, 3, 16, WIDTH)
    lanes = pl.ds(pl.multiple_of((1 - core) * 768, 128), 768)
    mine = pl.ds(pl.multiple_of(core * 768, 128), 768)
    swap = wires.go(product.at[:, :, :, :, lanes], g_out.at[core], near)
    for i in range(4):
        g_out[core, i] = product[i, :, :, :, mine]
    got([swap])
    wires.close()


def token_grad_call(d_rows, middle, gates, dy, rows, router, wo, ot):
    return pl.pallas_call(
        token_grad_kernel,
        out_shape=[
            shape((ROWS, WIDTH), F32),
            shape((256, 768)),
            shape((128, WIDTH), F32),
            shape((2, 4, 4, 3, 16, 768)),
        ],
        in_specs=[vm()] * 8,
        out_specs=[vm()] * 4,
        scratch_shapes=[
            pltpu.VMEM((2, ROWS, WIDTH), BF),
            pltpu.VMEM((4, 4, 3, 16, WIDTH), BF),
            *sum_rows_scratch(TALL),
            *wire_sems(16),
        ],
        compiler_params=pltpu.CompilerParams(
            collective_id=4, has_side_effects=True, vmem_limit_bytes=VMEM_BYTES
        ),
        name="token_grad",
    )(d_rows.reshape(4, 2, 2, 2, 64, TALL), middle, gates, dy, rows, router, wo, ot)


def gather_sums(ref, landings, wires, at):
    orders = tuple(order[::-1] for order in ORDERS)
    waits = [[], [], []]

    def send(part, phase):
        fixed = orders[part][: phase + 1]
        dim = fixed[-1]
        for step in (1, 2, 3):
            peer = ring(at, dim, step)
            spot = ref.at[block_of(ref, part, fixed, peer)]
            waits[part].append(wires.go(spot, landings[part][phase].at[step - 1], peer))

    def add(part, phase):
        got(waits[part])
        waits[part] = []
        fixed = orders[part][: phase + 1]
        index = block_of(ref, part, fixed, at)
        total = ref[index].astype(F32)
        for step in range(3):
            total += landings[part][phase][step].astype(F32)
        ref[index] = total.astype(BF)

    for part in range(3):
        send(part, 0)
    yield
    for phase in range(3):
        for part in range(3):
            add(part, phase)
            if phase < 2:
                send(part, phase + 1)
        yield


def landing_shapes():
    sizes = {0: 2, 1: 4, 2: 4}
    found = []
    for order in ORDERS:
        back = order[::-1]
        for phase in range(3):
            fixed = back[: phase + 1]
            dims = [
                size
                for size, dim in ((2, 0), (4, 2), (4, 1))
                if dim not in fixed
            ]
            found.append(
                pltpu.VMEM((3, *dims, 16, QUARTER if 0 in fixed else HALF), BF)
            )
    return found


def last_kernel(
    dkv, dq, h1t, weights, g_out, small, x, d_mid, rows, cosine, sine,
    grad_in, g_q, g_k, g_v, g_o, g_m,
    whole, product, arrived, slots, taken, cos_v, sin_v, *rest,
):
    landings = [rest[3 * i : 3 * i + 3] for i in range(3)]
    chips = rest[9:15]
    ssem, rsem, lsem = rest[15:]
    at = place()
    xx, y, z, core = at
    xh, chip = xx // 2, y * 2 + xx // 2
    near = sibling(at)
    diagonal = sibling(ring(at, 0, 2))
    greet(all_peers(at) + [near, diagonal])
    wires = Wires(ssem, rsem)
    tables = [
        pltpu.make_async_copy(src.at[pl.ds(pl.multiple_of(chip * 256, 256), 256)], dst, lsem.at[i])
        for i, (src, dst) in enumerate(((cosine, cos_v), (sine, sin_v)))
    ]
    for copy in tables:
        copy.start()
    steps = sum_chips(dkv, chips, wires, at)
    next(steps)
    whole[:, :, :, :, :, COL_O:COL_M] = g_out[...]
    n, inverse = normed(x[...].astype(F32))
    parts = final(steps)
    for copy in tables:
        copy.wait()
    total = jnp.concatenate(parts, 0)
    dk = turn(total[:, 0:256], cos_v[...], -sin_v[...]).astype(BF)
    grads = jnp.concatenate([dq[...], dk, total[:, 256:512].astype(BF)], 1)
    into = weights[:, :, :, :, :, 0:COL_O].reshape(WIDTH, COL_O)
    back = dot_t(grads, into)
    product[0] = back[0:128]
    product[1] = back[128:256]
    swap = wires.go(product.at[1 - core], arrived, near)
    whole[:, :, :, :, :, 0:COL_O] = dot(h1t[...], grads).astype(BF).reshape(2, 4, 4, 3, 16, COL_O)
    got([swap])
    d_hidden = product[core] + arrived[...]
    line = jnp.sum(d_hidden * n, 0, keepdims=True)
    tiny = small[...] + jnp.where(iota((128, WIDTH), 0) == EXPERTS, line, 0.0)
    whole[:, :, :, :, :, COL_M:COL_END] = (
        jnp.transpose(tiny).astype(BF).reshape(2, 4, 4, 3, 16, 128)
    )
    whole[:, :, :, :, :, COL_END:HALF] = jnp.zeros((2, 4, 4, 3, 16, HALF - COL_END), BF)
    sums = gather_sums(whole, landings, wires, at)
    next(sums)
    grad_in[...] = d_mid[...] + norm_back(d_hidden, rows[0:1], n, inverse)
    for _ in sums:
        pass
    lanes = pl.ds(pl.multiple_of(xh * QUARTER, 128), QUARTER)
    unit = jnp.concatenate([whole[xx % 2, z, y, part, :, lanes] for part in range(3)], 0)
    slots[...] = dot(regroup_back(), unit).astype(BF).reshape(4, 16, QUARTER)
    mine = core * 2 + xh
    copies = [
        wires.go(slots.at[peer[0] // 2 * 2 + peer[3]], taken.at[mine], peer)
        for peer in (near, ring(at, 0, 2), diagonal)
    ]
    taken[mine] = slots[xh * 2 + core]
    got(copies)
    halves = [
        jnp.concatenate([taken[2 * i], taken[2 * i + 1]], 1).astype(F32)[0:12] for i in range(2)
    ]
    for i, half in enumerate(halves):
        g_q[:, 768 * i : 768 * i + 768] = half[:, 0:COL_K]
        g_k[:, 256 * i : 256 * i + 256] = half[:, COL_K:COL_V]
        g_v[:, 256 * i : 256 * i + 256] = half[:, COL_V:COL_O]
        g_o[:, 768 * i : 768 * i + 768] = half[:, COL_O:COL_M]
    g_m[...] = halves[0][:, COL_M:COL_END] + halves[1][:, COL_M:COL_END]
    wires.close()


def last_call(dkv, dq, h1t, weights, g_out, small, x, d_mid, rows, cosine, sine):
    return pl.pallas_call(
        last_kernel,
        out_shape=[
            shape((ROWS, WIDTH), F32),
            shape((12, WIDTH), F32),
            shape((12, 512), F32),
            shape((12, 512), F32),
            shape((12, WIDTH), F32),
            shape((12, 128), F32),
        ],
        in_specs=[vm()] * 9 + [hbm()] * 2,
        out_specs=[vm()] * 6,
        scratch_shapes=[
            pltpu.VMEM((2, 4, 4, 3, 16, HALF), BF),
            pltpu.VMEM((2, ROWS, WIDTH), F32),
            pltpu.VMEM((ROWS, WIDTH), F32),
            pltpu.VMEM((4, 16, QUARTER), BF),
            pltpu.VMEM((4, 16, QUARTER), BF),
            pltpu.VMEM((256, 128), F32),
            pltpu.VMEM((256, 128), F32),
            *landing_shapes(),
            *sum_scratch(128, 512),
            *wire_sems(48),
            pltpu.SemaphoreType.DMA((2,)),
        ],
        compiler_params=pltpu.CompilerParams(
            collective_id=6, has_side_effects=True, vmem_limit_bytes=VMEM_BYTES
        ),
        name="weight_grad",
    )(
        dkv.reshape(2, 4, 2, 128, 512), dq, h1t, weights, g_out, small, x, d_mid, rows,
        cosine, sine,
    )


def tables():
    frequency = np.exp(
        np.arange(HEAD // 2, dtype=np.float32) * np.float32(-2.0 * math.log(10000.0) / HEAD)
    )
    angles = np.arange(LENGTH, dtype=np.float32)[:, None] * frequency[None, :]
    cosine, sine = np.cos(angles), np.sin(angles)
    return (
        np.concatenate([cosine] * 4, 1).astype(np.float32),
        np.concatenate([-sine, sine] * 2, 1).astype(np.float32),
    )


def stage_weights(w_query, key_weight, value_weight, w_out, w_router, gain_attn, gain_ffn):
    small = jnp.concatenate([w_router, gain_attn[:, None], gain_ffn[:, None]], 1)
    halves = []
    for i in range(2):
        halves += [
            w_query[:, 768 * i : 768 * i + 768],
            key_weight[:, 256 * i : 256 * i + 256],
            value_weight[:, 256 * i : 256 * i + 256],
            w_out[:, 768 * i : 768 * i + 768],
            small,
            jnp.zeros((12, HALF - COL_M - 34), BF),
        ]
    wide = jnp.concatenate(halves, 1)
    wide = jnp.pad(wide, ((0, 4), (0, 0)))
    return jnp.stack([wide[:, QUARTER * i : QUARTER * i + QUARTER] for i in range(4)])


def body(
    block_in, routes, cotangent, gain_attn, w_query, key_weight, value_weight, w_out,
    gain_ffn, w_router, w_gate, w_up, w_down,
):
    gate_full = lax.all_gather(w_gate, "seq", axis=1, tiled=True)
    up_full = lax.all_gather(w_up, "seq", axis=1, tiled=True)
    down_full = lax.all_gather(w_down, "seq", axis=1, tiled=True)
    cosine, sine = (jnp.asarray(table) for table in tables())
    x, dy = block_in[0], cotangent[0]
    stage = stage_weights(
        w_query, key_weight, value_weight, w_out, w_router, gain_attn, gain_ffn
    )
    weights, wo, rows, router, q, kv, h1t = first_call(stage, x, cosine, sine)
    kv = kv.reshape(LENGTH, 512)
    o, ot, lse = attend_call(q, kv)
    all_dy = share_call(dy.reshape(2, 64, WIDTH))
    middle, gates, tall = middle_call(o, wo, x, routes[0], rows, router)
    out_rows, d_rows, g_gate, g_up, g_down = expert_call(tall, all_dy, gate_full, up_full, down_full)
    g_gate = lax.psum_scatter(g_gate, "seq", scatter_dimension=1, tiled=True)
    g_up = lax.psum_scatter(g_up, "seq", scatter_dimension=1, tiled=True)
    g_down = lax.psum_scatter(g_down, "seq", scatter_dimension=1, tiled=True)
    d_mid, d_o, small, g_out = token_grad_call(
        d_rows, middle, gates, dy, rows, router, wo, ot
    )
    block_out = block_out_call(out_rows, middle)
    dq, dkv = attend_back_call(q, kv, d_o, lse, cosine, sine)
    grad_in, g_q, g_k, g_v, g_o, g_m = last_call(
        dkv, dq, h1t, weights, g_out, small, x, d_mid, rows, cosine, sine
    )
    return (
        block_out[None],
        grad_in[None],
        g_m[:, EXPERTS],
        g_q,
        g_k,
        g_v,
        g_o,
        g_m[:, EXPERTS + 1],
        g_m[:, 0:EXPERTS],
        g_gate.astype(F32),
        g_up.astype(F32),
        g_down.astype(F32),
    )


def solution(mesh):
    tokens, owned, experts = P("seq", "ctx", None), P(("seq", "ctx"), None), P("ctx", "seq", None)
    vector = P(("seq", "ctx"))
    return jax.shard_map(
        body,
        mesh=mesh,
        in_specs=(
            tokens, tokens, tokens, vector, owned, owned, owned, owned, vector, owned,
            experts, experts, experts,
        ),
        out_specs=(
            tokens, tokens, vector, owned, owned, owned, owned, vector, owned,
            experts, experts, experts,
        ),
        check_vma=False,
    )
```

```python
import functools
import math

import jax
import jax.numpy as jnp
import numpy as np
from jax import lax
from jax.experimental import pallas as pl
from jax.experimental.pallas import tpu as pltpu
from jax.sharding import PartitionSpec as P

WIDTH = 1536
HEADS = 24
KV_HEADS = 8
HEAD = 64
TOPK = 8
ROWS = 128
LENGTH = 2048
EXPERTS = 32
FF = 512
CAP = 48
EPSILON = 1e-06

BF = jnp.bfloat16
F32 = jnp.float32
MESH = pl.DeviceIdType.MESH
VMEM_BYTES = 60 << 20

IN_Q, OUT_Q = 768, 384
IN_H, OUT_H = 2 * IN_Q, 2 * OUT_Q
STAGE = IN_Q + OUT_Q
COL_K, COL_V, COL_M, COL_END = 768, 1024, 1280, 1408
TALL = WIDTH + 128


def vm():
    return pl.BlockSpec(memory_space=pltpu.VMEM)


def hbm():
    return pl.BlockSpec(memory_space=pl.ANY)


def shape(dims, dtype=BF):
    return jax.ShapeDtypeStruct(dims, dtype)


def place():
    seq, ctx = lax.axis_index("seq"), lax.axis_index("ctx")
    return (ctx // 2 % 2 * 2 + seq // 4, ctx // 4, seq % 4, ctx % 2)


def device(x, y, z, core):
    return (x % 2 * 4 + z, (y * 2 + x // 2) * 2 + core)


def ring(at, dim, step):
    x, y, z, core = at
    if dim == 0:
        return ((x + step) % 4, y, z, core)
    if dim == 1:
        return (x, (y + step) % 4, z, core)
    return (x, y, (z + step) % 4, core)


def sibling(at):
    return (at[0], at[1], at[2], 1 - at[3])


def greet(peers):
    barrier = pltpu.get_barrier_semaphore()
    for peer in peers:
        pl.semaphore_signal(barrier, inc=1, device_id=device(*peer), device_id_type=MESH)
    pl.semaphore_wait(barrier, len(peers))


class Wires:
    def __init__(self, send, recv):
        self.send, self.recv, self.used, self.open = send, recv, 0, []

    def go(self, src, dst, peer):
        n = self.used
        self.used += 1
        copy = pltpu.make_async_remote_copy(
            src_ref=src,
            dst_ref=dst,
            send_sem=self.send.at[n],
            recv_sem=self.recv.at[n],
            device_id=device(*peer),
            device_id_type=MESH,
        )
        copy.start()
        self.open.append(copy)
        return copy

    def close(self):
        for copy in self.open:
            copy.wait_send()


def wire_sems(n):
    return [pltpu.SemaphoreType.DMA((n,)), pltpu.SemaphoreType.DMA((n,))]


def got(copies):
    for copy in copies:
        copy.wait_recv()


def dot(a, b):
    return jnp.dot(a, b, preferred_element_type=F32)


def dot_t(a, b):
    return lax.dot_general(a, b, (((1,), (1,)), ((), ())), preferred_element_type=F32)


def t_dot(a, b):
    return lax.dot_general(a, b, (((0,), (0,)), ((), ())), preferred_element_type=F32)


def iota(dims, axis):
    return lax.broadcasted_iota(jnp.int32, dims, axis)


def turn(block, cosine, sine):
    low = iota((block.shape[0], 128), 1) % HEAD < HEAD // 2
    parts = []
    for i in range(block.shape[1] // 128):
        unit = block[:, 128 * i : 128 * i + 128]
        other = jnp.where(low, pltpu.roll(unit, 96, 1), pltpu.roll(unit, 32, 1))
        parts.append(unit * cosine + other * sine)
    return jnp.concatenate(parts, 1)


def regroup():
    r, c = iota((48, 64), 0), iota((48, 64), 1)
    owner = c // 16 % 2 * 2 + c // 32
    hit = (r == owner * 12 + c % 16) & (c % 16 < 12)
    return hit.astype(F32).astype(BF)


def regroup_back():
    r, c = iota((64, 48), 0), iota((64, 48), 1)
    hit = (c == r // 16 * 12 + r % 16) & (r % 16 < 12)
    return hit.astype(F32).astype(BF)


ORDERS = ((0, 1, 2), (1, 2, 0), (2, 0, 1))


def block_of(quarter, part, fixed, at):
    x, y, z, _ = at
    whole = slice(None)
    columns = (
        pl.ds(pl.multiple_of(x // 2 * quarter, 128), quarter)
        if 0 in fixed
        else pl.ds(0, 2 * quarter)
    )
    return (
        x % 2 if 0 in fixed else whole,
        z if 2 in fixed else whole,
        y if 1 in fixed else whole,
        part,
        whole,
        columns,
    )


def spread(ref, quarter, wires, at):
    waits = [[], [], []]
    for phase in range(3):
        for part in range(3):
            got(waits[part])
            waits[part] = []
            fixed = ORDERS[part][phase:]
            spot = ref.at[block_of(quarter, part, fixed, at)]
            for step in (1, 2, 3):
                waits[part].append(wires.go(spot, spot, ring(at, fixed[0], step)))
        yield
    for part in range(3):
        got(waits[part])


def finish(*tasks):
    for task in tasks:
        for _ in task:
            pass


def partner(at):
    return (at[0] + 1 - 2 * (at[0] % 2), at[1], at[2], at[3])


def expert_pairs(shard, pair, wires, at):
    spot = pair.at[:, at[0] % 2]
    return wires.go(shard, spot, partner(at))


def expert_spread(own, full, wires, at):
    z = at[2]
    left, right = ring(at, 2, 3), ring(at, 2, 1)
    spot = full.at[:, :, z]
    a = wires.go(own, spot, right)
    b = wires.go(own, spot, left)
    yield
    got([a])
    spot = full.at[0, :, (z + 3) % 4]
    a = wires.go(spot, spot, right)
    got([b])
    spot = full.at[1, :, (z + 1) % 4]
    b = wires.go(spot, spot, left)
    yield
    got([a, b])


def expert_sum_scratch(rows, columns):
    return [
        pltpu.VMEM((3, 2, 2, rows, columns), BF),
        pltpu.VMEM((2, 2, rows, columns), BF),
        pltpu.VMEM((2, 2, 2, rows, columns), BF),
        pltpu.VMEM((2, rows, columns), BF),
        pltpu.SemaphoreType.DMA((3,)),
    ]


def expert_sum(grads, result, scratch, wires, at):
    own, halves, pairs, last, lsem = scratch
    z, x_lo = at[2], at[0] % 2
    left, right = ring(at, 2, 3), ring(at, 2, 1)
    loads = [
        pltpu.make_async_copy(grads.at[:, :, (z + step) % 4], own.at[i], lsem.at[i])
        for i, step in enumerate((0, 1, 3))
    ]
    for copy in loads:
        copy.start()
    a = wires.go(grads.at[0, :, (z + 2) % 4], halves.at[0], right)
    b = wires.go(grads.at[1, :, (z + 2) % 4], halves.at[1], left)
    yield
    for copy in loads:
        copy.wait()
    got([a])
    for i in range(2):
        own[1, 0, i] = (own[1, 0, i].astype(F32) + halves[0, i].astype(F32)).astype(BF)
    a = wires.go(own.at[1], pairs.at[0], right)
    got([b])
    for i in range(2):
        own[2, 1, i] = (own[2, 1, i].astype(F32) + halves[1, i].astype(F32)).astype(BF)
    b = wires.go(own.at[2], pairs.at[1], left)
    yield
    got([a, b])
    for e in range(2):
        for i in range(2):
            own[0, e, i] = (
                own[0, e, i].astype(F32)
                + pairs[0, e, i].astype(F32)
                + pairs[1, e, i].astype(F32)
            ).astype(BF)
    a = wires.go(own.at[0, :, 1 - x_lo], last, partner(at))
    yield
    got([a])
    for e in range(2):
        result[e] = own[0, e, x_lo].astype(F32) + last[e].astype(F32)


def ctx_peers(at):
    return [ring(at, 1, 1), ring(at, 1, 2), ring(at, 1, 3), ring(at, 0, 2)]


def all_peers(at):
    return [ring(at, d, s) for d in range(3) for s in (1, 2, 3)]


def first_kernel(
    stage, x, cosine, sine, w_gate, w_up, w_down,
    weights, rows, router, q, kv, h1t, unit_o, gate_full, up_pair, down_pair,
    both, slots, cos_v, sin_v, ssem, rsem, lsem,
):
    at = place()
    xx, y, z, core = at
    xh, chip = xx // 2, y * 2 + xx // 2
    diagonal = sibling(ring(at, 0, 2))
    greet(all_peers(at) + [sibling(at), diagonal])
    wires = Wires(ssem, rsem)
    local = [
        (cosine.at[pl.ds(pl.multiple_of(chip * 256, 256), 256)], cos_v),
        (sine.at[pl.ds(pl.multiple_of(chip * 256, 256), 256)], sin_v),
        (w_gate, gate_full.at[:, xx % 2, z]),
        (w_up, up_pair.at[:, xx % 2]),
        (w_down, down_pair.at[:, xx % 2]),
    ]
    local = [pltpu.make_async_copy(src, dst, lsem.at[i]) for i, (src, dst) in enumerate(local)]
    for copy in local:
        copy.start()
    mine = core * 2 + xh
    first = [
        wires.go(stage.at[peer[3] * 2 + peer[0] // 2], slots.at[mine], peer)
        for peer in (sibling(at), ring(at, 0, 2), diagonal)
    ]
    tokens = wires.go(x, both.at[core], sibling(at))
    slots[mine] = stage[mine]
    both[core] = x[...]
    got(first)
    unit = dot(regroup(), slots[...].reshape(64, STAGE)).astype(BF)
    lanes = pl.ds(pl.multiple_of(xh * IN_Q, 128), IN_Q)
    for part in range(3):
        weights[xx % 2, z, y, part, :, lanes] = unit[16 * part : 16 * part + 16, 0:IN_Q]
        unit_o[part] = unit[16 * part : 16 * part + 16, IN_Q:STAGE]
    task = spread(weights, IN_Q, wires, at)
    next(task)
    spot = gate_full.at[:, xx % 2, z]
    pair = wires.go(w_gate, spot, partner(at))
    finish(task)
    for copy in local:
        copy.wait()
    got([pair])
    gate = expert_spread(gate_full.at[:, :, z], gate_full, wires, at)
    next(gate)
    pairs = [
        expert_pairs(w_up, up_pair, wires, at),
        expert_pairs(w_down, down_pair, wires, at),
    ]

    small = weights[:, :, :, :, :, COL_M:COL_END].reshape(WIDTH, 128)
    router[...] = small
    turned = jnp.transpose(small.astype(F32))
    rows[...] = turned[32:40]
    got([tokens])
    values = both[...].reshape(256, WIDTH).astype(F32)
    inverse = lax.rsqrt(jnp.mean(values * values, -1, keepdims=True) + EPSILON)
    hidden = (values * inverse * turned[32:33]).astype(BF)
    made = dot(hidden, weights[:, :, :, :, :, 0:COL_M].reshape(WIDTH, COL_M))
    cos, sin = cos_v[...], sin_v[...]
    key = turn(made[:, COL_K:COL_V], cos, sin).astype(BF)
    value = made[:, COL_V:COL_M].astype(BF)
    for part in range(2):
        kv[y, xh, part, :, 0:256] = key[128 * part : 128 * part + 128]
        kv[y, xh, part, :, 256:512] = value[128 * part : 128 * part + 128]
    own = [kv.at[y, xh, 0], kv.at[y, xh, 1]]
    a = [wires.go(own[0], own[0], ring(at, 1, s)) for s in (1, 2, 3)]
    b = [wires.go(own[1], own[1], ring(at, 0, 2))]
    q[...] = turn(made[:, 0:COL_K], cos, sin).astype(BF)
    got(a)
    column = kv.at[:, xh, 0]
    a = [wires.go(column, column, ring(at, 0, 2))]
    got(b)
    pair = kv.at[y, :, 1]
    b = [wires.go(pair, pair, ring(at, 1, s)) for s in (1, 2, 3)]
    h1t[...] = jnp.transpose(hidden.astype(F32)).astype(BF)
    next(gate)
    got(a)
    got(b)
    finish(gate)
    got(pairs)
    wires.close()


def first_call(stage, x, cosine, sine, w_gate, w_up, w_down):
    return pl.pallas_call(
        first_kernel,
        out_shape=[
            shape((2, 4, 4, 3, 16, IN_H)),
            shape((8, WIDTH), F32),
            shape((WIDTH, 128)),
            shape((256, 768)),
            shape((4, 2, 2, 128, 512)),
            shape((WIDTH, 256)),
            shape((3, 16, OUT_Q)),
            shape((2, 2, 4, 192, FF)),
            shape((2, 2, 192, FF)),
            shape((2, 2, 64, WIDTH)),
        ],
        in_specs=[vm(), vm()] + [hbm()] * 5,
        out_specs=[vm()] * 7 + [hbm()] * 3,
        scratch_shapes=[
            pltpu.VMEM((2, 128, WIDTH), BF),
            pltpu.VMEM((4, 16, STAGE), BF),
            pltpu.VMEM((256, 128), F32),
            pltpu.VMEM((256, 128), F32),
            *wire_sems(56),
            pltpu.SemaphoreType.DMA((5,)),
        ],
        compiler_params=pltpu.CompilerParams(
            collective_id=1, has_side_effects=True, vmem_limit_bytes=VMEM_BYTES
        ),
        name="weights_qkv",
    )(stage, x, cosine, sine, w_gate, w_up, w_down)


def share_rows(ref, wires, at):
    x, y, _, core = at
    xh = x // 2
    near, far = sibling(at), ring(at, 0, 2)

    def pass_on(spot, peer):
        return wires.go(spot, spot, peer)

    inner = [pass_on(ref.at[y, xh, core], near)]
    a = [pass_on(ref.at[y, xh, core, 0], ring(at, 1, s)) for s in (1, 2, 3)]
    b = [pass_on(ref.at[y, xh, core, 1], far)]
    yield
    got(b)
    b = [pass_on(ref.at[y, :, core, 1], ring(at, 1, s)) for s in (1, 2, 3)]
    got(a)
    a = [pass_on(ref.at[:, xh, core, 0], far)]
    inner.append(pass_on(ref.at[y, 1 - xh, core, 1], near))
    for s in (1, 2, 3):
        inner.append(pass_on(ref.at[(y + s) % 4, xh, core, 0], near))
    yield
    got(a)
    inner.append(pass_on(ref.at[:, 1 - xh, core, 0], near))
    got(b)
    for s in (1, 2, 3):
        inner.append(pass_on(ref.at[(y + s) % 4, :, core, 1], near))
    yield
    got(inner)


def ctx_and_sibling(at):
    return ctx_peers(at) + [sibling(at)]


def sum_scratch(rows, columns):
    return [
        pltpu.VMEM((4, rows, columns), BF),
        pltpu.VMEM((3, 2, rows, columns), BF),
        pltpu.VMEM((4, rows, columns), BF),
        pltpu.VMEM((2, rows, columns), BF),
        pltpu.VMEM((3, rows, columns), BF),
        pltpu.VMEM((1, rows, columns), BF),
    ]


def sum_chips(source, scratch, wires, at):
    e0, e1, t0, t1, f0, f1 = scratch
    x, y, _, _ = at
    xh = x // 2
    far = ring(at, 0, 2)
    a = [wires.go(source.at[0, :, 1 - xh], e0, far)]
    b = [
        wires.go(source.at[1, (y + s) % 4], e1.at[s - 1], ring(at, 1, s)) for s in (1, 2, 3)
    ]
    yield None
    got(a)
    for i in range(4):
        t0[i] = (source[0, i, xh].astype(F32) + e0[i].astype(F32)).astype(BF)
    a = [wires.go(t0.at[(y + s) % 4], f0.at[s - 1], ring(at, 1, s)) for s in (1, 2, 3)]
    got(b)
    for i in range(2):
        total = source[1, y, i].astype(F32)
        for s in range(3):
            total += e1[s, i].astype(F32)
        t1[i] = total.astype(BF)
    b = [wires.go(t1.at[1 - xh], f1.at[0], far)]
    yield None
    got(a)
    first = t0[y].astype(F32)
    for s in range(3):
        first += f0[s].astype(F32)
    got(b)
    yield first, t1[xh].astype(F32) + f1[0].astype(F32)


def sum_rows_scratch(columns):
    return [
        pltpu.VMEM((2, 4, 2, 64, columns), BF),
        pltpu.VMEM((2, 4, 2, 64, columns), BF),
        *sum_scratch(64, columns),
    ]


def sum_rows(rows, scratch, wires, at):
    landed, own, rest = scratch[0], scratch[1], scratch[2:]
    core = at[3]
    copies = [
        wires.go(rows.at[:, :, 1 - core, part], landed.at[part], sibling(at)) for part in range(2)
    ]
    yield None
    for part in range(2):
        got([copies[part]])
        for i in range(4):
            for h in range(2):
                own[part, i, h] = (
                    rows[i, h, core, part].astype(F32) + landed[part, i, h].astype(F32)
                ).astype(BF)
    for result in sum_chips(own, rest, wires, at):
        yield result


def final(steps):
    result = None
    for result in steps:
        pass
    return result


def gather_sums(ref, quarter, landings, wires, at):
    orders = tuple(order[::-1] for order in ORDERS)
    waits = [[], [], []]

    def send(part, phase):
        fixed = orders[part][: phase + 1]
        dim = fixed[-1]
        for step in (1, 2, 3):
            peer = ring(at, dim, step)
            spot = ref.at[block_of(quarter, part, fixed, peer)]
            waits[part].append(wires.go(spot, landings[part][phase].at[step - 1], peer))

    def add(part, phase):
        got(waits[part])
        waits[part] = []
        fixed = orders[part][: phase + 1]
        index = block_of(quarter, part, fixed, at)
        total = ref[index].astype(F32)
        for step in range(3):
            total += landings[part][phase][step].astype(F32)
        ref[index] = total.astype(BF)

    for part in range(3):
        send(part, 0)
    yield
    for phase in range(3):
        for part in range(3):
            add(part, phase)
            if phase < 2:
                send(part, phase + 1)
        yield


def landing_shapes(quarter):
    found = []
    for order in ORDERS:
        for phase in range(3):
            fixed = order[::-1][: phase + 1]
            dims = [size for size, dim in ((2, 0), (4, 2), (4, 1)) if dim not in fixed]
            found.append(pltpu.VMEM((3, *dims, 16, quarter if 0 in fixed else 2 * quarter), BF))
    return found


def attend_kernel(
    q, kv, unit_o, dy, up_pair,
    o, ot, lse, wo, all_dy, up_full,
    scores, vt, qt, qz, out_t, columns, ssem, rsem, lsem,
):
    at = place()
    x, y, z, core = at
    chip = y * 2 + x // 2
    near = sibling(at)
    greet(all_peers(at) + [near])
    wires = Wires(ssem, rsem)
    local = [
        pltpu.make_async_copy(dy, all_dy.at[y, x // 2, core], lsem.at[0]),
        pltpu.make_async_copy(up_pair, up_full.at[:, :, z], lsem.at[1]),
    ]
    for copy in local:
        copy.start()
    lanes = pl.ds(pl.multiple_of(x // 2 * OUT_Q, 128), OUT_Q)
    for part in range(3):
        columns[x % 2, z, y, part, :, lanes] = unit_o[part]
    out_task = spread(columns, OUT_Q, wires, at)
    up_task = expert_spread(up_pair, up_full, wires, at)
    dy_task = share_rows(all_dy, wires, at)
    next(out_task)
    next(up_task)
    local[0].wait()
    next(dy_task)
    mine = pl.ds(pl.multiple_of(core * 768, 128), 768)

    def swap_out():
        finish(out_task)
        swap.append(
            wires.go(columns.at[1 - core], wo.at[:, :, :, :, mine], near)
        )
        for i in range(4):
            wo[i, :, :, :, mine] = columns[core, i]

    swap = []
    beside = [
        lambda: next(out_task),
        lambda: next(dy_task),
        lambda: next(out_task),
        lambda: next(up_task),
        swap_out,
        lambda: next(dy_task),
        lambda: finish(up_task),
        lambda: None,
    ]
    qt[...] = jnp.transpose(q[...].astype(F32) * 0.125).astype(BF)
    for kb in range(8):
        vt[kb] = jnp.transpose(kv[256 * kb : 256 * kb + 256, 256:512].astype(F32)).astype(BF)
    allowed = iota((256, 768), 0) <= iota((256, 768), 1) % 256
    for j in range(4):
        u, half = j // 2, j % 2
        qz[...] = jnp.zeros_like(qz)
        for g in range(3):
            h = 3 * j + g
            qz[64 * half : 64 * half + 64, 256 * g : 256 * g + 256] = qt[64 * h : 64 * h + 64]

        def score(kb):
            rows = pl.ds(pl.multiple_of(kb * 256, 256), 256)
            return rows, dot(kv[rows, 128 * u : 128 * u + 128], qz[...])

        def top(kb, most):
            rows, s = score(kb)
            scores[rows] = s
            return jnp.maximum(most, jnp.max(s.reshape(32, 8, 768), 0))

        most = lax.fori_loop(0, chip, top, jnp.full((8, 768), -1e30, F32))
        rows, s = score(chip)
        s = jnp.where(allowed, s, -1e30)
        scores[rows] = s
        most = jnp.maximum(most, jnp.max(s.reshape(32, 8, 768), 0))
        most = jnp.max(most, 0, keepdims=True)

        def raise_(kb, total):
            rows = pl.ds(pl.multiple_of(kb * 256, 256), 256)
            e = jnp.exp(scores[rows] - most)
            scores[rows] = e
            return total + jnp.sum(e.reshape(32, 8, 768), 0)

        beside[2 * j]()
        total = lax.fori_loop(0, chip + 1, raise_, jnp.zeros((8, 768), F32))
        total = jnp.sum(total, 0, keepdims=True)
        lse[j] = jnp.broadcast_to(most + jnp.log(total), (8, 768))
        inverse = 1.0 / total

        def mix(kb, acc):
            rows = pl.ds(pl.multiple_of(kb * 256, 256), 256)
            p = (scores[rows] * inverse).astype(BF)
            return acc + dot(vt[kb, 64 * j : 64 * j + 64], p)

        acc = lax.fori_loop(0, chip + 1, mix, jnp.zeros((64, 768), F32))
        for g in range(3):
            h = 3 * j + g
            out_t[64 * h : 64 * h + 64] = acc[:, 256 * g : 256 * g + 256]
        beside[2 * j + 1]()
    ot[...] = out_t[...].astype(BF)
    o[...] = jnp.transpose(out_t[...]).astype(BF)
    finish(dy_task)
    got(swap)
    local[1].wait()
    wires.close()


def attend_call(q, kv, unit_o, dy, up_pair):
    return pl.pallas_call(
        attend_kernel,
        out_shape=[
            shape((256, 768)),
            shape((768, 256)),
            shape((4, 8, 768), F32),
            shape((4, 4, 3, 16, WIDTH)),
            shape((4, 2, 2, 2, 64, WIDTH)),
            shape((2, 2, 4, 192, FF)),
        ],
        in_specs=[vm()] * 3 + [hbm()] * 2,
        out_specs=[vm()] * 4 + [hbm()] * 2,
        scratch_shapes=[
            pltpu.VMEM((LENGTH, 768), F32),
            pltpu.VMEM((8, 256, 256), BF),
            pltpu.VMEM((768, 256), BF),
            pltpu.VMEM((128, 768), BF),
            pltpu.VMEM((768, 256), F32),
            pltpu.VMEM((2, 4, 4, 3, 16, OUT_H), BF),
            *wire_sems(56),
            pltpu.SemaphoreType.DMA((2,)),
        ],
        compiler_params=pltpu.CompilerParams(
            collective_id=2, has_side_effects=True, vmem_limit_bytes=VMEM_BYTES
        ),
        name="attend",
    )(q, kv, unit_o, dy, up_pair)


def attend_back_kernel(
    q, kv, d_o, lse, out_rows, middle, g_out, g_gate, cosine, sine,
    dq, dkv, block_out, unit_o, gate_sum,
    probs, grads, kt, qt, dot_, qz, oz, acc, dqt, cos_v, sin_v, columns, *rest,
):
    row_scratch, landings = rest[:8], [rest[8 + 3 * i : 11 + 3 * i] for i in range(3)]
    expert_scratch = rest[17:22]
    ssem, rsem, lsem = rest[22:]
    at = place()
    xx, y, z, _ = at
    chip = y * 2 + xx // 2
    greet(all_peers(at) + [sibling(at)])
    wires = Wires(ssem, rsem)
    columns_in = pltpu.make_async_copy(g_out, columns, lsem.at[2])
    columns_in.start()
    tables = [
        pltpu.make_async_copy(src.at[pl.ds(pl.multiple_of(chip * 256, 256), 256)], dst, lsem.at[i])
        for i, (src, dst) in enumerate(((cosine, cos_v), (sine, sin_v)))
    ]
    for copy in tables:
        copy.start()
    row_task = sum_rows(out_rows, row_scratch, wires, at)
    gate_task = expert_sum(g_gate, gate_sum, expert_scratch, wires, at)
    out_task = gather_sums(columns, OUT_Q, landings, wires, at)
    next(row_task)
    next(gate_task)

    def start_out():
        columns_in.wait()
        next(out_task)

    beside = [
        lambda: next(row_task),
        lambda: next(gate_task),
        start_out,
        lambda: next(gate_task),
        lambda: next(row_task),
        lambda: next(out_task),
        lambda: finish(gate_task),
        lambda: next(out_task),
    ]
    qt[...] = jnp.transpose(q[...].astype(F32) * 0.125).astype(BF)
    dot_[...] = jnp.transpose(d_o[...].astype(F32)).astype(BF)
    for kb in range(8):
        kt[kb] = jnp.transpose(kv[256 * kb : 256 * kb + 256, 0:256].astype(F32)).astype(BF)
    acc[...] = jnp.zeros_like(acc)
    allowed = iota((256, 768), 0) <= iota((256, 768), 1) % 256
    for j in range(4):
        u, half = j // 2, j % 2
        qz[...] = jnp.zeros_like(qz)
        oz[...] = jnp.zeros_like(oz)
        for g in range(3):
            h = 3 * j + g
            qz[64 * half : 64 * half + 64, 256 * g : 256 * g + 256] = qt[64 * h : 64 * h + 64]
            oz[64 * half : 64 * half + 64, 256 * g : 256 * g + 256] = dot_[64 * h : 64 * h + 64]
        level = lse[j, 0:1]

        def share(kb, centre, masked):
            rows = pl.ds(pl.multiple_of(kb * 256, 256), 256)
            p = jnp.exp(dot(kv[rows, 128 * u : 128 * u + 128], qz[...]) - level)
            if masked:
                p = jnp.where(allowed, p, 0.0)
            probs[rows] = p
            dp = dot(kv[rows, 256 + 128 * u : 384 + 128 * u], oz[...])
            grads[rows] = dp
            acc[rows, 256 + 128 * u : 384 + 128 * u] += dot_t(p.astype(BF), oz[...])
            return centre + jnp.sum((p * dp).reshape(32, 8, 768), 0)

        centre = lax.fori_loop(
            0, chip, functools.partial(share, masked=False), jnp.zeros((8, 768), F32)
        )
        centre = share(chip, centre, True)
        centre = jnp.sum(centre, 0, keepdims=True)
        beside[2 * j]()

        def back(kb, total):
            rows = pl.ds(pl.multiple_of(kb * 256, 256), 256)
            ds = (probs[rows] * (grads[rows] - centre)).astype(BF)
            acc[rows, 128 * u : 128 * u + 128] += dot_t(ds, qz[...])
            return total + dot(kt[kb, 64 * j : 64 * j + 64], ds)

        total = lax.fori_loop(0, chip + 1, back, jnp.zeros((64, 768), F32))
        for g in range(3):
            h = 3 * j + g
            dqt[64 * h : 64 * h + 64] = total[:, 256 * g : 256 * g + 256] * 0.125
        beside[2 * j + 1]()
    for kb in range(8):
        for part in range(2):
            at_row = 256 * kb + 128 * part
            dkv[part, kb] = acc[at_row : at_row + 128].astype(BF)
    for copy in tables:
        copy.wait()
    dq[...] = turn(jnp.transpose(dqt[...]), cos_v[...], -sin_v[...]).astype(BF)
    parts = final(row_task)
    for part in range(2):
        cut = slice(64 * part, 64 * part + 64)
        block_out[cut] = (middle[cut] + parts[part]).astype(BF)
    finish(out_task)
    lanes = pl.ds(pl.multiple_of(xx // 2 * OUT_Q, 128), OUT_Q)
    for part in range(3):
        unit_o[part] = columns[xx % 2, z, y, part, :, lanes]
    wires.close()


def attend_back_call(q, kv, d_o, lse, out_rows, middle, g_out, g_gate, cosine, sine):
    return pl.pallas_call(
        attend_back_kernel,
        out_shape=[
            shape((256, 768)),
            shape((2, 8, 128, 512)),
            shape((ROWS, WIDTH)),
            shape((3, 16, OUT_Q)),
            shape((2, 192, FF), F32),
        ],
        in_specs=[vm()] * 6 + [hbm()] * 4,
        out_specs=[vm()] * 5,
        scratch_shapes=[
            pltpu.VMEM((LENGTH, 768), F32),
            pltpu.VMEM((LENGTH, 768), F32),
            pltpu.VMEM((8, 256, 256), BF),
            pltpu.VMEM((768, 256), BF),
            pltpu.VMEM((768, 256), BF),
            pltpu.VMEM((128, 768), BF),
            pltpu.VMEM((128, 768), BF),
            pltpu.VMEM((LENGTH, 512), F32),
            pltpu.VMEM((768, 256), F32),
            pltpu.VMEM((256, 128), F32),
            pltpu.VMEM((256, 128), F32),
            pltpu.VMEM((2, 4, 4, 3, 16, OUT_H), BF),
            *sum_rows_scratch(WIDTH),
            *landing_shapes(OUT_Q),
            *expert_sum_scratch(192, FF),
            *wire_sems(56),
            pltpu.SemaphoreType.DMA((3,)),
        ],
        compiler_params=pltpu.CompilerParams(
            collective_id=5, has_side_effects=True, vmem_limit_bytes=VMEM_BYTES
        ),
        name="attend_back",
    )(
        q, kv, d_o, lse, out_rows.reshape(4, 2, 2, 2, 64, WIDTH), middle, g_out,
        g_gate.reshape(2, 2, 4, 192, FF), cosine, sine,
    )


def normed(values):
    inverse = lax.rsqrt(jnp.mean(values * values, -1, keepdims=True) + EPSILON)
    return values * inverse, inverse


def middle_kernel(
    o, wo, x, routes, rows, router, down_pair,
    middle, gates, tall, down_full,
    product, arrived, ssem, rsem, lsem,
):
    at = place()
    xx, y, z, core = at
    near = sibling(at)
    greet(ctx_and_sibling(at) + [ring(at, 2, 1), ring(at, 2, 3)])
    wires = Wires(ssem, rsem)
    local = pltpu.make_async_copy(down_pair, down_full.at[:, :, z], lsem)
    local.start()
    down_task = expert_spread(down_pair, down_full, wires, at)
    next(down_task)
    full = wo[...].reshape(768, WIDTH)
    product[0] = dot(o[1 - core], full)
    swap = wires.go(product.at[0], arrived, near)
    product[1] = dot(o[core], full)
    lane = iota((ROWS, 128), 1)
    named = routes[:, 0:1] == lane
    for i in range(1, TOPK):
        named = named | (routes[:, i : i + 1] == lane)
    got([swap])
    mid = x[...].astype(F32) + product[1] + arrived[...]
    middle[...] = mid
    hidden = (normed(mid)[0] * rows[1:2]).astype(BF)
    logits = jnp.where(named, dot(hidden, router[...]), -jnp.inf)
    raised = jnp.exp(logits - jnp.max(logits, -1, keepdims=True))
    gate = raised / jnp.sum(raised, -1, keepdims=True)
    gates[...] = gate
    high = gate.astype(BF).astype(F32)
    both = high + pltpu.roll(gate - high, EXPERTS, 1)
    for part in range(2):
        cut = slice(64 * part, 64 * part + 64)
        tall[y, xx // 2, core, part, :, 0:WIDTH] = hidden[cut]
        tall[y, xx // 2, core, part, :, WIDTH:TALL] = both[cut].astype(BF)
    share = share_rows(tall, wires, at)
    next(share)
    next(share)
    next(down_task)
    finish(share, down_task)
    local.wait()
    wires.close()


def middle_call(o, wo, x, routes, rows, router, down_pair):
    return pl.pallas_call(
        middle_kernel,
        out_shape=[
            shape((ROWS, WIDTH), F32),
            shape((ROWS, 128), F32),
            shape((4, 2, 2, 2, 64, TALL)),
            shape((2, 2, 4, 64, WIDTH)),
        ],
        in_specs=[vm()] * 6 + [hbm()],
        out_specs=[vm()] * 3 + [hbm()],
        scratch_shapes=[
            pltpu.VMEM((2, ROWS, WIDTH), F32),
            pltpu.VMEM((ROWS, WIDTH), F32),
            *wire_sems(32),
            pltpu.SemaphoreType.DMA,
        ],
        compiler_params=pltpu.CompilerParams(
            collective_id=3, has_side_effects=True, vmem_limit_bytes=VMEM_BYTES
        ),
        name="middle",
    )(o.reshape(2, ROWS, 768), wo, x, routes, rows, router, down_pair)


def expert_kernel(
    tall, dy, w_gate, w_up, w_down,
    out_rows, d_rows, g_gate, g_up, g_down,
    big, wide, a_rows, y_rows, r_rows, back, wg, wu, wd, gg, gu, gd, m_s, dg_s, du_s, slot_t, sem,
):
    ctx = lax.axis_index("ctx")
    loads = [
        pltpu.make_async_copy(src, dst, sem.at[i])
        for i, (src, dst) in enumerate(
            ((tall, big), (dy, wide), (w_gate, wg), (w_up, wu), (w_down, wd))
        )
    ]
    for copy in loads:
        copy.start()
    lane = iota((128, 128), 1)
    earlier = (iota((128, 128), 1) < iota((128, 128), 0)).astype(F32).astype(BF)
    slots = iota((CAP, 128), 0).astype(F32)
    loads[0].wait()
    loads[1].wait()

    def collect(b, _):
        rows = pl.ds(pl.multiple_of(b * 128, 128), 128)
        packed = pl.ds(pl.multiple_of(b * CAP, CAP), CAP)
        both = big[rows, WIDTH:TALL].astype(F32)
        gate = both + pltpu.roll(both, 128 - EXPERTS, 1)
        hot = (gate > 0.0) & (lane < EXPERTS)
        rank = dot(earlier, hot.astype(F32).astype(BF))
        slot = jnp.where(hot, rank, -1.0)
        slot_t[...] = jnp.transpose(slot)
        picks = [
            (slot_t[pl.ds(2 * ctx + i, 1), :] == slots).astype(F32).astype(BF) for i in range(2)
        ]
        pick = jnp.concatenate(picks, 0)
        found = dot(pick, big[rows, :]).astype(BF)
        grads = dot(pick, wide[rows, :]).astype(BF)
        for i in range(2):
            a_rows[i, packed] = found[CAP * i : CAP * i + CAP]
            y_rows[i, packed] = grads[CAP * i : CAP * i + CAP]
        column = [
            jnp.sum(jnp.where(lane == 2 * ctx + i, slot, 0.0), 1, keepdims=True) for i in range(2)
        ]
        spot = lane.astype(F32)
        put = jnp.where(lane < CAP, column[0], column[1] + CAP) == spot
        back[b] = put.astype(F32).astype(BF)
        return 0

    lax.fori_loop(0, 16, collect, 0)
    for copy in loads[2:]:
        copy.wait()
    stores = []
    for e in range(2):
        number = 2 * ctx + e

        def forward(c, _):
            rows = pl.ds(pl.multiple_of(c * 384, 384), 384)
            a = a_rows[e, rows, 0:WIDTH]
            ag, au = dot(a, wg[e]), dot(a, wu[e])
            sg = jax.nn.sigmoid(ag)
            act = ag * sg
            m = (act * au).astype(BF)
            r = dot(m, wd[e]).astype(BF).astype(F32)
            lanes = iota((384, 128), 1)
            hits = (lanes == number) | (lanes == number + EXPERTS)
            gate = jnp.sum(
                jnp.where(hits, a_rows[e, rows, WIDTH:TALL].astype(F32), 0.0), 1, keepdims=True
            )
            y = y_rows[e, rows].astype(F32)
            d_gate = jnp.sum(y * r, 1, keepdims=True)
            r_rows[e, rows] = (gate * r).astype(BF)
            gr = (gate * y).astype(BF)
            y_rows[e, rows] = gr
            dm = dot_t(gr, wd[e])
            m_s[rows] = m
            dg_s[rows] = (dm * au * (sg * (1.0 + ag * (1.0 - sg)))).astype(BF)
            du_s[rows] = (dm * act).astype(BF)
            high = d_gate.astype(BF).astype(F32)
            d_both = jnp.where(
                lanes == number, high, jnp.where(lanes == number + EXPERTS, d_gate - high, 0.0)
            )
            a_rows[e, rows, WIDTH:TALL] = d_both.astype(BF)
            return 0

        lax.fori_loop(0, 2, forward, 0)
        gd[e] = t_dot(m_s[...], y_rows[e]).astype(BF)
        gg[e] = t_dot(a_rows[e, :, 0:WIDTH], dg_s[...]).astype(BF)
        gu[e] = t_dot(a_rows[e, :, 0:WIDTH], du_s[...]).astype(BF)
        for i, (src, dst) in enumerate(((gd, g_down), (gg, g_gate), (gu, g_up))):
            copy = pltpu.make_async_copy(src.at[e], dst.at[e], sem.at[5 + 3 * e + i])
            copy.start()
            stores.append(copy)

        def to_tokens(c, _):
            rows = pl.ds(pl.multiple_of(c * 384, 384), 384)
            back_rows = dot_t(dg_s[rows], wg[e]) + dot_t(du_s[rows], wu[e])
            a_rows[e, rows, 0:WIDTH] = back_rows.astype(BF)
            return 0

        lax.fori_loop(0, 2, to_tokens, 0)

    def hand_back(b, _):
        rows = pl.ds(pl.multiple_of(b * 128, 128), 128)
        packed = pl.ds(pl.multiple_of(b * CAP, CAP), CAP)
        put = back[b][:, 0 : 2 * CAP]
        big[rows, :] = dot(put, jnp.concatenate([a_rows[0, packed], a_rows[1, packed]], 0)).astype(BF)
        wide[rows, :] = dot(put, jnp.concatenate([r_rows[0, packed], r_rows[1, packed]], 0)).astype(BF)
        return 0

    lax.fori_loop(0, 16, hand_back, 0)
    for i, (src, dst) in enumerate(((big, d_rows), (wide, out_rows))):
        copy = pltpu.make_async_copy(src, dst, sem.at[i])
        copy.start()
        stores.append(copy)
    for copy in stores:
        copy.wait()


def expert_call(tall, dy, w_gate, w_up, w_down):
    slots = 16 * CAP
    return pl.pallas_call(
        expert_kernel,
        out_shape=[
            shape((LENGTH, WIDTH)),
            shape((LENGTH, TALL)),
            shape((2, WIDTH, FF)),
            shape((2, WIDTH, FF)),
            shape((2, FF, WIDTH)),
        ],
        in_specs=[hbm()] * 5,
        out_specs=[hbm()] * 5,
        scratch_shapes=[
            pltpu.VMEM((LENGTH, TALL), BF),
            pltpu.VMEM((LENGTH, WIDTH), BF),
            pltpu.VMEM((2, slots, TALL), BF),
            pltpu.VMEM((2, slots, WIDTH), BF),
            pltpu.VMEM((2, slots, WIDTH), BF),
            pltpu.VMEM((16, 128, 128), BF),
            pltpu.VMEM((2, WIDTH, FF), BF),
            pltpu.VMEM((2, WIDTH, FF), BF),
            pltpu.VMEM((2, FF, WIDTH), BF),
            pltpu.VMEM((2, WIDTH, FF), BF),
            pltpu.VMEM((2, WIDTH, FF), BF),
            pltpu.VMEM((2, FF, WIDTH), BF),
            pltpu.VMEM((slots, FF), BF),
            pltpu.VMEM((slots, FF), BF),
            pltpu.VMEM((slots, FF), BF),
            pltpu.VMEM((128, 128), F32),
            pltpu.SemaphoreType.DMA((11,)),
        ],
        compiler_params=pltpu.CompilerParams(vmem_limit_bytes=VMEM_BYTES),
        name="experts",
    )(
        tall.reshape(LENGTH, TALL), dy.reshape(LENGTH, WIDTH), w_gate.reshape(2, WIDTH, FF),
        w_up.reshape(2, WIDTH, FF), w_down.reshape(2, FF, WIDTH),
    )


def split_dot(left, right, form):
    high = left.astype(BF)
    low = (left - high.astype(F32)).astype(BF)
    return form(high, right) + form(low, right)


def norm_back(grad, gain, n, inverse):
    scaled = grad * gain
    return inverse * (scaled - n * jnp.mean(scaled * n, -1, keepdims=True))


def token_grad_kernel(
    d_rows, middle, gates, dy, rows, router, wo, ot, g_down,
    d_mid, d_o, small, g_out, down_sum,
    low, product, *rest,
):
    scratch, expert_scratch, (ssem, rsem) = rest[:8], rest[8:13], rest[13:]
    at = place()
    core = at[3]
    near = sibling(at)
    greet(ctx_and_sibling(at) + [ring(at, 2, 1), ring(at, 2, 3), partner(at)])
    wires = Wires(ssem, rsem)
    steps = sum_rows(d_rows, scratch, wires, at)
    next(steps)
    down_task = expert_sum(g_down, down_sum, expert_scratch, wires, at)
    next(down_task)
    next(steps)
    next(down_task)
    n, inverse = normed(middle[...])
    hidden = (n * rows[1:2]).astype(BF)
    parts = final(steps)
    total = jnp.concatenate(parts, 0)
    d_hidden = total[:, 0:WIDTH]
    both = total[:, WIDTH:TALL]
    gate = gates[...]
    lane = iota((ROWS, 128), 1)
    d_gate = jnp.where(lane < EXPERTS, both + pltpu.roll(both, 128 - EXPERTS, 1), 0.0)
    centre = jnp.sum(gate * d_gate, -1, keepdims=True)
    d_logits = gate * (d_gate - centre)
    d_hidden += split_dot(d_logits, router[...], dot_t)
    d_middle = norm_back(d_hidden, rows[1:2], n, inverse) + dy[...].astype(F32)
    d_low = d_middle.astype(BF)
    low[core] = d_low
    swap = wires.go(low.at[core], low.at[core], near)
    d_mid[...] = d_middle
    grads = split_dot(jnp.transpose(d_logits), hidden, dot)
    line = jnp.sum(d_hidden * n, 0, keepdims=True)
    small[...] = grads + jnp.where(iota((128, WIDTH), 0) == EXPERTS + 1, line, 0.0)
    next(down_task)
    got([swap])
    chip_rows = low[...].reshape(256, WIDTH)
    d_o[...] = dot_t(chip_rows, wo[...].reshape(768, WIDTH)).astype(BF)
    product[...] = dot(ot[...], chip_rows).astype(BF).reshape(4, 4, 3, 16, WIDTH)
    lanes = pl.ds(pl.multiple_of((1 - core) * 768, 128), 768)
    mine = pl.ds(pl.multiple_of(core * 768, 128), 768)
    swap = wires.go(product.at[:, :, :, :, lanes], g_out.at[core], near)
    for i in range(4):
        g_out[core, i] = product[i, :, :, :, mine]
    finish(down_task)
    got([swap])
    wires.close()


def token_grad_call(d_rows, middle, gates, dy, rows, router, wo, ot, g_down):
    return pl.pallas_call(
        token_grad_kernel,
        out_shape=[
            shape((ROWS, WIDTH), F32),
            shape((256, 768)),
            shape((128, WIDTH), F32),
            shape((2, 4, 4, 3, 16, 768)),
            shape((2, 64, WIDTH), F32),
        ],
        in_specs=[vm()] * 8 + [hbm()],
        out_specs=[vm()] * 5,
        scratch_shapes=[
            pltpu.VMEM((2, ROWS, WIDTH), BF),
            pltpu.VMEM((4, 4, 3, 16, WIDTH), BF),
            *sum_rows_scratch(TALL),
            *expert_sum_scratch(64, WIDTH),
            *wire_sems(24),
        ],
        compiler_params=pltpu.CompilerParams(
            collective_id=4, has_side_effects=True, vmem_limit_bytes=VMEM_BYTES
        ),
        name="token_grad",
    )(
        d_rows.reshape(4, 2, 2, 2, 64, TALL), middle, gates, dy, rows, router, wo, ot,
        g_down.reshape(2, 2, 4, 64, WIDTH),
    )


def last_kernel(
    dkv, dq, h1t, weights, unit_o, small, x, d_mid, rows, g_up, cosine, sine,
    grad_in, g_q, g_k, g_v, g_o, g_m, up_sum,
    whole, product, arrived, slots, taken, cos_v, sin_v, *rest,
):
    landings = [rest[3 * i : 3 * i + 3] for i in range(3)]
    chips, expert_scratch = rest[9:15], rest[15:20]
    ssem, rsem, lsem = rest[20:]
    at = place()
    xx, y, z, core = at
    xh, chip = xx // 2, y * 2 + xx // 2
    near = sibling(at)
    diagonal = sibling(ring(at, 0, 2))
    greet(all_peers(at) + [near, diagonal])
    wires = Wires(ssem, rsem)
    tables = [
        pltpu.make_async_copy(src.at[pl.ds(pl.multiple_of(chip * 256, 256), 256)], dst, lsem.at[i])
        for i, (src, dst) in enumerate(((cosine, cos_v), (sine, sin_v)))
    ]
    for copy in tables:
        copy.start()
    steps = sum_chips(dkv, chips, wires, at)
    next(steps)
    up_task = expert_sum(g_up, up_sum, expert_scratch, wires, at)
    next(up_task)
    n, inverse = normed(x[...].astype(F32))
    next(steps)
    next(up_task)
    parts = final(steps)
    for copy in tables:
        copy.wait()
    total = jnp.concatenate(parts, 0)
    dk = turn(total[:, 0:256], cos_v[...], -sin_v[...]).astype(BF)
    grads = jnp.concatenate([dq[...], dk, total[:, 256:512].astype(BF)], 1)
    into = weights[:, :, :, :, :, 0:COL_M].reshape(WIDTH, COL_M)
    back = dot_t(grads, into)
    product[0] = back[0:128]
    product[1] = back[128:256]
    swap = wires.go(product.at[1 - core], arrived, near)
    whole[:, :, :, :, :, 0:COL_M] = dot(h1t[...], grads).astype(BF).reshape(2, 4, 4, 3, 16, COL_M)
    whole[:, :, :, :, :, COL_END:IN_H] = jnp.zeros((2, 4, 4, 3, 16, IN_H - COL_END), BF)
    got([swap])
    d_hidden = product[core] + arrived[...]
    line = jnp.sum(d_hidden * n, 0, keepdims=True)
    tiny = small[...] + jnp.where(iota((128, WIDTH), 0) == EXPERTS, line, 0.0)
    whole[:, :, :, :, :, COL_M:COL_END] = (
        jnp.transpose(tiny).astype(BF).reshape(2, 4, 4, 3, 16, 128)
    )
    sums = gather_sums(whole, IN_Q, landings, wires, at)
    next(sums)
    grad_in[...] = d_mid[...] + norm_back(d_hidden, rows[0:1], n, inverse)
    next(up_task)
    finish(sums, up_task)
    lanes = pl.ds(pl.multiple_of(xh * IN_Q, 128), IN_Q)
    unit = jnp.concatenate([whole[xx % 2, z, y, part, :, lanes] for part in range(3)], 0)
    unit = jnp.concatenate([unit, unit_o[...].reshape(48, OUT_Q)], 1)
    slots[...] = dot(regroup_back(), unit).astype(BF).reshape(4, 16, STAGE)
    mine = core * 2 + xh
    copies = [
        wires.go(slots.at[peer[0] // 2 * 2 + peer[3]], taken.at[mine], peer)
        for peer in (near, ring(at, 0, 2), diagonal)
    ]
    taken[mine] = slots[xh * 2 + core]
    got(copies)
    tiny = jnp.zeros((12, 128), F32)
    for i in range(2):
        left, right = taken[2 * i].astype(F32)[0:12], taken[2 * i + 1].astype(F32)[0:12]
        g_q[:, 768 * i : 768 * i + 768] = left[:, 0:IN_Q]
        g_k[:, 256 * i : 256 * i + 256] = right[:, 0:256]
        g_v[:, 256 * i : 256 * i + 256] = right[:, 256:512]
        g_o[:, 768 * i : 768 * i + OUT_Q] = left[:, IN_Q:STAGE]
        g_o[:, 768 * i + OUT_Q : 768 * i + 768] = right[:, IN_Q:STAGE]
        tiny += right[:, 512:640]
    g_m[...] = tiny
    wires.close()


def last_call(dkv, dq, h1t, weights, unit_o, small, x, d_mid, rows, g_up, cosine, sine):
    return pl.pallas_call(
        last_kernel,
        out_shape=[
            shape((ROWS, WIDTH), F32),
            shape((12, WIDTH), F32),
            shape((12, 512), F32),
            shape((12, 512), F32),
            shape((12, WIDTH), F32),
            shape((12, 128), F32),
            shape((2, 192, FF), F32),
        ],
        in_specs=[vm()] * 9 + [hbm()] * 3,
        out_specs=[vm()] * 7,
        scratch_shapes=[
            pltpu.VMEM((2, 4, 4, 3, 16, IN_H), BF),
            pltpu.VMEM((2, ROWS, WIDTH), F32),
            pltpu.VMEM((ROWS, WIDTH), F32),
            pltpu.VMEM((4, 16, STAGE), BF),
            pltpu.VMEM((4, 16, STAGE), BF),
            pltpu.VMEM((256, 128), F32),
            pltpu.VMEM((256, 128), F32),
            *landing_shapes(IN_Q),
            *sum_scratch(128, 512),
            *expert_sum_scratch(192, FF),
            *wire_sems(56),
            pltpu.SemaphoreType.DMA((2,)),
        ],
        compiler_params=pltpu.CompilerParams(
            collective_id=6, has_side_effects=True, vmem_limit_bytes=VMEM_BYTES
        ),
        name="weight_grad",
    )(
        dkv.reshape(2, 4, 2, 128, 512), dq, h1t, weights, unit_o, small, x, d_mid, rows,
        g_up.reshape(2, 2, 4, 192, FF), cosine, sine,
    )


def tables():
    frequency = np.exp(
        np.arange(HEAD // 2, dtype=np.float32) * np.float32(-2.0 * math.log(10000.0) / HEAD)
    )
    angles = np.arange(LENGTH, dtype=np.float32)[:, None] * frequency[None, :]
    cosine, sine = np.cos(angles), np.sin(angles)
    return (
        np.concatenate([cosine] * 4, 1).astype(np.float32),
        np.concatenate([-sine, sine] * 2, 1).astype(np.float32),
    )


def stage_weights(w_query, key_weight, value_weight, w_out, w_router, gain_attn, gain_ffn):
    small = jnp.concatenate([w_router, gain_attn[:, None], gain_ffn[:, None]], 1)
    small = jnp.pad(small, ((0, 0), (0, IN_H - COL_M - EXPERTS - 2)))
    quarters = []
    for i in range(2):
        own_out = w_out[:, 768 * i : 768 * i + 768]
        quarters.append([w_query[:, 768 * i : 768 * i + 768], own_out[:, :OUT_Q]])
        quarters.append(
            [
                key_weight[:, 256 * i : 256 * i + 256],
                value_weight[:, 256 * i : 256 * i + 256],
                small,
                own_out[:, OUT_Q:],
            ]
        )
    stage = jnp.stack([jnp.concatenate(quarter, 1) for quarter in quarters])
    return jnp.pad(stage, ((0, 0), (0, 4), (0, 0)))


def body(
    block_in, routes, cotangent, gain_attn, w_query, key_weight, value_weight, w_out,
    gain_ffn, w_router, w_gate, w_up, w_down,
):
    cosine, sine = (jnp.asarray(table) for table in tables())
    x, dy = block_in[0], cotangent[0]
    stage = stage_weights(
        w_query, key_weight, value_weight, w_out, w_router, gain_attn, gain_ffn
    )
    weights, rows, router, q, kv, h1t, unit_o, gate_full, up_pair, down_pair = first_call(
        stage, x, cosine, sine, w_gate, w_up, w_down
    )
    kv = kv.reshape(LENGTH, 512)
    o, ot, lse, wo, all_dy, up_full = attend_call(q, kv, unit_o, dy.reshape(2, 64, WIDTH), up_pair)
    middle, gates, tall, down_full = middle_call(o, wo, x, routes[0], rows, router, down_pair)
    out_rows, d_rows, g_gate, g_up, g_down = expert_call(tall, all_dy, gate_full, up_full, down_full)
    d_mid, d_o, small, g_out, g_down = token_grad_call(
        d_rows, middle, gates, dy, rows, router, wo, ot, g_down
    )
    dq, dkv, block_out, unit_o, g_gate = attend_back_call(
        q, kv, d_o, lse, out_rows, middle, g_out, g_gate, cosine, sine
    )
    grad_in, g_q, g_k, g_v, g_o, g_m, g_up = last_call(
        dkv, dq, h1t, weights, unit_o, small, x, d_mid, rows, g_up, cosine, sine
    )
    return (
        block_out[None],
        grad_in[None],
        g_m[:, EXPERTS],
        g_q,
        g_k,
        g_v,
        g_o,
        g_m[:, EXPERTS + 1],
        g_m[:, 0:EXPERTS],
        g_gate,
        g_up,
        g_down,
    )


def solution(mesh):
    tokens, owned, experts = P("seq", "ctx", None), P(("seq", "ctx"), None), P("ctx", "seq", None)
    vector = P(("seq", "ctx"))
    return jax.shard_map(
        body,
        mesh=mesh,
        in_specs=(
            tokens, tokens, tokens, vector, owned, owned, owned, owned, vector, owned,
            experts, experts, experts,
        ),
        out_specs=(
            tokens, tokens, vector, owned, owned, owned, owned, vector, owned,
            experts, experts, experts,
        ),
        check_vma=False,
    )
```

```python
import functools
import math

import jax
import jax.numpy as jnp
import numpy as np
from jax import lax
from jax.experimental import pallas as pl
from jax.experimental.pallas import tpu as pltpu
from jax.sharding import PartitionSpec as P

WIDTH = 1536
HEADS = 24
KV_HEADS = 8
HEAD = 64
TOPK = 8
ROWS = 128
LENGTH = 2048
EXPERTS = 32
FF = 512
CAP = 48
EPSILON = 1e-06

BF = jnp.bfloat16
F32 = jnp.float32
MESH = pl.DeviceIdType.MESH
VMEM_BYTES = 60 << 20

IN_Q, OUT_Q = 768, 384
IN_H, OUT_H = 2 * IN_Q, 2 * OUT_Q
STAGE = IN_Q + OUT_Q
COL_K, COL_V, COL_M, COL_END = 768, 1024, 1280, 1408
TALL = WIDTH + 128


def vm():
    return pl.BlockSpec(memory_space=pltpu.VMEM)


def hbm():
    return pl.BlockSpec(memory_space=pl.ANY)


def shape(dims, dtype=BF):
    return jax.ShapeDtypeStruct(dims, dtype)


def place():
    seq, ctx = lax.axis_index("seq"), lax.axis_index("ctx")
    return (ctx // 2 % 2 * 2 + seq // 4, ctx // 4, seq % 4, ctx % 2)


def device(x, y, z, core):
    return (x % 2 * 4 + z, (y * 2 + x // 2) * 2 + core)


def ring(at, dim, step):
    x, y, z, core = at
    if dim == 0:
        return ((x + step) % 4, y, z, core)
    if dim == 1:
        return (x, (y + step) % 4, z, core)
    return (x, y, (z + step) % 4, core)


def sibling(at):
    return (at[0], at[1], at[2], 1 - at[3])


def greet(peers):
    barrier = pltpu.get_barrier_semaphore()
    for peer in peers:
        pl.semaphore_signal(barrier, inc=1, device_id=device(*peer), device_id_type=MESH)
    pl.semaphore_wait(barrier, len(peers))


class Wires:
    def __init__(self, send, recv):
        self.send, self.recv, self.used, self.open = send, recv, 0, []

    def go(self, src, dst, peer):
        n = self.used
        self.used += 1
        copy = pltpu.make_async_remote_copy(
            src_ref=src,
            dst_ref=dst,
            send_sem=self.send.at[n],
            recv_sem=self.recv.at[n],
            device_id=device(*peer),
            device_id_type=MESH,
        )
        copy.start()
        self.open.append(copy)
        return copy

    def close(self):
        for copy in self.open:
            copy.wait_send()


def wire_sems(n):
    return [pltpu.SemaphoreType.DMA((n,)), pltpu.SemaphoreType.DMA((n,))]


def got(copies):
    for copy in copies:
        copy.wait_recv()


def dot(a, b):
    return jnp.dot(a, b, preferred_element_type=F32)


def dot_t(a, b):
    return lax.dot_general(a, b, (((1,), (1,)), ((), ())), preferred_element_type=F32)


def t_dot(a, b):
    return lax.dot_general(a, b, (((0,), (0,)), ((), ())), preferred_element_type=F32)


def iota(dims, axis):
    return lax.broadcasted_iota(jnp.int32, dims, axis)


def turn(block, cosine, sine):
    low = iota((block.shape[0], 128), 1) % HEAD < HEAD // 2
    parts = []
    for i in range(block.shape[1] // 128):
        unit = block[:, 128 * i : 128 * i + 128]
        other = jnp.where(low, pltpu.roll(unit, 96, 1), pltpu.roll(unit, 32, 1))
        parts.append(unit * cosine + other * sine)
    return jnp.concatenate(parts, 1)


def regroup():
    r, c = iota((48, 64), 0), iota((48, 64), 1)
    owner = c // 16 % 2 * 2 + c // 32
    hit = (r == owner * 12 + c % 16) & (c % 16 < 12)
    return hit.astype(F32).astype(BF)


def regroup_back():
    r, c = iota((64, 48), 0), iota((64, 48), 1)
    hit = (c == r // 16 * 12 + r % 16) & (r % 16 < 12)
    return hit.astype(F32).astype(BF)


ORDERS = ((0, 1, 2), (1, 2, 0), (2, 0, 1))


def block_of(quarter, part, fixed, at):
    x, y, z, _ = at
    whole = slice(None)
    columns = (
        pl.ds(pl.multiple_of(x // 2 * quarter, 128), quarter)
        if 0 in fixed
        else pl.ds(0, 2 * quarter)
    )
    return (
        x % 2 if 0 in fixed else whole,
        z if 2 in fixed else whole,
        y if 1 in fixed else whole,
        part,
        whole,
        columns,
    )


def spread(ref, quarter, wires, at):
    waits = [[], [], []]
    for phase in range(3):
        for part in range(3):
            got(waits[part])
            waits[part] = []
            fixed = ORDERS[part][phase:]
            spot = ref.at[block_of(quarter, part, fixed, at)]
            for step in (1, 2, 3):
                waits[part].append(wires.go(spot, spot, ring(at, fixed[0], step)))
        yield
    for part in range(3):
        got(waits[part])


def finish(*tasks):
    for task in tasks:
        for _ in task:
            pass


def partner(at):
    return (at[0] + 1 - 2 * (at[0] % 2), at[1], at[2], at[3])


def expert_spread(shard, full, wires, at, sem):
    x, _, z, _ = at
    left, right = ring(at, 2, 3), ring(at, 2, 1)
    spot = full.at[:, x % 2, z]
    local = pltpu.make_async_copy(shard, spot, sem)
    local.start()
    pair = wires.go(shard, spot, partner(at))
    yield
    local.wait()
    got([pair])
    spot = full.at[:, :, z]
    a = wires.go(spot, spot, right)
    b = wires.go(spot, spot, left)
    yield
    got([a])
    spot = full.at[0, :, (z + 3) % 4]
    a = wires.go(spot, spot, right)
    got([b])
    spot = full.at[1, :, (z + 1) % 4]
    b = wires.go(spot, spot, left)
    yield
    got([a, b])


def expert_sum_scratch(rows, columns):
    return [
        pltpu.VMEM((3, 2, 2, rows, columns), BF),
        pltpu.VMEM((2, 2, rows, columns), BF),
        pltpu.VMEM((2, 2, 2, rows, columns), BF),
        pltpu.VMEM((2, rows, columns), BF),
        pltpu.SemaphoreType.DMA((3,)),
    ]


def expert_sum(grads, result, scratch, wires, at):
    own, halves, pairs, last, lsem = scratch
    z, x_lo = at[2], at[0] % 2
    left, right = ring(at, 2, 3), ring(at, 2, 1)
    loads = [
        pltpu.make_async_copy(grads.at[:, :, (z + step) % 4], own.at[i], lsem.at[i])
        for i, step in enumerate((0, 1, 3))
    ]
    for copy in loads:
        copy.start()
    a = wires.go(grads.at[0, :, (z + 2) % 4], halves.at[0], right)
    b = wires.go(grads.at[1, :, (z + 2) % 4], halves.at[1], left)
    yield
    for copy in loads:
        copy.wait()
    got([a])
    for i in range(2):
        own[1, 0, i] = (own[1, 0, i].astype(F32) + halves[0, i].astype(F32)).astype(BF)
    a = wires.go(own.at[1], pairs.at[0], right)
    got([b])
    for i in range(2):
        own[2, 1, i] = (own[2, 1, i].astype(F32) + halves[1, i].astype(F32)).astype(BF)
    b = wires.go(own.at[2], pairs.at[1], left)
    yield
    got([a, b])
    for e in range(2):
        for i in range(2):
            own[0, e, i] = (
                own[0, e, i].astype(F32)
                + pairs[0, e, i].astype(F32)
                + pairs[1, e, i].astype(F32)
            ).astype(BF)
    a = wires.go(own.at[0, :, 1 - x_lo], last, partner(at))
    yield
    got([a])
    for e in range(2):
        result[e] = own[0, e, x_lo].astype(F32) + last[e].astype(F32)


def ctx_peers(at):
    return [ring(at, 1, 1), ring(at, 1, 2), ring(at, 1, 3), ring(at, 0, 2)]


def all_peers(at):
    return [ring(at, d, s) for d in range(3) for s in (1, 2, 3)]


def share(spot, wires, at, inner=True):
    x, y, _, _ = at
    xh = x // 2
    near, far, up, down = sibling(at), ring(at, 0, 2), ring(at, 1, 1), ring(at, 1, 3)
    above, below, across = (y + 1) % 4, (y + 3) % 4, (y + 2) % 4
    kept = []

    def send(where, peer):
        return wires.go(spot(*where), spot(*where), peer)

    def pass_on(*where):
        if inner:
            kept.append(send(where, near))

    a, b = send((y, xh), up), send((y, xh), down)
    c = send((y, xh), far)
    pass_on(y, xh)
    yield
    got([a])
    a1 = send((below, xh, 0), up)
    got([b])
    b1 = send((above, xh, 1), down)
    pass_on(below, xh)
    pass_on(above, xh)
    got([c])
    a2, b2 = send((y, 1 - xh), up), send((y, 1 - xh), down)
    pass_on(y, 1 - xh)
    yield
    got([a1, b1])
    pass_on(across, xh)
    got([a2])
    a3 = send((below, 1 - xh, 0), up)
    got([b2])
    b3 = send((above, 1 - xh, 1), down)
    pass_on(below, 1 - xh)
    pass_on(above, 1 - xh)
    yield
    got([a3, b3])
    pass_on(across, 1 - xh)
    yield
    got(kept)


def share_rows(ref, wires, at):
    core = at[3]
    return share(lambda y, xh, *half: ref.at[(y, xh, core, *half)], wires, at)


def ctx_and_sibling(at):
    return ctx_peers(at) + [sibling(at)]


def sum_scratch(rows, columns):
    return [
        pltpu.VMEM((4, rows, columns), BF),
        pltpu.VMEM((3, 2, rows, columns), BF),
        pltpu.VMEM((4, rows, columns), BF),
        pltpu.VMEM((2, rows, columns), BF),
        pltpu.VMEM((3, rows, columns), BF),
        pltpu.VMEM((1, rows, columns), BF),
    ]


def sum_chips(source, scratch, wires, at):
    e0, e1, t0, t1, f0, f1 = scratch
    x, y, _, _ = at
    xh = x // 2
    far = ring(at, 0, 2)
    a = [wires.go(source.at[0, :, 1 - xh], e0, far)]
    b = [
        wires.go(source.at[1, (y + s) % 4], e1.at[s - 1], ring(at, 1, s)) for s in (1, 2, 3)
    ]
    yield None
    got(a)
    for i in range(4):
        t0[i] = (source[0, i, xh].astype(F32) + e0[i].astype(F32)).astype(BF)
    a = [wires.go(t0.at[(y + s) % 4], f0.at[s - 1], ring(at, 1, s)) for s in (1, 2, 3)]
    got(b)
    for i in range(2):
        total = source[1, y, i].astype(F32)
        for s in range(3):
            total += e1[s, i].astype(F32)
        t1[i] = total.astype(BF)
    b = [wires.go(t1.at[1 - xh], f1.at[0], far)]
    yield None
    got(a)
    first = t0[y].astype(F32)
    for s in range(3):
        first += f0[s].astype(F32)
    got(b)
    yield first, t1[xh].astype(F32) + f1[0].astype(F32)


def sum_rows_scratch(columns):
    return [
        pltpu.VMEM((2, 4, 2, 64, columns), BF),
        pltpu.VMEM((2, 4, 2, 64, columns), BF),
        *sum_scratch(64, columns),
    ]


def sum_rows(rows, scratch, wires, at):
    landed, own, rest = scratch[0], scratch[1], scratch[2:]
    core = at[3]
    copies = [
        wires.go(rows.at[:, :, 1 - core, part], landed.at[part], sibling(at)) for part in range(2)
    ]
    yield None
    for part in range(2):
        got([copies[part]])
        for i in range(4):
            for h in range(2):
                own[part, i, h] = (
                    rows[i, h, core, part].astype(F32) + landed[part, i, h].astype(F32)
                ).astype(BF)
    for result in sum_chips(own, rest, wires, at):
        yield result


def final(steps):
    result = None
    for result in steps:
        pass
    return result


def gather_sums(ref, quarter, landings, wires, at):
    orders = tuple(order[::-1] for order in ORDERS)
    waits = [[], [], []]

    def send(part, phase):
        fixed = orders[part][: phase + 1]
        dim = fixed[-1]
        for step in (1, 2, 3):
            peer = ring(at, dim, step)
            spot = ref.at[block_of(quarter, part, fixed, peer)]
            waits[part].append(wires.go(spot, landings[part][phase].at[step - 1], peer))

    def add(part, phase):
        got(waits[part])
        waits[part] = []
        fixed = orders[part][: phase + 1]
        index = block_of(quarter, part, fixed, at)
        total = ref[index].astype(F32)
        for step in range(3):
            total += landings[part][phase][step].astype(F32)
        ref[index] = total.astype(BF)

    for part in range(3):
        send(part, 0)
    yield
    for phase in range(3):
        for part in range(3):
            add(part, phase)
            if phase < 2:
                send(part, phase + 1)
        yield


def landing_shapes(quarter):
    found = []
    for order in ORDERS:
        for phase in range(3):
            fixed = order[::-1][: phase + 1]
            dims = [size for size, dim in ((2, 0), (4, 2), (4, 1)) if dim not in fixed]
            found.append(pltpu.VMEM((3, *dims, 16, quarter if 0 in fixed else 2 * quarter), BF))
    return found


def normed(values):
    inverse = lax.rsqrt(jnp.mean(values * values, -1, keepdims=True) + EPSILON)
    return values * inverse, inverse


def attend(q, kv, o, ot, lse, scratch, chip, beside):
    scores, vt, qt, qz, out_t = scratch
    qt[...] = jnp.transpose(q[...].astype(F32) * 0.125).astype(BF)
    for kb in range(8):
        block = kv[kb // 2, kb % 2, :, :, 256:512].reshape(256, 256)
        vt[kb] = jnp.transpose(block.astype(F32)).astype(BF)
    allowed = iota((256, 768), 0) <= iota((256, 768), 1) % 256
    for j in range(4):
        u, half = j // 2, j % 2
        qz[...] = jnp.zeros_like(qz)
        for g in range(3):
            h = 3 * j + g
            qz[64 * half : 64 * half + 64, 256 * g : 256 * g + 256] = qt[64 * h : 64 * h + 64]

        def score(kb):
            rows = pl.ds(pl.multiple_of(kb * 256, 256), 256)
            keys = kv[kb // 2, kb % 2, :, :, 128 * u : 128 * u + 128].reshape(256, 128)
            return rows, dot(keys, qz[...])

        def top(kb, most):
            rows, s = score(kb)
            scores[rows] = s
            return jnp.maximum(most, jnp.max(s.reshape(32, 8, 768), 0))

        most = lax.fori_loop(0, chip, top, jnp.full((8, 768), -1e30, F32))
        rows, s = score(chip)
        s = jnp.where(allowed, s, -1e30)
        scores[rows] = s
        most = jnp.maximum(most, jnp.max(s.reshape(32, 8, 768), 0))
        most = jnp.max(most, 0, keepdims=True)

        def raise_(kb, total):
            rows = pl.ds(pl.multiple_of(kb * 256, 256), 256)
            e = jnp.exp(scores[rows] - most)
            scores[rows] = e
            return total + jnp.sum(e.reshape(32, 8, 768), 0)

        beside[2 * j]()
        total = lax.fori_loop(0, chip + 1, raise_, jnp.zeros((8, 768), F32))
        total = jnp.sum(total, 0, keepdims=True)
        lse[j] = jnp.broadcast_to(most + jnp.log(total), (8, 768))
        inverse = 1.0 / total

        def mix(kb, acc):
            rows = pl.ds(pl.multiple_of(kb * 256, 256), 256)
            p = (scores[rows] * inverse).astype(BF)
            return acc + dot(vt[kb, 64 * j : 64 * j + 64], p)

        acc = lax.fori_loop(0, chip + 1, mix, jnp.zeros((64, 768), F32))
        for g in range(3):
            h = 3 * j + g
            out_t[64 * h : 64 * h + 64] = acc[:, 256 * g : 256 * g + 256]
        beside[2 * j + 1]()
    ot[...] = out_t[...].astype(BF)
    out = jnp.transpose(out_t[...]).astype(BF)
    o[0], o[1] = out[0:128], out[128:256]


def forward_kernel(
    stage, x, routes, cosine, sine, dy, w_gate, w_up, w_down,
    rows, router, q, h1t, ot, lse, middle, gates,
    weights_out, wo_out, kv_out, tall, all_dy, gate_full, up_full, down_full,
    weights, columns, wo, kv, both, slots, cos_v, sin_v, o, tall_own, product, arrived,
    scores, vt, qt, qz, out_t, ssem, rsem, lsem,
):
    at = place()
    xx, y, z, core = at
    xh, chip = xx // 2, y * 2 + xx // 2
    near = sibling(at)
    diagonal = sibling(ring(at, 0, 2))
    greet(all_peers(at) + [near, diagonal])
    wires = Wires(ssem, rsem)

    def local(n, src, dst):
        copy = pltpu.make_async_copy(src, dst, lsem.at[n])
        copy.start()
        return copy

    angle = pl.ds(pl.multiple_of(chip * 256, 256), 256)
    angles = [local(0, cosine.at[angle], cos_v), local(1, sine.at[angle], sin_v)]
    dy_in = local(2, dy, all_dy.at[y, xh, core])
    mine = core * 2 + xh
    first = [
        wires.go(stage.at[peer[3] * 2 + peer[0] // 2], slots.at[mine], peer)
        for peer in (near, ring(at, 0, 2), diagonal)
    ]
    tokens = wires.go(x, both.at[core], near)
    slots[mine] = stage[mine]
    both[core] = x[...]
    got(first)
    unit = dot(regroup(), slots[...].reshape(64, STAGE)).astype(BF)
    in_lanes = pl.ds(pl.multiple_of(xh * IN_Q, 128), IN_Q)
    out_lanes = pl.ds(pl.multiple_of(xh * OUT_Q, 128), OUT_Q)
    for part in range(3):
        weights[xx % 2, z, y, part, :, in_lanes] = unit[16 * part : 16 * part + 16, 0:IN_Q]
        columns[xx % 2, z, y, part, :, out_lanes] = unit[16 * part : 16 * part + 16, IN_Q:STAGE]
    in_task = spread(weights, IN_Q, wires, at)
    out_task = spread(columns, OUT_Q, wires, at)
    dy_task = share_rows(all_dy, wires, at)
    gate_task = expert_spread(w_gate, gate_full, wires, at, lsem.at[3])
    up_task = expert_spread(w_up, up_full, wires, at, lsem.at[4])
    down_task = expert_spread(w_down, down_full, wires, at, lsem.at[5])
    next(in_task)
    next(in_task)
    next(gate_task)
    next(in_task)
    finish(in_task)
    weights_kept = local(6, weights, weights_out)
    next(gate_task)
    next(up_task)
    dy_in.wait()
    next(dy_task)

    small = weights[:, :, :, :, :, COL_M:COL_END].reshape(WIDTH, 128)
    router[...] = small
    turned = jnp.transpose(small.astype(F32))
    rows[...] = turned[32:40]
    got([tokens])
    values = both[...].reshape(256, WIDTH).astype(F32)
    hidden = (normed(values)[0] * turned[32:33]).astype(BF)
    made = dot(hidden, weights[:, :, :, :, :, 0:COL_M].reshape(WIDTH, COL_M))
    for copy in angles:
        copy.wait()
    cos, sin = cos_v[...], sin_v[...]
    key = turn(made[:, COL_K:COL_V], cos, sin).astype(BF)
    value = made[:, COL_V:COL_M].astype(BF)
    for part in range(2):
        kv[y, xh, part, :, 0:256] = key[128 * part : 128 * part + 128]
        kv[y, xh, part, :, 256:512] = value[128 * part : 128 * part + 128]
    own = [kv.at[y, xh, 0], kv.at[y, xh, 1]]
    a = [wires.go(own[0], own[0], ring(at, 1, s)) for s in (1, 2, 3)]
    b = [wires.go(own[1], own[1], ring(at, 0, 2))]
    q[...] = turn(made[:, 0:COL_K], cos, sin).astype(BF)
    got(b)
    pair = kv.at[y, :, 1]
    b = [wires.go(pair, pair, ring(at, 1, s)) for s in (1, 2, 3)]
    got(a)
    column = kv.at[:, xh, 0]
    a = [wires.go(column, column, ring(at, 0, 2))]
    next(out_task)
    h1t[...] = jnp.transpose(hidden.astype(F32)).astype(BF)
    next(up_task)
    next(down_task)
    next(out_task)
    got(a)
    got(b)
    kv_kept = local(7, kv, kv_out)
    next(gate_task)
    next(dy_task)

    half = pl.ds(pl.multiple_of(core * 768, 128), 768)
    swap = []

    def swap_out():
        finish(out_task)
        swap.append(wires.go(columns.at[1 - core], wo.at[:, :, :, :, half], near))
        for i in range(4):
            wo[i, :, :, :, half] = columns[core, i]

    beside = [
        lambda: next(out_task),
        lambda: next(down_task),
        lambda: next(dy_task),
        lambda: next(up_task),
        swap_out,
        lambda: next(dy_task),
        lambda: None,
        lambda: None,
    ]
    attend(q, kv, o, ot, lse, (scores, vt, qt, qz, out_t), chip, beside)
    got(swap)
    wo_kept = local(8, wo, wo_out)

    full = wo[...].reshape(768, WIDTH)
    product[0] = dot(o[1 - core], full)
    swap = wires.go(product.at[0], arrived, near)
    product[1] = dot(o[core], full)
    lane = iota((ROWS, 128), 1)
    named = routes[:, 0:1] == lane
    for i in range(1, TOPK):
        named = named | (routes[:, i : i + 1] == lane)
    got([swap])
    mid = x[...].astype(F32) + product[1] + arrived[...]
    middle[...] = mid
    hidden = (normed(mid)[0] * rows[1:2]).astype(BF)
    logits = jnp.where(named, dot(hidden, router[...]), -jnp.inf)
    raised = jnp.exp(logits - jnp.max(logits, -1, keepdims=True))
    gate = raised / jnp.sum(raised, -1, keepdims=True)
    gates[...] = gate
    high = gate.astype(BF).astype(F32)
    two = high + pltpu.roll(gate - high, EXPERTS, 1)
    for part in range(2):
        cut = slice(64 * part, 64 * part + 64)
        tall_own[part, :, 0:WIDTH] = hidden[cut]
        tall_own[part, :, WIDTH:TALL] = two[cut].astype(BF)
    tall_in = local(9, tall_own, tall.at[y, xh, core])
    tall_task = share_rows(tall, wires, at)
    tall_in.wait()
    next(tall_task)
    next(down_task)
    next(tall_task)
    next(tall_task)
    finish(dy_task, gate_task, up_task)
    finish(tall_task, down_task)
    for copy in (weights_kept, kv_kept, wo_kept):
        copy.wait()
    wires.close()


def forward_call(stage, x, routes, cosine, sine, dy, w_gate, w_up, w_down):
    return pl.pallas_call(
        forward_kernel,
        out_shape=[
            shape((8, WIDTH), F32),
            shape((WIDTH, 128)),
            shape((256, 768)),
            shape((WIDTH, 256)),
            shape((768, 256)),
            shape((4, 8, 768), F32),
            shape((ROWS, WIDTH), F32),
            shape((ROWS, 128), F32),
            shape((2, 4, 4, 3, 16, IN_H)),
            shape((4, 4, 3, 16, WIDTH)),
            shape((4, 2, 2, 128, 512)),
            shape((4, 2, 2, 2, 64, TALL)),
            shape((4, 2, 2, 2, 64, WIDTH)),
            shape((2, 2, 4, 192, FF)),
            shape((2, 2, 4, 192, FF)),
            shape((2, 2, 4, 64, WIDTH)),
        ],
        in_specs=[vm()] * 3 + [hbm()] * 2 + [vm()] * 4,
        out_specs=[vm()] * 8 + [hbm()] * 8,
        scratch_shapes=[
            pltpu.VMEM((2, 4, 4, 3, 16, IN_H), BF),
            pltpu.VMEM((2, 4, 4, 3, 16, OUT_H), BF),
            pltpu.VMEM((4, 4, 3, 16, WIDTH), BF),
            pltpu.VMEM((4, 2, 2, 128, 512), BF),
            pltpu.VMEM((2, 128, WIDTH), BF),
            pltpu.VMEM((4, 16, STAGE), BF),
            pltpu.VMEM((256, 128), F32),
            pltpu.VMEM((256, 128), F32),
            pltpu.VMEM((2, 128, 768), BF),
            pltpu.VMEM((2, 64, TALL), BF),
            pltpu.VMEM((2, ROWS, WIDTH), F32),
            pltpu.VMEM((ROWS, WIDTH), F32),
            pltpu.VMEM((LENGTH, 768), F32),
            pltpu.VMEM((8, 256, 256), BF),
            pltpu.VMEM((768, 256), BF),
            pltpu.VMEM((128, 768), BF),
            pltpu.VMEM((768, 256), F32),
            *wire_sems(144),
            pltpu.SemaphoreType.DMA((10,)),
        ],
        compiler_params=pltpu.CompilerParams(
            collective_id=1, has_side_effects=True, vmem_limit_bytes=VMEM_BYTES
        ),
        name="forward",
    )(stage, x, routes, cosine, sine, dy, w_gate, w_up, w_down)


def expert_kernel(
    tall, dy, w_gate, w_up, w_down,
    out_rows, d_rows, g_gate, g_up, g_down,
    big, wide, a_rows, y_rows, r_rows, back, wg, wu, wd, gg, gu, gd, m_s, dg_s, du_s, slot_t, sem,
):
    ctx = lax.axis_index("ctx")
    loads = [
        pltpu.make_async_copy(src, dst, sem.at[i])
        for i, (src, dst) in enumerate(
            ((tall, big), (dy, wide), (w_gate, wg), (w_up, wu), (w_down, wd))
        )
    ]
    for copy in loads:
        copy.start()
    lane = iota((128, 128), 1)
    earlier = (iota((128, 128), 1) < iota((128, 128), 0)).astype(F32).astype(BF)
    slots = iota((CAP, 128), 0).astype(F32)
    loads[0].wait()
    loads[1].wait()

    def collect(b, _):
        rows = pl.ds(pl.multiple_of(b * 128, 128), 128)
        packed = pl.ds(pl.multiple_of(b * CAP, CAP), CAP)
        both = big[rows, WIDTH:TALL].astype(F32)
        gate = both + pltpu.roll(both, 128 - EXPERTS, 1)
        hot = (gate > 0.0) & (lane < EXPERTS)
        rank = dot(earlier, hot.astype(F32).astype(BF))
        slot = jnp.where(hot, rank, -1.0)
        slot_t[...] = jnp.transpose(slot)
        picks = [
            (slot_t[pl.ds(2 * ctx + i, 1), :] == slots).astype(F32).astype(BF) for i in range(2)
        ]
        pick = jnp.concatenate(picks, 0)
        found = dot(pick, big[rows, :]).astype(BF)
        grads = dot(pick, wide[rows, :]).astype(BF)
        for i in range(2):
            a_rows[i, packed] = found[CAP * i : CAP * i + CAP]
            y_rows[i, packed] = grads[CAP * i : CAP * i + CAP]
        column = [
            jnp.sum(jnp.where(lane == 2 * ctx + i, slot, 0.0), 1, keepdims=True) for i in range(2)
        ]
        spot = lane.astype(F32)
        put = jnp.where(lane < CAP, column[0], column[1] + CAP) == spot
        back[b] = put.astype(F32).astype(BF)
        return 0

    lax.fori_loop(0, 16, collect, 0)
    for copy in loads[2:]:
        copy.wait()
    stores = []
    for e in range(2):
        number = 2 * ctx + e

        def forward(c, _):
            rows = pl.ds(pl.multiple_of(c * 384, 384), 384)
            a = a_rows[e, rows, 0:WIDTH]
            ag, au = dot(a, wg[e]), dot(a, wu[e])
            sg = jax.nn.sigmoid(ag)
            act = ag * sg
            m = (act * au).astype(BF)
            r = dot(m, wd[e]).astype(BF).astype(F32)
            lanes = iota((384, 128), 1)
            hits = (lanes == number) | (lanes == number + EXPERTS)
            gate = jnp.sum(
                jnp.where(hits, a_rows[e, rows, WIDTH:TALL].astype(F32), 0.0), 1, keepdims=True
            )
            y = y_rows[e, rows].astype(F32)
            d_gate = jnp.sum(y * r, 1, keepdims=True)
            r_rows[e, rows] = (gate * r).astype(BF)
            gr = (gate * y).astype(BF)
            y_rows[e, rows] = gr
            dm = dot_t(gr, wd[e])
            m_s[rows] = m
            dg_s[rows] = (dm * au * (sg * (1.0 + ag * (1.0 - sg)))).astype(BF)
            du_s[rows] = (dm * act).astype(BF)
            high = d_gate.astype(BF).astype(F32)
            d_both = jnp.where(
                lanes == number, high, jnp.where(lanes == number + EXPERTS, d_gate - high, 0.0)
            )
            a_rows[e, rows, WIDTH:TALL] = d_both.astype(BF)
            return 0

        lax.fori_loop(0, 2, forward, 0)
        gd[e] = t_dot(m_s[...], y_rows[e]).astype(BF)
        gg[e] = t_dot(a_rows[e, :, 0:WIDTH], dg_s[...]).astype(BF)
        gu[e] = t_dot(a_rows[e, :, 0:WIDTH], du_s[...]).astype(BF)
        for i, (src, dst) in enumerate(((gd, g_down), (gg, g_gate), (gu, g_up))):
            copy = pltpu.make_async_copy(src.at[e], dst.at[e], sem.at[5 + 3 * e + i])
            copy.start()
            stores.append(copy)

        def to_tokens(c, _):
            rows = pl.ds(pl.multiple_of(c * 384, 384), 384)
            back_rows = dot_t(dg_s[rows], wg[e]) + dot_t(du_s[rows], wu[e])
            a_rows[e, rows, 0:WIDTH] = back_rows.astype(BF)
            return 0

        lax.fori_loop(0, 2, to_tokens, 0)

    def hand_back(b, _):
        rows = pl.ds(pl.multiple_of(b * 128, 128), 128)
        packed = pl.ds(pl.multiple_of(b * CAP, CAP), CAP)
        put = back[b][:, 0 : 2 * CAP]
        big[rows, :] = dot(put, jnp.concatenate([a_rows[0, packed], a_rows[1, packed]], 0)).astype(BF)
        wide[rows, :] = dot(put, jnp.concatenate([r_rows[0, packed], r_rows[1, packed]], 0)).astype(BF)
        return 0

    lax.fori_loop(0, 16, hand_back, 0)
    for i, (src, dst) in enumerate(((big, d_rows), (wide, out_rows))):
        copy = pltpu.make_async_copy(src, dst, sem.at[i])
        copy.start()
        stores.append(copy)
    for copy in stores:
        copy.wait()


def expert_call(tall, dy, w_gate, w_up, w_down):
    slots = 16 * CAP
    return pl.pallas_call(
        expert_kernel,
        out_shape=[
            shape((LENGTH, WIDTH)),
            shape((LENGTH, TALL)),
            shape((2, WIDTH, FF)),
            shape((2, WIDTH, FF)),
            shape((2, FF, WIDTH)),
        ],
        in_specs=[hbm()] * 5,
        out_specs=[hbm()] * 5,
        scratch_shapes=[
            pltpu.VMEM((LENGTH, TALL), BF),
            pltpu.VMEM((LENGTH, WIDTH), BF),
            pltpu.VMEM((2, slots, TALL), BF),
            pltpu.VMEM((2, slots, WIDTH), BF),
            pltpu.VMEM((2, slots, WIDTH), BF),
            pltpu.VMEM((16, 128, 128), BF),
            pltpu.VMEM((2, WIDTH, FF), BF),
            pltpu.VMEM((2, WIDTH, FF), BF),
            pltpu.VMEM((2, FF, WIDTH), BF),
            pltpu.VMEM((2, WIDTH, FF), BF),
            pltpu.VMEM((2, WIDTH, FF), BF),
            pltpu.VMEM((2, FF, WIDTH), BF),
            pltpu.VMEM((slots, FF), BF),
            pltpu.VMEM((slots, FF), BF),
            pltpu.VMEM((slots, FF), BF),
            pltpu.VMEM((128, 128), F32),
            pltpu.SemaphoreType.DMA((11,)),
        ],
        compiler_params=pltpu.CompilerParams(vmem_limit_bytes=VMEM_BYTES),
        name="experts",
    )(
        tall.reshape(LENGTH, TALL), dy.reshape(LENGTH, WIDTH), w_gate.reshape(2, WIDTH, FF),
        w_up.reshape(2, WIDTH, FF), w_down.reshape(2, FF, WIDTH),
    )


def split_dot(left, right, form):
    high = left.astype(BF)
    low = (left - high.astype(F32)).astype(BF)
    return form(high, right) + form(low, right)


def norm_back(grad, gain, n, inverse):
    scaled = grad * gain
    return inverse * (scaled - n * jnp.mean(scaled * n, -1, keepdims=True))


def token_grad_kernel(
    d_rows, middle, gates, dy, rows, router, wo, ot, g_down,
    d_mid, d_o, small, g_out, down_sum,
    low, product, *rest,
):
    scratch, expert_scratch, (ssem, rsem) = rest[:8], rest[8:13], rest[13:]
    at = place()
    core = at[3]
    near = sibling(at)
    greet(ctx_and_sibling(at) + [ring(at, 2, 1), ring(at, 2, 3), partner(at)])
    wires = Wires(ssem, rsem)
    steps = sum_rows(d_rows, scratch, wires, at)
    next(steps)
    down_task = expert_sum(g_down, down_sum, expert_scratch, wires, at)
    next(down_task)
    next(steps)
    next(down_task)
    n, inverse = normed(middle[...])
    hidden = (n * rows[1:2]).astype(BF)
    parts = final(steps)
    total = jnp.concatenate(parts, 0)
    d_hidden = total[:, 0:WIDTH]
    both = total[:, WIDTH:TALL]
    gate = gates[...]
    lane = iota((ROWS, 128), 1)
    d_gate = jnp.where(lane < EXPERTS, both + pltpu.roll(both, 128 - EXPERTS, 1), 0.0)
    centre = jnp.sum(gate * d_gate, -1, keepdims=True)
    d_logits = gate * (d_gate - centre)
    d_hidden += split_dot(d_logits, router[...], dot_t)
    d_middle = norm_back(d_hidden, rows[1:2], n, inverse) + dy[...].astype(F32)
    d_low = d_middle.astype(BF)
    low[core] = d_low
    swap = wires.go(low.at[core], low.at[core], near)
    d_mid[...] = d_middle
    grads = split_dot(jnp.transpose(d_logits), hidden, dot)
    line = jnp.sum(d_hidden * n, 0, keepdims=True)
    small[...] = grads + jnp.where(iota((128, WIDTH), 0) == EXPERTS + 1, line, 0.0)
    next(down_task)
    got([swap])
    chip_rows = low[...].reshape(256, WIDTH)
    d_o[...] = dot_t(chip_rows, wo[...].reshape(768, WIDTH)).astype(BF)
    product[...] = dot(ot[...], chip_rows).astype(BF).reshape(4, 4, 3, 16, WIDTH)
    lanes = pl.ds(pl.multiple_of((1 - core) * 768, 128), 768)
    mine = pl.ds(pl.multiple_of(core * 768, 128), 768)
    swap = wires.go(product.at[:, :, :, :, lanes], g_out.at[core], near)
    for i in range(4):
        g_out[core, i] = product[i, :, :, :, mine]
    finish(down_task)
    got([swap])
    wires.close()


def token_grad_call(d_rows, middle, gates, dy, rows, router, wo, ot, g_down):
    return pl.pallas_call(
        token_grad_kernel,
        out_shape=[
            shape((ROWS, WIDTH), F32),
            shape((256, 768)),
            shape((128, WIDTH), F32),
            shape((2, 4, 4, 3, 16, 768)),
            shape((2, 64, WIDTH), F32),
        ],
        in_specs=[vm()] * 8 + [hbm()],
        out_specs=[vm()] * 5,
        scratch_shapes=[
            pltpu.VMEM((2, ROWS, WIDTH), BF),
            pltpu.VMEM((4, 4, 3, 16, WIDTH), BF),
            *sum_rows_scratch(TALL),
            *expert_sum_scratch(64, WIDTH),
            *wire_sems(24),
        ],
        compiler_params=pltpu.CompilerParams(
            collective_id=4, has_side_effects=True, vmem_limit_bytes=VMEM_BYTES
        ),
        name="token_grad",
    )(
        d_rows.reshape(4, 2, 2, 2, 64, TALL), middle, gates, dy, rows, router, wo, ot,
        g_down.reshape(2, 2, 4, 64, WIDTH),
    )


def attend_back_kernel(
    q, kv, d_o, lse, out_rows, middle, g_out, g_gate, cosine, sine,
    dq, dkv, block_out, unit_o, gate_sum,
    probs, grads, kt, qt, dot_, qz, oz, acc, dqt, cos_v, sin_v, columns, *rest,
):
    row_scratch, landings = rest[:8], [rest[8 + 3 * i : 11 + 3 * i] for i in range(3)]
    expert_scratch = rest[17:22]
    ssem, rsem, lsem = rest[22:]
    at = place()
    xx, y, z, _ = at
    chip = y * 2 + xx // 2
    greet(all_peers(at) + [sibling(at)])
    wires = Wires(ssem, rsem)
    columns_in = pltpu.make_async_copy(g_out, columns, lsem.at[2])
    columns_in.start()
    tables = [
        pltpu.make_async_copy(src.at[pl.ds(pl.multiple_of(chip * 256, 256), 256)], dst, lsem.at[i])
        for i, (src, dst) in enumerate(((cosine, cos_v), (sine, sin_v)))
    ]
    for copy in tables:
        copy.start()
    row_task = sum_rows(out_rows, row_scratch, wires, at)
    gate_task = expert_sum(g_gate, gate_sum, expert_scratch, wires, at)
    out_task = gather_sums(columns, OUT_Q, landings, wires, at)
    next(row_task)
    next(gate_task)

    def start_out():
        columns_in.wait()
        next(out_task)

    beside = [
        lambda: next(row_task),
        lambda: next(gate_task),
        start_out,
        lambda: next(gate_task),
        lambda: next(row_task),
        lambda: next(out_task),
        lambda: finish(gate_task),
        lambda: next(out_task),
    ]
    qt[...] = jnp.transpose(q[...].astype(F32) * 0.125).astype(BF)
    dot_[...] = jnp.transpose(d_o[...].astype(F32)).astype(BF)
    for kb in range(8):
        kt[kb] = jnp.transpose(kv[256 * kb : 256 * kb + 256, 0:256].astype(F32)).astype(BF)
    acc[...] = jnp.zeros_like(acc)
    allowed = iota((256, 768), 0) <= iota((256, 768), 1) % 256
    for j in range(4):
        u, half = j // 2, j % 2
        qz[...] = jnp.zeros_like(qz)
        oz[...] = jnp.zeros_like(oz)
        for g in range(3):
            h = 3 * j + g
            qz[64 * half : 64 * half + 64, 256 * g : 256 * g + 256] = qt[64 * h : 64 * h + 64]
            oz[64 * half : 64 * half + 64, 256 * g : 256 * g + 256] = dot_[64 * h : 64 * h + 64]
        level = lse[j, 0:1]

        def share(kb, centre, masked):
            rows = pl.ds(pl.multiple_of(kb * 256, 256), 256)
            p = jnp.exp(dot(kv[rows, 128 * u : 128 * u + 128], qz[...]) - level)
            if masked:
                p = jnp.where(allowed, p, 0.0)
            probs[rows] = p
            dp = dot(kv[rows, 256 + 128 * u : 384 + 128 * u], oz[...])
            grads[rows] = dp
            acc[rows, 256 + 128 * u : 384 + 128 * u] += dot_t(p.astype(BF), oz[...])
            return centre + jnp.sum((p * dp).reshape(32, 8, 768), 0)

        centre = lax.fori_loop(
            0, chip, functools.partial(share, masked=False), jnp.zeros((8, 768), F32)
        )
        centre = share(chip, centre, True)
        centre = jnp.sum(centre, 0, keepdims=True)
        beside[2 * j]()

        def back(kb, total):
            rows = pl.ds(pl.multiple_of(kb * 256, 256), 256)
            ds = (probs[rows] * (grads[rows] - centre)).astype(BF)
            acc[rows, 128 * u : 128 * u + 128] += dot_t(ds, qz[...])
            return total + dot(kt[kb, 64 * j : 64 * j + 64], ds)

        total = lax.fori_loop(0, chip + 1, back, jnp.zeros((64, 768), F32))
        for g in range(3):
            h = 3 * j + g
            dqt[64 * h : 64 * h + 64] = total[:, 256 * g : 256 * g + 256] * 0.125
        beside[2 * j + 1]()
    for kb in range(8):
        for part in range(2):
            at_row = 256 * kb + 128 * part
            dkv[part, kb] = acc[at_row : at_row + 128].astype(BF)
    for copy in tables:
        copy.wait()
    dq[...] = turn(jnp.transpose(dqt[...]), cos_v[...], -sin_v[...]).astype(BF)
    parts = final(row_task)
    for part in range(2):
        cut = slice(64 * part, 64 * part + 64)
        block_out[cut] = (middle[cut] + parts[part]).astype(BF)
    finish(out_task)
    lanes = pl.ds(pl.multiple_of(xx // 2 * OUT_Q, 128), OUT_Q)
    for part in range(3):
        unit_o[part] = columns[xx % 2, z, y, part, :, lanes]
    wires.close()


def attend_back_call(q, kv, d_o, lse, out_rows, middle, g_out, g_gate, cosine, sine):
    return pl.pallas_call(
        attend_back_kernel,
        out_shape=[
            shape((256, 768)),
            shape((2, 8, 128, 512)),
            shape((ROWS, WIDTH)),
            shape((3, 16, OUT_Q)),
            shape((2, 192, FF), F32),
        ],
        in_specs=[vm()] * 6 + [hbm()] * 4,
        out_specs=[vm()] * 5,
        scratch_shapes=[
            pltpu.VMEM((LENGTH, 768), F32),
            pltpu.VMEM((LENGTH, 768), F32),
            pltpu.VMEM((8, 256, 256), BF),
            pltpu.VMEM((768, 256), BF),
            pltpu.VMEM((768, 256), BF),
            pltpu.VMEM((128, 768), BF),
            pltpu.VMEM((128, 768), BF),
            pltpu.VMEM((LENGTH, 512), F32),
            pltpu.VMEM((768, 256), F32),
            pltpu.VMEM((256, 128), F32),
            pltpu.VMEM((256, 128), F32),
            pltpu.VMEM((2, 4, 4, 3, 16, OUT_H), BF),
            *sum_rows_scratch(WIDTH),
            *landing_shapes(OUT_Q),
            *expert_sum_scratch(192, FF),
            *wire_sems(56),
            pltpu.SemaphoreType.DMA((3,)),
        ],
        compiler_params=pltpu.CompilerParams(
            collective_id=5, has_side_effects=True, vmem_limit_bytes=VMEM_BYTES
        ),
        name="attend_back",
    )(
        q, kv, d_o, lse, out_rows.reshape(4, 2, 2, 2, 64, WIDTH), middle, g_out,
        g_gate.reshape(2, 2, 4, 192, FF), cosine, sine,
    )


def last_kernel(
    dkv, dq, h1t, weights, unit_o, small, x, d_mid, rows, g_up, cosine, sine,
    grad_in, g_q, g_k, g_v, g_o, g_m, up_sum,
    whole, product, arrived, slots, taken, cos_v, sin_v, *rest,
):
    landings = [rest[3 * i : 3 * i + 3] for i in range(3)]
    chips, expert_scratch = rest[9:15], rest[15:20]
    ssem, rsem, lsem = rest[20:]
    at = place()
    xx, y, z, core = at
    xh, chip = xx // 2, y * 2 + xx // 2
    near = sibling(at)
    diagonal = sibling(ring(at, 0, 2))
    greet(all_peers(at) + [near, diagonal])
    wires = Wires(ssem, rsem)
    tables = [
        pltpu.make_async_copy(src.at[pl.ds(pl.multiple_of(chip * 256, 256), 256)], dst, lsem.at[i])
        for i, (src, dst) in enumerate(((cosine, cos_v), (sine, sin_v)))
    ]
    for copy in tables:
        copy.start()
    steps = sum_chips(dkv, chips, wires, at)
    next(steps)
    up_task = expert_sum(g_up, up_sum, expert_scratch, wires, at)
    next(up_task)
    n, inverse = normed(x[...].astype(F32))
    next(steps)
    next(up_task)
    parts = final(steps)
    for copy in tables:
        copy.wait()
    total = jnp.concatenate(parts, 0)
    dk = turn(total[:, 0:256], cos_v[...], -sin_v[...]).astype(BF)
    grads = jnp.concatenate([dq[...], dk, total[:, 256:512].astype(BF)], 1)
    into = weights[:, :, :, :, :, 0:COL_M].reshape(WIDTH, COL_M)
    back = dot_t(grads, into)
    product[0] = back[0:128]
    product[1] = back[128:256]
    swap = wires.go(product.at[1 - core], arrived, near)
    whole[:, :, :, :, :, 0:COL_M] = dot(h1t[...], grads).astype(BF).reshape(2, 4, 4, 3, 16, COL_M)
    whole[:, :, :, :, :, COL_END:IN_H] = jnp.zeros((2, 4, 4, 3, 16, IN_H - COL_END), BF)
    got([swap])
    d_hidden = product[core] + arrived[...]
    line = jnp.sum(d_hidden * n, 0, keepdims=True)
    tiny = small[...] + jnp.where(iota((128, WIDTH), 0) == EXPERTS, line, 0.0)
    whole[:, :, :, :, :, COL_M:COL_END] = (
        jnp.transpose(tiny).astype(BF).reshape(2, 4, 4, 3, 16, 128)
    )
    sums = gather_sums(whole, IN_Q, landings, wires, at)
    next(sums)
    grad_in[...] = d_mid[...] + norm_back(d_hidden, rows[0:1], n, inverse)
    next(up_task)
    finish(sums, up_task)
    lanes = pl.ds(pl.multiple_of(xh * IN_Q, 128), IN_Q)
    unit = jnp.concatenate([whole[xx % 2, z, y, part, :, lanes] for part in range(3)], 0)
    unit = jnp.concatenate([unit, unit_o[...].reshape(48, OUT_Q)], 1)
    slots[...] = dot(regroup_back(), unit).astype(BF).reshape(4, 16, STAGE)
    mine = core * 2 + xh
    copies = [
        wires.go(slots.at[peer[0] // 2 * 2 + peer[3]], taken.at[mine], peer)
        for peer in (near, ring(at, 0, 2), diagonal)
    ]
    taken[mine] = slots[xh * 2 + core]
    got(copies)
    tiny = jnp.zeros((12, 128), F32)
    for i in range(2):
        left, right = taken[2 * i].astype(F32)[0:12], taken[2 * i + 1].astype(F32)[0:12]
        g_q[:, 768 * i : 768 * i + 768] = left[:, 0:IN_Q]
        g_k[:, 256 * i : 256 * i + 256] = right[:, 0:256]
        g_v[:, 256 * i : 256 * i + 256] = right[:, 256:512]
        g_o[:, 768 * i : 768 * i + OUT_Q] = left[:, IN_Q:STAGE]
        g_o[:, 768 * i + OUT_Q : 768 * i + 768] = right[:, IN_Q:STAGE]
        tiny += right[:, 512:640]
    g_m[...] = tiny
    wires.close()


def last_call(dkv, dq, h1t, weights, unit_o, small, x, d_mid, rows, g_up, cosine, sine):
    return pl.pallas_call(
        last_kernel,
        out_shape=[
            shape((ROWS, WIDTH), F32),
            shape((12, WIDTH), F32),
            shape((12, 512), F32),
            shape((12, 512), F32),
            shape((12, WIDTH), F32),
            shape((12, 128), F32),
            shape((2, 192, FF), F32),
        ],
        in_specs=[vm()] * 9 + [hbm()] * 3,
        out_specs=[vm()] * 7,
        scratch_shapes=[
            pltpu.VMEM((2, 4, 4, 3, 16, IN_H), BF),
            pltpu.VMEM((2, ROWS, WIDTH), F32),
            pltpu.VMEM((ROWS, WIDTH), F32),
            pltpu.VMEM((4, 16, STAGE), BF),
            pltpu.VMEM((4, 16, STAGE), BF),
            pltpu.VMEM((256, 128), F32),
            pltpu.VMEM((256, 128), F32),
            *landing_shapes(IN_Q),
            *sum_scratch(128, 512),
            *expert_sum_scratch(192, FF),
            *wire_sems(56),
            pltpu.SemaphoreType.DMA((2,)),
        ],
        compiler_params=pltpu.CompilerParams(
            collective_id=6, has_side_effects=True, vmem_limit_bytes=VMEM_BYTES
        ),
        name="weight_grad",
    )(
        dkv.reshape(2, 4, 2, 128, 512), dq, h1t, weights, unit_o, small, x, d_mid, rows,
        g_up.reshape(2, 2, 4, 192, FF), cosine, sine,
    )


def tables():
    frequency = np.exp(
        np.arange(HEAD // 2, dtype=np.float32) * np.float32(-2.0 * math.log(10000.0) / HEAD)
    )
    angles = np.arange(LENGTH, dtype=np.float32)[:, None] * frequency[None, :]
    cosine, sine = np.cos(angles), np.sin(angles)
    return (
        np.concatenate([cosine] * 4, 1).astype(np.float32),
        np.concatenate([-sine, sine] * 2, 1).astype(np.float32),
    )


def stage_weights(w_query, key_weight, value_weight, w_out, w_router, gain_attn, gain_ffn):
    small = jnp.concatenate([w_router, gain_attn[:, None], gain_ffn[:, None]], 1)
    small = jnp.pad(small, ((0, 0), (0, IN_H - COL_M - EXPERTS - 2)))
    quarters = []
    for i in range(2):
        own_out = w_out[:, 768 * i : 768 * i + 768]
        quarters.append([w_query[:, 768 * i : 768 * i + 768], own_out[:, :OUT_Q]])
        quarters.append(
            [
                key_weight[:, 256 * i : 256 * i + 256],
                value_weight[:, 256 * i : 256 * i + 256],
                small,
                own_out[:, OUT_Q:],
            ]
        )
    stage = jnp.stack([jnp.concatenate(quarter, 1) for quarter in quarters])
    return jnp.pad(stage, ((0, 0), (0, 4), (0, 0)))


def body(
    block_in, routes, cotangent, gain_attn, w_query, key_weight, value_weight, w_out,
    gain_ffn, w_router, w_gate, w_up, w_down,
):
    cosine, sine = (jnp.asarray(table) for table in tables())
    x, dy = block_in[0], cotangent[0]
    stage = stage_weights(
        w_query, key_weight, value_weight, w_out, w_router, gain_attn, gain_ffn
    )
    (
        rows, router, q, h1t, ot, lse, middle, gates,
        weights, wo, kv, tall, all_dy, gate_full, up_full, down_full,
    ) = forward_call(
        stage, x, routes[0], cosine, sine, dy.reshape(2, 64, WIDTH), w_gate, w_up, w_down
    )
    kv = kv.reshape(LENGTH, 512)
    out_rows, d_rows, g_gate, g_up, g_down = expert_call(tall, all_dy, gate_full, up_full, down_full)
    d_mid, d_o, small, g_out, g_down = token_grad_call(
        d_rows, middle, gates, dy, rows, router, wo, ot, g_down
    )
    dq, dkv, block_out, unit_o, g_gate = attend_back_call(
        q, kv, d_o, lse, out_rows, middle, g_out, g_gate, cosine, sine
    )
    grad_in, g_q, g_k, g_v, g_o, g_m, g_up = last_call(
        dkv, dq, h1t, weights, unit_o, small, x, d_mid, rows, g_up, cosine, sine
    )
    return (
        block_out[None],
        grad_in[None],
        g_m[:, EXPERTS],
        g_q,
        g_k,
        g_v,
        g_o,
        g_m[:, EXPERTS + 1],
        g_m[:, 0:EXPERTS],
        g_gate,
        g_up,
        g_down,
    )


def solution(mesh):
    tokens, owned, experts = P("seq", "ctx", None), P(("seq", "ctx"), None), P("ctx", "seq", None)
    vector = P(("seq", "ctx"))
    return jax.shard_map(
        body,
        mesh=mesh,
        in_specs=(
            tokens, tokens, tokens, vector, owned, owned, owned, owned, vector, owned,
            experts, experts, experts,
        ),
        out_specs=(
            tokens, tokens, vector, owned, owned, owned, owned, vector, owned,
            experts, experts, experts,
        ),
        check_vma=False,
    )
```

```python
import functools
import math

import jax
import jax.numpy as jnp
import numpy as np
from jax import lax
from jax.experimental import pallas as pl
from jax.experimental.pallas import tpu as pltpu
from jax.sharding import PartitionSpec as P

WIDTH = 1536
HEADS = 24
KV_HEADS = 8
HEAD = 64
TOPK = 8
ROWS = 128
LENGTH = 2048
EXPERTS = 32
FF = 512
CAP = 48
EPSILON = 1e-06

BF = jnp.bfloat16
F32 = jnp.float32
MESH = pl.DeviceIdType.MESH
VMEM_BYTES = 60 << 20

IN_Q, OUT_Q = 768, 384
IN_H, OUT_H = 2 * IN_Q, 2 * OUT_Q
STAGE = IN_Q + OUT_Q
COL_K, COL_V, COL_M, COL_END = 768, 1024, 1280, 1408
TALL = WIDTH + 128


def vm():
    return pl.BlockSpec(memory_space=pltpu.VMEM)


def hbm():
    return pl.BlockSpec(memory_space=pl.ANY)


def shape(dims, dtype=BF):
    return jax.ShapeDtypeStruct(dims, dtype)


def place():
    seq, ctx = lax.axis_index("seq"), lax.axis_index("ctx")
    return (ctx // 2 % 2 * 2 + seq // 4, ctx // 4, seq % 4, ctx % 2)


def device(x, y, z, core):
    return (x % 2 * 4 + z, (y * 2 + x // 2) * 2 + core)


def ring(at, dim, step):
    x, y, z, core = at
    if dim == 0:
        return ((x + step) % 4, y, z, core)
    if dim == 1:
        return (x, (y + step) % 4, z, core)
    return (x, y, (z + step) % 4, core)


def sibling(at):
    return (at[0], at[1], at[2], 1 - at[3])


def greet(peers):
    barrier = pltpu.get_barrier_semaphore()
    for peer in peers:
        pl.semaphore_signal(barrier, inc=1, device_id=device(*peer), device_id_type=MESH)
    pl.semaphore_wait(barrier, len(peers))


class Wires:
    def __init__(self, send, recv):
        self.send, self.recv, self.used, self.open = send, recv, 0, []

    def go(self, src, dst, peer):
        n = self.used
        self.used += 1
        copy = pltpu.make_async_remote_copy(
            src_ref=src,
            dst_ref=dst,
            send_sem=self.send.at[n],
            recv_sem=self.recv.at[n],
            device_id=device(*peer),
            device_id_type=MESH,
        )
        copy.start()
        self.open.append(copy)
        return copy

    def close(self):
        for copy in self.open:
            copy.wait_send()


def wire_sems(n):
    return [pltpu.SemaphoreType.DMA((n,)), pltpu.SemaphoreType.DMA((n,))]


def got(copies):
    for copy in copies:
        copy.wait_recv()


def dot(a, b):
    return jnp.dot(a, b, preferred_element_type=F32)


def dot_t(a, b):
    return lax.dot_general(a, b, (((1,), (1,)), ((), ())), preferred_element_type=F32)


def t_dot(a, b):
    return lax.dot_general(a, b, (((0,), (0,)), ((), ())), preferred_element_type=F32)


def iota(dims, axis):
    return lax.broadcasted_iota(jnp.int32, dims, axis)


def turn(block, cosine, sine):
    low = iota((block.shape[0], 128), 1) % HEAD < HEAD // 2
    parts = []
    for i in range(block.shape[1] // 128):
        unit = block[:, 128 * i : 128 * i + 128]
        other = jnp.where(low, pltpu.roll(unit, 96, 1), pltpu.roll(unit, 32, 1))
        parts.append(unit * cosine + other * sine)
    return jnp.concatenate(parts, 1)


def regroup():
    r, c = iota((48, 64), 0), iota((48, 64), 1)
    owner = c // 16 % 2 * 2 + c // 32
    hit = (r == owner * 12 + c % 16) & (c % 16 < 12)
    return hit.astype(F32).astype(BF)


def regroup_back():
    r, c = iota((64, 48), 0), iota((64, 48), 1)
    hit = (c == r // 16 * 12 + r % 16) & (r % 16 < 12)
    return hit.astype(F32).astype(BF)


ORDERS = ((0, 1, 2), (1, 2, 0), (2, 0, 1))


def block_of(quarter, part, fixed, at):
    x, y, z, _ = at
    whole = slice(None)
    columns = (
        pl.ds(pl.multiple_of(x // 2 * quarter, 128), quarter)
        if 0 in fixed
        else pl.ds(0, 2 * quarter)
    )
    return (
        x % 2 if 0 in fixed else whole,
        z if 2 in fixed else whole,
        y if 1 in fixed else whole,
        part,
        whole,
        columns,
    )


def spread(ref, quarter, wires, at):
    waits = [[], [], []]
    for phase in range(3):
        for part in range(3):
            got(waits[part])
            waits[part] = []
            fixed = ORDERS[part][phase:]
            spot = ref.at[block_of(quarter, part, fixed, at)]
            for step in (1, 2, 3):
                waits[part].append(wires.go(spot, spot, ring(at, fixed[0], step)))
        yield
    for part in range(3):
        got(waits[part])


def finish(*tasks):
    for task in tasks:
        for _ in task:
            pass


def partner(at):
    return (at[0] + 1 - 2 * (at[0] % 2), at[1], at[2], at[3])


def expert_spread(shard, full, wires, at, sem):
    x, _, z, _ = at
    left, right = ring(at, 2, 3), ring(at, 2, 1)
    spot = full.at[:, x % 2, z]
    local = pltpu.make_async_copy(shard, spot, sem)
    local.start()
    pair = wires.go(shard, spot, partner(at))
    yield
    local.wait()
    got([pair])
    spot = full.at[:, :, z]
    a = wires.go(spot, spot, right)
    b = wires.go(spot, spot, left)
    yield
    got([a])
    spot = full.at[0, :, (z + 3) % 4]
    a = wires.go(spot, spot, right)
    got([b])
    spot = full.at[1, :, (z + 1) % 4]
    b = wires.go(spot, spot, left)
    yield
    got([a, b])


def expert_sum_scratch(rows, columns):
    return [
        pltpu.VMEM((2, 2, rows, columns), BF),
        pltpu.VMEM((2, 2, rows, columns), BF),
        pltpu.VMEM((2, 2, rows, columns), BF),
        pltpu.VMEM((2, 2, 2, rows, columns), BF),
        pltpu.VMEM((2, rows, columns), BF),
        pltpu.SemaphoreType.DMA((3,)),
    ]


def expert_sum(grads, result, scratch, wires, at):
    passing, own, halves, pairs, last, lsem = scratch
    z, x_lo = at[2], at[0] % 2
    up, down = ring(at, 2, 1), ring(at, 2, 3)
    above, below, across = (z + 1) % 4, (z + 3) % 4, (z + 2) % 4
    loads = [
        pltpu.make_async_copy(src, dst, lsem.at[i])
        for i, (src, dst) in enumerate(
            (
                (grads.at[0, :, above], passing.at[0]),
                (grads.at[1, :, below], passing.at[1]),
                (grads.at[:, :, z], own),
            )
        )
    ]
    for copy in loads:
        copy.start()
    a = wires.go(grads.at[0, :, across], halves.at[0], up)
    b = wires.go(grads.at[1, :, across], halves.at[1], down)
    direct = [
        wires.go(grads.at[1, :, above], pairs.at[0, 1], up),
        wires.go(grads.at[0, :, below], pairs.at[1, 0], down),
    ]
    yield
    for copy in loads:
        copy.wait()
    got([a])
    for i in range(2):
        passing[0, i] = (passing[0, i].astype(F32) + halves[0, i].astype(F32)).astype(BF)
    a = wires.go(passing.at[0], pairs.at[0, 0], up)
    got([b])
    for i in range(2):
        passing[1, i] = (passing[1, i].astype(F32) + halves[1, i].astype(F32)).astype(BF)
    b = wires.go(passing.at[1], pairs.at[1, 1], down)
    yield
    got([*direct, a, b])
    for e in range(2):
        for i in range(2):
            own[e, i] = (
                own[e, i].astype(F32) + pairs[0, e, i].astype(F32) + pairs[1, e, i].astype(F32)
            ).astype(BF)
    a = wires.go(own.at[:, 1 - x_lo], last, partner(at))
    yield
    got([a])
    for e in range(2):
        result[e] = own[e, x_lo].astype(F32) + last[e].astype(F32)


def ctx_peers(at):
    return [ring(at, 1, 1), ring(at, 1, 2), ring(at, 1, 3), ring(at, 0, 2)]


def all_peers(at):
    return [ring(at, d, s) for d in range(3) for s in (1, 2, 3)]


def share(spot, wires, at, inner=True):
    x, y, _, _ = at
    xh = x // 2
    near, far, up, down = sibling(at), ring(at, 0, 2), ring(at, 1, 1), ring(at, 1, 3)
    above, below, across = (y + 1) % 4, (y + 3) % 4, (y + 2) % 4
    kept = []

    def send(where, peer):
        return wires.go(spot(*where), spot(*where), peer)

    def pass_on(*where):
        if inner:
            kept.append(send(where, near))

    a, b = send((y, xh), up), send((y, xh), down)
    c = send((y, xh), far)
    pass_on(y, xh)
    yield
    got([a])
    a1 = send((below, xh, 0), up)
    got([b])
    b1 = send((above, xh, 1), down)
    pass_on(below, xh)
    pass_on(above, xh)
    got([c])
    a2, b2 = send((y, 1 - xh), up), send((y, 1 - xh), down)
    pass_on(y, 1 - xh)
    yield
    got([a1, b1])
    pass_on(across, xh)
    got([a2])
    a3 = send((below, 1 - xh, 0), up)
    got([b2])
    b3 = send((above, 1 - xh, 1), down)
    pass_on(below, 1 - xh)
    pass_on(above, 1 - xh)
    yield
    got([a3, b3])
    pass_on(across, 1 - xh)
    yield
    got(kept)


def share_rows(ref, wires, at):
    core = at[3]
    return share(lambda y, xh, *half: ref.at[(y, xh, core, *half)], wires, at)


def share_rows_two(ref, wires, at):
    x, y, _, core = at
    xh = x // 2
    near, far = sibling(at), ring(at, 0, 2)

    def pass_on(spot, peer):
        return wires.go(spot, spot, peer)

    inner = [pass_on(ref.at[y, xh, core], near)]
    a = [pass_on(ref.at[y, xh, core, 0], ring(at, 1, s)) for s in (1, 2, 3)]
    b = [pass_on(ref.at[y, xh, core, 1], far)]
    yield
    got(b)
    b = [pass_on(ref.at[y, :, core, 1], ring(at, 1, s)) for s in (1, 2, 3)]
    got(a)
    a = [pass_on(ref.at[:, xh, core, 0], far)]
    inner.append(pass_on(ref.at[y, 1 - xh, core, 1], near))
    for s in (1, 2, 3):
        inner.append(pass_on(ref.at[(y + s) % 4, xh, core, 0], near))
    yield
    got(a)
    inner.append(pass_on(ref.at[:, 1 - xh, core, 0], near))
    got(b)
    for s in (1, 2, 3):
        inner.append(pass_on(ref.at[(y + s) % 4, :, core, 1], near))
    yield
    got(inner)


def ctx_and_sibling(at):
    return ctx_peers(at) + [sibling(at)]


def sum_scratch(rows, columns):
    return [
        pltpu.VMEM((4, rows, columns), BF),
        pltpu.VMEM((3, 2, rows, columns), BF),
        pltpu.VMEM((4, rows, columns), BF),
        pltpu.VMEM((2, rows, columns), BF),
        pltpu.VMEM((3, rows, columns), BF),
        pltpu.VMEM((1, rows, columns), BF),
    ]


def sum_chips(source, scratch, wires, at):
    e0, e1, t0, t1, f0, f1 = scratch
    x, y, _, _ = at
    xh = x // 2
    far = ring(at, 0, 2)
    a = [wires.go(source.at[:, 1 - xh, 0], e0, far)]
    b = [
        wires.go(source.at[(y + s) % 4, :, 1], e1.at[s - 1], ring(at, 1, s)) for s in (1, 2, 3)
    ]
    yield None
    got(a)
    for i in range(4):
        t0[i] = (source[i, xh, 0].astype(F32) + e0[i].astype(F32)).astype(BF)
    a = [wires.go(t0.at[(y + s) % 4], f0.at[s - 1], ring(at, 1, s)) for s in (1, 2, 3)]
    got(b)
    for i in range(2):
        total = source[y, i, 1].astype(F32)
        for s in range(3):
            total += e1[s, i].astype(F32)
        t1[i] = total.astype(BF)
    b = [wires.go(t1.at[1 - xh], f1.at[0], far)]
    yield None
    got(a)
    first = t0[y].astype(F32)
    for s in range(3):
        first += f0[s].astype(F32)
    got(b)
    yield first, t1[xh].astype(F32) + f1[0].astype(F32)


def sum_rows_scratch(columns):
    return [
        pltpu.VMEM((4, 2, 2, 64, columns), BF),
        pltpu.VMEM((4, 2, 2, 64, columns), BF),
        *sum_scratch(64, columns),
        pltpu.SemaphoreType.DMA((2,)),
    ]


def sum_rows(rows, scratch, wires, at):
    landed, own, lsem = scratch[0], scratch[1], scratch[-1]
    core = at[3]
    copies = [
        wires.go(rows.at[:, :, 1 - core, part], landed.at[:, :, part], sibling(at)) for part in range(2)
    ]
    loads = [
        pltpu.make_async_copy(rows.at[:, :, core, part], own.at[:, :, part], lsem.at[part])
        for part in range(2)
    ]
    for copy in loads:
        copy.start()
    yield None
    for part in range(2):
        loads[part].wait()
        got([copies[part]])
        for i in range(4):
            for h in range(2):
                own[i, h, part] = (
                    own[i, h, part].astype(F32) + landed[i, h, part].astype(F32)
                ).astype(BF)
    for result in sum_chips(own, scratch[2:-1], wires, at):
        yield result


def final(steps):
    result = None
    for result in steps:
        pass
    return result


def gather_sums(ref, quarter, landings, wires, at):
    orders = tuple(order[::-1] for order in ORDERS)
    waits = [[], [], []]

    def send(part, phase):
        fixed = orders[part][: phase + 1]
        dim = fixed[-1]
        for step in (1, 2, 3):
            peer = ring(at, dim, step)
            spot = ref.at[block_of(quarter, part, fixed, peer)]
            waits[part].append(wires.go(spot, landings[part][phase].at[step - 1], peer))

    def add(part, phase):
        got(waits[part])
        waits[part] = []
        fixed = orders[part][: phase + 1]
        index = block_of(quarter, part, fixed, at)
        total = ref[index].astype(F32)
        for step in range(3):
            total += landings[part][phase][step].astype(F32)
        ref[index] = total.astype(BF)

    for part in range(3):
        send(part, 0)
    yield
    for phase in range(3):
        for part in range(3):
            add(part, phase)
            if phase < 2:
                send(part, phase + 1)
        yield


def landing_shapes(quarter):
    found = []
    for order in ORDERS:
        for phase in range(3):
            fixed = order[::-1][: phase + 1]
            dims = [size for size, dim in ((2, 0), (4, 2), (4, 1)) if dim not in fixed]
            found.append(pltpu.VMEM((3, *dims, 16, quarter if 0 in fixed else 2 * quarter), BF))
    return found


def normed(values):
    inverse = lax.rsqrt(jnp.mean(values * values, -1, keepdims=True) + EPSILON)
    return values * inverse, inverse


def attend(q, kv, o, ot, lse, scratch, chip, beside):
    scores, vt, qt, qz, out_t = scratch
    qt[...] = jnp.transpose(q[...].astype(F32) * 0.125).astype(BF)
    for kb in range(8):
        block = kv[kb // 2, kb % 2, :, :, 256:512].reshape(256, 256)
        vt[kb] = jnp.transpose(block.astype(F32)).astype(BF)
    allowed = iota((256, 768), 0) <= iota((256, 768), 1) % 256
    for j in range(4):
        u, half = j // 2, j % 2
        qz[...] = jnp.zeros_like(qz)
        for g in range(3):
            h = 3 * j + g
            qz[64 * half : 64 * half + 64, 256 * g : 256 * g + 256] = qt[64 * h : 64 * h + 64]

        def score(kb):
            rows = pl.ds(pl.multiple_of(kb * 256, 256), 256)
            keys = kv[kb // 2, kb % 2, :, :, 128 * u : 128 * u + 128].reshape(256, 128)
            return rows, dot(keys, qz[...])

        def top(kb, most):
            rows, s = score(kb)
            scores[rows] = s
            return jnp.maximum(most, jnp.max(s.reshape(32, 8, 768), 0))

        most = lax.fori_loop(0, chip, top, jnp.full((8, 768), -1e30, F32))
        rows, s = score(chip)
        s = jnp.where(allowed, s, -1e30)
        scores[rows] = s
        most = jnp.maximum(most, jnp.max(s.reshape(32, 8, 768), 0))
        most = jnp.max(most, 0, keepdims=True)

        def raise_(kb, total):
            rows = pl.ds(pl.multiple_of(kb * 256, 256), 256)
            e = jnp.exp(scores[rows] - most)
            scores[rows] = e
            return total + jnp.sum(e.reshape(32, 8, 768), 0)

        beside[2 * j]()
        total = lax.fori_loop(0, chip + 1, raise_, jnp.zeros((8, 768), F32))
        total = jnp.sum(total, 0, keepdims=True)
        lse[j] = jnp.broadcast_to(most + jnp.log(total), (8, 768))
        inverse = 1.0 / total

        def mix(kb, acc):
            rows = pl.ds(pl.multiple_of(kb * 256, 256), 256)
            p = (scores[rows] * inverse).astype(BF)
            return acc + dot(vt[kb, 64 * j : 64 * j + 64], p)

        acc = lax.fori_loop(0, chip + 1, mix, jnp.zeros((64, 768), F32))
        for g in range(3):
            h = 3 * j + g
            out_t[64 * h : 64 * h + 64] = acc[:, 256 * g : 256 * g + 256]
        beside[2 * j + 1]()
    ot[...] = out_t[...].astype(BF)
    out = jnp.transpose(out_t[...]).astype(BF)
    o[0], o[1] = out[0:128], out[128:256]


def forward_kernel(
    stage, x, routes, cosine, sine, dy, w_gate, w_up, w_down,
    rows, router, q, h1t, ot, lse, middle, gates,
    weights_out, wo_out, kv_out, tall, all_dy, gate_full, up_full, down_full,
    weights, columns, wo, kv, both, slots, cos_v, sin_v, o, tall_own, product, arrived,
    scores, vt, qt, qz, out_t, ssem, rsem, lsem,
):
    at = place()
    xx, y, z, core = at
    xh, chip = xx // 2, y * 2 + xx // 2
    near = sibling(at)
    diagonal = sibling(ring(at, 0, 2))
    greet(all_peers(at) + [near, diagonal])
    wires = Wires(ssem, rsem)

    def local(n, src, dst):
        copy = pltpu.make_async_copy(src, dst, lsem.at[n])
        copy.start()
        return copy

    angle = pl.ds(pl.multiple_of(chip * 256, 256), 256)
    angles = [local(0, cosine.at[angle], cos_v), local(1, sine.at[angle], sin_v)]
    dy_in = local(2, dy, all_dy.at[y, xh, core])
    mine = core * 2 + xh
    first = [
        wires.go(stage.at[peer[3] * 2 + peer[0] // 2], slots.at[mine], peer)
        for peer in (near, ring(at, 0, 2), diagonal)
    ]
    tokens = wires.go(x, both.at[core], near)
    slots[mine] = stage[mine]
    both[core] = x[...]
    got(first)
    unit = dot(regroup(), slots[...].reshape(64, STAGE)).astype(BF)
    in_lanes = pl.ds(pl.multiple_of(xh * IN_Q, 128), IN_Q)
    out_lanes = pl.ds(pl.multiple_of(xh * OUT_Q, 128), OUT_Q)
    for part in range(3):
        weights[xx % 2, z, y, part, :, in_lanes] = unit[16 * part : 16 * part + 16, 0:IN_Q]
        columns[xx % 2, z, y, part, :, out_lanes] = unit[16 * part : 16 * part + 16, IN_Q:STAGE]
    in_task = spread(weights, IN_Q, wires, at)
    out_task = spread(columns, OUT_Q, wires, at)
    dy_task = share_rows_two(all_dy, wires, at)
    gate_task = expert_spread(w_gate, gate_full, wires, at, lsem.at[3])
    up_task = expert_spread(w_up, up_full, wires, at, lsem.at[4])
    down_task = expert_spread(w_down, down_full, wires, at, lsem.at[5])
    next(in_task)
    next(in_task)
    next(gate_task)
    next(in_task)
    finish(in_task)
    weights_kept = local(6, weights, weights_out)
    next(gate_task)
    next(up_task)
    dy_in.wait()
    next(dy_task)

    small = weights[:, :, :, :, :, COL_M:COL_END].reshape(WIDTH, 128)
    router[...] = small
    turned = jnp.transpose(small.astype(F32))
    rows[...] = turned[32:40]
    got([tokens])
    values = both[...].reshape(256, WIDTH).astype(F32)
    hidden = (normed(values)[0] * turned[32:33]).astype(BF)
    made = dot(hidden, weights[:, :, :, :, :, 0:COL_M].reshape(WIDTH, COL_M))
    for copy in angles:
        copy.wait()
    cos, sin = cos_v[...], sin_v[...]
    key = turn(made[:, COL_K:COL_V], cos, sin).astype(BF)
    value = made[:, COL_V:COL_M].astype(BF)
    for part in range(2):
        kv[y, xh, part, :, 0:256] = key[128 * part : 128 * part + 128]
        kv[y, xh, part, :, 256:512] = value[128 * part : 128 * part + 128]
    own = [kv.at[y, xh, 0], kv.at[y, xh, 1]]
    a = [wires.go(own[0], own[0], ring(at, 1, s)) for s in (1, 2, 3)]
    b = [wires.go(own[1], own[1], ring(at, 0, 2))]
    q[...] = turn(made[:, 0:COL_K], cos, sin).astype(BF)
    got(b)
    pair = kv.at[y, :, 1]
    b = [wires.go(pair, pair, ring(at, 1, s)) for s in (1, 2, 3)]
    got(a)
    column = kv.at[:, xh, 0]
    a = [wires.go(column, column, ring(at, 0, 2))]
    next(out_task)
    h1t[...] = jnp.transpose(hidden.astype(F32)).astype(BF)
    next(up_task)
    next(down_task)
    next(out_task)
    got(a)
    got(b)
    kv_kept = local(7, kv, kv_out)
    next(gate_task)

    half = pl.ds(pl.multiple_of(core * 768, 128), 768)
    swap = []

    def swap_out():
        finish(out_task)
        swap.append(wires.go(columns.at[1 - core], wo.at[:, :, :, :, half], near))
        for i in range(4):
            wo[i, :, :, :, half] = columns[core, i]

    beside = [
        lambda: next(out_task),
        lambda: next(down_task),
        lambda: next(dy_task),
        lambda: next(up_task),
        swap_out,
        lambda: None,
        lambda: None,
        lambda: None,
    ]
    attend(q, kv, o, ot, lse, (scores, vt, qt, qz, out_t), chip, beside)
    got(swap)
    wo_kept = local(8, wo, wo_out)

    full = wo[...].reshape(768, WIDTH)
    product[0] = dot(o[1 - core], full)
    swap = wires.go(product.at[0], arrived, near)
    product[1] = dot(o[core], full)
    lane = iota((ROWS, 128), 1)
    named = routes[:, 0:1] == lane
    for i in range(1, TOPK):
        named = named | (routes[:, i : i + 1] == lane)
    got([swap])
    mid = x[...].astype(F32) + product[1] + arrived[...]
    middle[...] = mid
    hidden = (normed(mid)[0] * rows[1:2]).astype(BF)
    logits = jnp.where(named, dot(hidden, router[...]), -jnp.inf)
    raised = jnp.exp(logits - jnp.max(logits, -1, keepdims=True))
    gate = raised / jnp.sum(raised, -1, keepdims=True)
    gates[...] = gate
    high = gate.astype(BF).astype(F32)
    two = high + pltpu.roll(gate - high, EXPERTS, 1)
    for part in range(2):
        cut = slice(64 * part, 64 * part + 64)
        tall_own[part, :, 0:WIDTH] = hidden[cut]
        tall_own[part, :, WIDTH:TALL] = two[cut].astype(BF)
    tall_in = local(9, tall_own, tall.at[y, xh, core])
    tall_task = share_rows(tall, wires, at)
    tall_in.wait()
    next(tall_task)
    next(down_task)
    next(dy_task)
    next(tall_task)
    next(tall_task)
    finish(dy_task, gate_task, up_task)
    finish(tall_task, down_task)
    for copy in (weights_kept, kv_kept, wo_kept):
        copy.wait()
    wires.close()


def forward_call(stage, x, routes, cosine, sine, dy, w_gate, w_up, w_down):
    return pl.pallas_call(
        forward_kernel,
        out_shape=[
            shape((8, WIDTH), F32),
            shape((WIDTH, 128)),
            shape((256, 768)),
            shape((WIDTH, 256)),
            shape((768, 256)),
            shape((4, 8, 768), F32),
            shape((ROWS, WIDTH), F32),
            shape((ROWS, 128), F32),
            shape((2, 4, 4, 3, 16, IN_H)),
            shape((4, 4, 3, 16, WIDTH)),
            shape((4, 2, 2, 128, 512)),
            shape((4, 2, 2, 2, 64, TALL)),
            shape((4, 2, 2, 2, 64, WIDTH)),
            shape((2, 2, 4, 192, FF)),
            shape((2, 2, 4, 192, FF)),
            shape((2, 2, 4, 64, WIDTH)),
        ],
        in_specs=[vm()] * 3 + [hbm()] * 2 + [vm()] * 4,
        out_specs=[vm()] * 8 + [hbm()] * 8,
        scratch_shapes=[
            pltpu.VMEM((2, 4, 4, 3, 16, IN_H), BF),
            pltpu.VMEM((2, 4, 4, 3, 16, OUT_H), BF),
            pltpu.VMEM((4, 4, 3, 16, WIDTH), BF),
            pltpu.VMEM((4, 2, 2, 128, 512), BF),
            pltpu.VMEM((2, 128, WIDTH), BF),
            pltpu.VMEM((4, 16, STAGE), BF),
            pltpu.VMEM((256, 128), F32),
            pltpu.VMEM((256, 128), F32),
            pltpu.VMEM((2, 128, 768), BF),
            pltpu.VMEM((2, 64, TALL), BF),
            pltpu.VMEM((2, ROWS, WIDTH), F32),
            pltpu.VMEM((ROWS, WIDTH), F32),
            pltpu.VMEM((LENGTH, 768), F32),
            pltpu.VMEM((8, 256, 256), BF),
            pltpu.VMEM((768, 256), BF),
            pltpu.VMEM((128, 768), BF),
            pltpu.VMEM((768, 256), F32),
            *wire_sems(144),
            pltpu.SemaphoreType.DMA((10,)),
        ],
        compiler_params=pltpu.CompilerParams(
            collective_id=1, has_side_effects=True, vmem_limit_bytes=VMEM_BYTES
        ),
        name="forward",
    )(stage, x, routes, cosine, sine, dy, w_gate, w_up, w_down)


def expert_kernel(
    tall, dy, w_gate, w_up, w_down,
    out_rows, d_rows, g_gate, g_up, g_down,
    big, wide, a_rows, y_rows, r_rows, back, wg, wu, wd, gg, gu, gd, m_s, dg_s, du_s, slot_t, sem,
):
    ctx = lax.axis_index("ctx")
    loads = [
        pltpu.make_async_copy(src, dst, sem.at[i])
        for i, (src, dst) in enumerate(
            ((tall, big), (dy, wide), (w_gate, wg), (w_up, wu), (w_down, wd))
        )
    ]
    for copy in loads:
        copy.start()
    lane = iota((128, 128), 1)
    earlier = (iota((128, 128), 1) < iota((128, 128), 0)).astype(F32).astype(BF)
    slots = iota((CAP, 128), 0).astype(F32)
    loads[0].wait()
    loads[1].wait()

    def collect(b, _):
        rows = pl.ds(pl.multiple_of(b * 128, 128), 128)
        packed = pl.ds(pl.multiple_of(b * CAP, CAP), CAP)
        both = big[rows, WIDTH:TALL].astype(F32)
        gate = both + pltpu.roll(both, 128 - EXPERTS, 1)
        hot = (gate > 0.0) & (lane < EXPERTS)
        rank = dot(earlier, hot.astype(F32).astype(BF))
        slot = jnp.where(hot, rank, -1.0)
        slot_t[...] = jnp.transpose(slot)
        picks = [
            (slot_t[pl.ds(2 * ctx + i, 1), :] == slots).astype(F32).astype(BF) for i in range(2)
        ]
        pick = jnp.concatenate(picks, 0)
        found = dot(pick, big[rows, :]).astype(BF)
        grads = dot(pick, wide[rows, :]).astype(BF)
        for i in range(2):
            a_rows[i, packed] = found[CAP * i : CAP * i + CAP]
            y_rows[i, packed] = grads[CAP * i : CAP * i + CAP]
        column = [
            jnp.sum(jnp.where(lane == 2 * ctx + i, slot, 0.0), 1, keepdims=True) for i in range(2)
        ]
        spot = lane.astype(F32)
        put = jnp.where(lane < CAP, column[0], column[1] + CAP) == spot
        back[b] = put.astype(F32).astype(BF)
        return 0

    lax.fori_loop(0, 16, collect, 0)
    for copy in loads[2:]:
        copy.wait()
    stores = []
    for e in range(2):
        number = 2 * ctx + e

        def forward(c, _):
            rows = pl.ds(pl.multiple_of(c * 384, 384), 384)
            a = a_rows[e, rows, 0:WIDTH]
            ag, au = dot(a, wg[e]), dot(a, wu[e])
            sg = jax.nn.sigmoid(ag)
            act = ag * sg
            m = (act * au).astype(BF)
            r = dot(m, wd[e]).astype(BF).astype(F32)
            lanes = iota((384, 128), 1)
            hits = (lanes == number) | (lanes == number + EXPERTS)
            gate = jnp.sum(
                jnp.where(hits, a_rows[e, rows, WIDTH:TALL].astype(F32), 0.0), 1, keepdims=True
            )
            y = y_rows[e, rows].astype(F32)
            d_gate = jnp.sum(y * r, 1, keepdims=True)
            r_rows[e, rows] = (gate * r).astype(BF)
            gr = (gate * y).astype(BF)
            y_rows[e, rows] = gr
            dm = dot_t(gr, wd[e])
            m_s[rows] = m
            dg_s[rows] = (dm * au * (sg * (1.0 + ag * (1.0 - sg)))).astype(BF)
            du_s[rows] = (dm * act).astype(BF)
            high = d_gate.astype(BF).astype(F32)
            d_both = jnp.where(
                lanes == number, high, jnp.where(lanes == number + EXPERTS, d_gate - high, 0.0)
            )
            a_rows[e, rows, WIDTH:TALL] = d_both.astype(BF)
            return 0

        lax.fori_loop(0, 2, forward, 0)
        gd[e] = t_dot(m_s[...], y_rows[e]).astype(BF)
        gg[e] = t_dot(a_rows[e, :, 0:WIDTH], dg_s[...]).astype(BF)
        gu[e] = t_dot(a_rows[e, :, 0:WIDTH], du_s[...]).astype(BF)
        for i, (src, dst) in enumerate(((gd, g_down), (gg, g_gate), (gu, g_up))):
            copy = pltpu.make_async_copy(src.at[e], dst.at[e], sem.at[5 + 3 * e + i])
            copy.start()
            stores.append(copy)

        def to_tokens(c, _):
            rows = pl.ds(pl.multiple_of(c * 384, 384), 384)
            back_rows = dot_t(dg_s[rows], wg[e]) + dot_t(du_s[rows], wu[e])
            a_rows[e, rows, 0:WIDTH] = back_rows.astype(BF)
            return 0

        lax.fori_loop(0, 2, to_tokens, 0)

    def hand_back(b, _):
        rows = pl.ds(pl.multiple_of(b * 128, 128), 128)
        packed = pl.ds(pl.multiple_of(b * CAP, CAP), CAP)
        put = back[b][:, 0 : 2 * CAP]
        big[rows, :] = dot(put, jnp.concatenate([a_rows[0, packed], a_rows[1, packed]], 0)).astype(BF)
        wide[rows, :] = dot(put, jnp.concatenate([r_rows[0, packed], r_rows[1, packed]], 0)).astype(BF)
        return 0

    lax.fori_loop(0, 16, hand_back, 0)
    for i, (src, dst) in enumerate(((big, d_rows), (wide, out_rows))):
        copy = pltpu.make_async_copy(src, dst, sem.at[i])
        copy.start()
        stores.append(copy)
    for copy in stores:
        copy.wait()


def expert_call(tall, dy, w_gate, w_up, w_down):
    slots = 16 * CAP
    return pl.pallas_call(
        expert_kernel,
        out_shape=[
            shape((LENGTH, WIDTH)),
            shape((LENGTH, TALL)),
            shape((2, WIDTH, FF)),
            shape((2, WIDTH, FF)),
            shape((2, FF, WIDTH)),
        ],
        in_specs=[hbm()] * 5,
        out_specs=[hbm()] * 5,
        scratch_shapes=[
            pltpu.VMEM((LENGTH, TALL), BF),
            pltpu.VMEM((LENGTH, WIDTH), BF),
            pltpu.VMEM((2, slots, TALL), BF),
            pltpu.VMEM((2, slots, WIDTH), BF),
            pltpu.VMEM((2, slots, WIDTH), BF),
            pltpu.VMEM((16, 128, 128), BF),
            pltpu.VMEM((2, WIDTH, FF), BF),
            pltpu.VMEM((2, WIDTH, FF), BF),
            pltpu.VMEM((2, FF, WIDTH), BF),
            pltpu.VMEM((2, WIDTH, FF), BF),
            pltpu.VMEM((2, WIDTH, FF), BF),
            pltpu.VMEM((2, FF, WIDTH), BF),
            pltpu.VMEM((slots, FF), BF),
            pltpu.VMEM((slots, FF), BF),
            pltpu.VMEM((slots, FF), BF),
            pltpu.VMEM((128, 128), F32),
            pltpu.SemaphoreType.DMA((11,)),
        ],
        compiler_params=pltpu.CompilerParams(vmem_limit_bytes=VMEM_BYTES),
        name="experts",
    )(
        tall.reshape(LENGTH, TALL), dy.reshape(LENGTH, WIDTH), w_gate.reshape(2, WIDTH, FF),
        w_up.reshape(2, WIDTH, FF), w_down.reshape(2, FF, WIDTH),
    )


def split_dot(left, right, form):
    high = left.astype(BF)
    low = (left - high.astype(F32)).astype(BF)
    return form(high, right) + form(low, right)


def norm_back(grad, gain, n, inverse):
    scaled = grad * gain
    return inverse * (scaled - n * jnp.mean(scaled * n, -1, keepdims=True))


def token_grad_kernel(
    d_rows, middle, gates, dy, rows, router, wo, ot, g_down,
    d_mid, d_o, small, g_out, down_sum,
    low, product, *rest,
):
    scratch, expert_scratch, (ssem, rsem) = rest[:9], rest[9:15], rest[15:]
    at = place()
    core = at[3]
    near = sibling(at)
    greet(ctx_and_sibling(at) + [ring(at, 2, 1), ring(at, 2, 3), partner(at)])
    wires = Wires(ssem, rsem)
    steps = sum_rows(d_rows, scratch, wires, at)
    next(steps)
    down_task = expert_sum(g_down, down_sum, expert_scratch, wires, at)
    next(down_task)
    next(steps)
    next(down_task)
    n, inverse = normed(middle[...])
    hidden = (n * rows[1:2]).astype(BF)
    parts = final(steps)
    total = jnp.concatenate(parts, 0)
    d_hidden = total[:, 0:WIDTH]
    both = total[:, WIDTH:TALL]
    gate = gates[...]
    lane = iota((ROWS, 128), 1)
    d_gate = jnp.where(lane < EXPERTS, both + pltpu.roll(both, 128 - EXPERTS, 1), 0.0)
    centre = jnp.sum(gate * d_gate, -1, keepdims=True)
    d_logits = gate * (d_gate - centre)
    d_hidden += split_dot(d_logits, router[...], dot_t)
    d_middle = norm_back(d_hidden, rows[1:2], n, inverse) + dy[...].astype(F32)
    d_low = d_middle.astype(BF)
    low[core] = d_low
    swap = wires.go(low.at[core], low.at[core], near)
    d_mid[...] = d_middle
    grads = split_dot(jnp.transpose(d_logits), hidden, dot)
    line = jnp.sum(d_hidden * n, 0, keepdims=True)
    small[...] = (grads + jnp.where(iota((128, WIDTH), 0) == EXPERTS + 1, line, 0.0))[0:40]
    next(down_task)
    got([swap])
    chip_rows = low[...].reshape(256, WIDTH)
    d_o[...] = dot_t(chip_rows, wo[...].reshape(768, WIDTH)).astype(BF)
    product[...] = dot(ot[...], chip_rows).astype(BF).reshape(4, 4, 3, 16, WIDTH)
    lanes = pl.ds(pl.multiple_of((1 - core) * 768, 128), 768)
    mine = pl.ds(pl.multiple_of(core * 768, 128), 768)
    swap = wires.go(product.at[:, :, :, :, lanes], g_out.at[core], near)
    for i in range(4):
        g_out[core, i] = product[i, :, :, :, mine]
    finish(down_task)
    got([swap])
    wires.close()


def token_grad_call(d_rows, middle, gates, dy, rows, router, wo, ot, g_down):
    return pl.pallas_call(
        token_grad_kernel,
        out_shape=[
            shape((ROWS, WIDTH), F32),
            shape((256, 768)),
            shape((40, WIDTH), F32),
            shape((2, 4, 4, 3, 16, 768)),
            shape((2, 64, WIDTH), F32),
        ],
        in_specs=[hbm()] + [vm()] * 7 + [hbm()],
        out_specs=[vm()] * 5,
        scratch_shapes=[
            pltpu.VMEM((2, ROWS, WIDTH), BF),
            pltpu.VMEM((4, 4, 3, 16, WIDTH), BF),
            *sum_rows_scratch(TALL),
            *expert_sum_scratch(64, WIDTH),
            *wire_sems(24),
        ],
        compiler_params=pltpu.CompilerParams(
            collective_id=4, has_side_effects=True, vmem_limit_bytes=VMEM_BYTES
        ),
        name="token_grad",
    )(
        d_rows.reshape(4, 2, 2, 2, 64, TALL), middle, gates, dy, rows, router, wo, ot,
        g_down.reshape(2, 2, 4, 64, WIDTH),
    )


def attend_back(q, kv, d_o, lse, dq, scratch, chip, turned_back, beside):
    probs, acc, kt, qt, dot_, qz, oz, dqt = scratch
    qt[...] = jnp.transpose(q[...].astype(F32) * 0.125).astype(BF)
    dot_[...] = jnp.transpose(d_o[...].astype(F32)).astype(BF)
    for kb in range(8):
        block = kv[kb // 2, kb % 2, :, :, 0:256].reshape(256, 256)
        kt[kb] = jnp.transpose(block.astype(F32)).astype(BF)
    allowed = iota((256, 768), 0) <= iota((256, 768), 1) % 256
    for j in range(4):
        u, half = j // 2, j % 2
        keys, values = slice(128 * u, 128 * u + 128), slice(256 + 128 * u, 384 + 128 * u)
        if half == 0:
            acc[...] = jnp.zeros_like(acc)
        qz[...] = jnp.zeros_like(qz)
        oz[...] = jnp.zeros_like(oz)
        for g in range(3):
            h = 3 * j + g
            qz[64 * half : 64 * half + 64, 256 * g : 256 * g + 256] = qt[64 * h : 64 * h + 64]
            oz[64 * half : 64 * half + 64, 256 * g : 256 * g + 256] = dot_[64 * h : 64 * h + 64]
        level = lse[j, 0:1]

        def d_share(kb):
            return dot(kv[kb // 2, kb % 2, :, :, values].reshape(256, 128), oz[...])

        def share_of(kb, centre, masked):
            rows = pl.ds(pl.multiple_of(kb * 256, 256), 256)
            block = kv[kb // 2, kb % 2, :, :, keys].reshape(256, 128)
            p = jnp.exp(dot(block, qz[...]) - level)
            if masked:
                p = jnp.where(allowed, p, 0.0)
            probs[rows] = p
            acc[rows, 128:256] += dot_t(p.astype(BF), oz[...])
            return centre + jnp.sum((p * d_share(kb)).reshape(32, 8, 768), 0)

        centre = lax.fori_loop(
            0, chip, functools.partial(share_of, masked=False), jnp.zeros((8, 768), F32)
        )
        beside(4 * j)
        centre = share_of(chip, centre, True)
        centre = jnp.sum(centre, 0, keepdims=True)
        beside(4 * j + 1)

        def back(kb, total):
            rows = pl.ds(pl.multiple_of(kb * 256, 256), 256)
            ds = (probs[rows] * (d_share(kb) - centre)).astype(BF)
            acc[rows, 0:128] += dot_t(ds, qz[...])
            return total + dot(kt[kb, 64 * j : 64 * j + 64], ds)

        total = lax.fori_loop(0, chip, back, jnp.zeros((64, 768), F32))
        beside(4 * j + 2)
        total = back(chip, total)
        for g in range(3):
            h = 3 * j + g
            dqt[64 * h : 64 * h + 64] = total[:, 256 * g : 256 * g + 256] * 0.125
        if half == 1:
            for kb in range(8):
                for part in range(2):
                    row = 256 * kb + 128 * part
                    kv[kb // 2, kb % 2, part, :, keys] = acc[row : row + 128, 0:128].astype(BF)
                    kv[kb // 2, kb % 2, part, :, values] = acc[row : row + 128, 128:256].astype(BF)
        beside(4 * j + 3)
    dq[...] = turned_back(jnp.transpose(dqt[...])).astype(BF)


def backward_kernel(
    q, d_o, lse, middle, h1t, small, x, rows,
    kv_in, d_mid, out_rows, g_out, g_gate, g_up, weights, cosine, sine,
    grad_in, block_out, g_q, g_k, g_v, g_o, g_m, gate_sum, up_sum,
    columns, whole, kv, dq, product, arrived, slots, taken, cos_v, sin_v, *rest,
):
    att_scratch, rest = rest[:8], rest[8:]
    row_scratch, rest = rest[:9], rest[9:]
    out_landings, rest = [rest[3 * i : 3 * i + 3] for i in range(3)], rest[9:]
    in_landings, rest = [rest[3 * i : 3 * i + 3] for i in range(3)], rest[9:]
    gate_scratch, up_scratch, chips, (ssem, rsem, lsem) = rest[:6], rest[6:12], rest[12:18], rest[18:]
    at = place()
    xx, y, z, core = at
    xh, chip = xx // 2, y * 2 + xx // 2
    near = sibling(at)
    diagonal = sibling(ring(at, 0, 2))
    greet(all_peers(at) + [near, diagonal])
    wires = Wires(ssem, rsem)

    def local(n, src, dst):
        copy = pltpu.make_async_copy(src, dst, lsem.at[n])
        copy.start()
        return copy

    columns_in = local(2, g_out, columns)
    kv_loaded = local(4, kv_in, kv)
    d_mid_in = local(5, d_mid, grad_in)
    angle = pl.ds(pl.multiple_of(chip * 256, 256), 256)
    angles = [local(0, cosine.at[angle], cos_v), local(1, sine.at[angle], sin_v)]
    row_task = sum_rows(out_rows, row_scratch, wires, at)
    gate_task = expert_sum(g_gate, gate_sum, gate_scratch, wires, at)
    up_task = expert_sum(g_up, up_sum, up_scratch, wires, at)
    out_task = gather_sums(columns, OUT_Q, out_landings, wires, at)
    next(row_task)
    next(gate_task)
    columns_in.wait()
    next(out_task)

    def put_out():
        parts = final(row_task)
        for part in range(2):
            cut = slice(64 * part, 64 * part + 64)
            block_out[cut] = (middle[cut] + parts[part]).astype(BF)

    steps_beside = {
        3: lambda: next(row_task),
        9: lambda: next(gate_task),
        12: lambda: next(row_task),
    }

    def beside(n):
        if n in steps_beside:
            steps_beside[n]()

    def turned_back(values):
        for copy in angles:
            copy.wait()
        return turn(values, cos_v[...], -sin_v[...])

    weights_in = local(3, weights, whole)
    kv_loaded.wait()
    attend_back(q, kv, d_o, lse, dq, att_scratch, chip, turned_back, beside)
    steps = sum_chips(kv, chips, wires, at)
    next(steps)
    n, inverse = normed(x[...].astype(F32))
    next(gate_task)
    next(up_task)
    next(out_task)
    next(steps)
    next(out_task)
    parts = final(steps)
    next(out_task)
    next(up_task)
    total = jnp.concatenate(parts, 0)
    dk = turn(total[:, 0:256], cos_v[...], -sin_v[...]).astype(BF)
    grads = jnp.concatenate([dq[...], dk, total[:, 256:512].astype(BF)], 1)
    weights_in.wait()
    back = dot_t(grads, whole[:, :, :, :, :, 0:COL_M].reshape(WIDTH, COL_M))
    product[0] = back[0:128]
    product[1] = back[128:256]
    swap = wires.go(product.at[1 - core], arrived, near)
    for i in range(8):
        made = dot(h1t[192 * i : 192 * i + 192], grads).astype(BF)
        whole[i // 4, i % 4, :, :, :, 0:COL_M] = made.reshape(4, 3, 16, COL_M)
    whole[:, :, :, :, :, COL_END:IN_H] = jnp.zeros((2, 4, 4, 3, 16, IN_H - COL_END), BF)
    put_out()
    got([swap])
    d_hidden = product[core] + arrived[...]
    line = jnp.sum(d_hidden * n, 0, keepdims=True)
    tiny = small[...] + jnp.where(iota((40, WIDTH), 0) == EXPERTS, line, 0.0)
    tiny = jnp.concatenate([tiny, jnp.zeros((88, WIDTH), F32)], 0)
    whole[:, :, :, :, :, COL_M:COL_END] = (
        jnp.transpose(tiny).astype(BF).reshape(2, 4, 4, 3, 16, 128)
    )
    sums = gather_sums(whole, IN_Q, in_landings, wires, at)
    next(sums)
    d_mid_in.wait()
    grad_in[...] += norm_back(d_hidden, rows[0:1], n, inverse)
    next(up_task)
    finish(gate_task, out_task)
    finish(sums, up_task)
    in_lanes = pl.ds(pl.multiple_of(xh * IN_Q, 128), IN_Q)
    out_lanes = pl.ds(pl.multiple_of(xh * OUT_Q, 128), OUT_Q)
    unit = jnp.concatenate([whole[xx % 2, z, y, part, :, in_lanes] for part in range(3)], 0)
    out_unit = jnp.concatenate([columns[xx % 2, z, y, part, :, out_lanes] for part in range(3)], 0)
    unit = jnp.concatenate([unit, out_unit], 1)
    slots[...] = dot(regroup_back(), unit).astype(BF).reshape(4, 16, STAGE)
    mine = core * 2 + xh
    copies = [
        wires.go(slots.at[peer[0] // 2 * 2 + peer[3]], taken.at[mine], peer)
        for peer in (near, ring(at, 0, 2), diagonal)
    ]
    taken[mine] = slots[xh * 2 + core]
    got(copies)
    tiny = jnp.zeros((12, 128), F32)
    for i in range(2):
        left, right = taken[2 * i].astype(F32)[0:12], taken[2 * i + 1].astype(F32)[0:12]
        g_q[:, 768 * i : 768 * i + 768] = left[:, 0:IN_Q]
        g_k[:, 256 * i : 256 * i + 256] = right[:, 0:256]
        g_v[:, 256 * i : 256 * i + 256] = right[:, 256:512]
        g_o[:, 768 * i : 768 * i + OUT_Q] = left[:, IN_Q:STAGE]
        g_o[:, 768 * i + OUT_Q : 768 * i + 768] = right[:, IN_Q:STAGE]
        tiny += right[:, 512:640]
    g_m[...] = tiny
    wires.close()


def backward_call(
    q, d_o, lse, middle, h1t, small, x, rows, kv, d_mid,
    out_rows, g_out, g_gate, g_up, weights, cosine, sine,
):
    return pl.pallas_call(
        backward_kernel,
        out_shape=[
            shape((ROWS, WIDTH), F32),
            shape((ROWS, WIDTH)),
            shape((12, WIDTH), F32),
            shape((12, 512), F32),
            shape((12, 512), F32),
            shape((12, WIDTH), F32),
            shape((12, 128), F32),
            shape((2, 192, FF), F32),
            shape((2, 192, FF), F32),
        ],
        in_specs=[vm()] * 8 + [hbm()] * 9,
        out_specs=[vm()] * 9,
        scratch_shapes=[
            pltpu.VMEM((2, 4, 4, 3, 16, OUT_H), BF),
            pltpu.VMEM((2, 4, 4, 3, 16, IN_H), BF),
            pltpu.VMEM((4, 2, 2, 128, 512), BF),
            pltpu.VMEM((256, 768), BF),
            pltpu.VMEM((2, ROWS, WIDTH), F32),
            pltpu.VMEM((ROWS, WIDTH), F32),
            pltpu.VMEM((4, 16, STAGE), BF),
            pltpu.VMEM((4, 16, STAGE), BF),
            pltpu.VMEM((256, 128), F32),
            pltpu.VMEM((256, 128), F32),
            pltpu.VMEM((LENGTH, 768), F32),
            pltpu.VMEM((LENGTH, 256), F32),
            pltpu.VMEM((8, 256, 256), BF),
            pltpu.VMEM((768, 256), BF),
            pltpu.VMEM((768, 256), BF),
            pltpu.VMEM((128, 768), BF),
            pltpu.VMEM((128, 768), BF),
            pltpu.VMEM((768, 256), F32),
            *sum_rows_scratch(WIDTH),
            *landing_shapes(OUT_Q),
            *landing_shapes(IN_Q),
            *expert_sum_scratch(192, FF),
            *expert_sum_scratch(192, FF),
            *sum_scratch(128, 512),
            *wire_sems(112),
            pltpu.SemaphoreType.DMA((6,)),
        ],
        compiler_params=pltpu.CompilerParams(
            collective_id=5, has_side_effects=True, vmem_limit_bytes=VMEM_BYTES
        ),
        name="backward",
    )(
        q, d_o, lse, middle, h1t, small, x, rows, kv, d_mid,
        out_rows.reshape(4, 2, 2, 2, 64, WIDTH), g_out, g_gate.reshape(2, 2, 4, 192, FF),
        g_up.reshape(2, 2, 4, 192, FF), weights, cosine, sine,
    )


def tables():
    frequency = np.exp(
        np.arange(HEAD // 2, dtype=np.float32) * np.float32(-2.0 * math.log(10000.0) / HEAD)
    )
    angles = np.arange(LENGTH, dtype=np.float32)[:, None] * frequency[None, :]
    cosine, sine = np.cos(angles), np.sin(angles)
    return (
        np.concatenate([cosine] * 4, 1).astype(np.float32),
        np.concatenate([-sine, sine] * 2, 1).astype(np.float32),
    )


def stage_weights(w_query, key_weight, value_weight, w_out, w_router, gain_attn, gain_ffn):
    small = jnp.concatenate([w_router, gain_attn[:, None], gain_ffn[:, None]], 1)
    small = jnp.pad(small, ((0, 0), (0, IN_H - COL_M - EXPERTS - 2)))
    quarters = []
    for i in range(2):
        own_out = w_out[:, 768 * i : 768 * i + 768]
        quarters.append([w_query[:, 768 * i : 768 * i + 768], own_out[:, :OUT_Q]])
        quarters.append(
            [
                key_weight[:, 256 * i : 256 * i + 256],
                value_weight[:, 256 * i : 256 * i + 256],
                small,
                own_out[:, OUT_Q:],
            ]
        )
    stage = jnp.stack([jnp.concatenate(quarter, 1) for quarter in quarters])
    return jnp.pad(stage, ((0, 0), (0, 4), (0, 0)))


def body(
    block_in, routes, cotangent, gain_attn, w_query, key_weight, value_weight, w_out,
    gain_ffn, w_router, w_gate, w_up, w_down,
):
    cosine, sine = (jnp.asarray(table) for table in tables())
    x, dy = block_in[0], cotangent[0]
    stage = stage_weights(
        w_query, key_weight, value_weight, w_out, w_router, gain_attn, gain_ffn
    )
    (
        rows, router, q, h1t, ot, lse, middle, gates,
        weights, wo, kv, tall, all_dy, gate_full, up_full, down_full,
    ) = forward_call(
        stage, x, routes[0], cosine, sine, dy.reshape(2, 64, WIDTH), w_gate, w_up, w_down
    )
    out_rows, d_rows, g_gate, g_up, g_down = expert_call(tall, all_dy, gate_full, up_full, down_full)
    d_mid, d_o, small, g_out, g_down = token_grad_call(
        d_rows, middle, gates, dy, rows, router, wo, ot, g_down
    )
    grad_in, block_out, g_q, g_k, g_v, g_o, g_m, g_gate, g_up = backward_call(
        q, d_o, lse, middle, h1t, small, x, rows, kv, d_mid,
        out_rows, g_out, g_gate, g_up, weights, cosine, sine,
    )
    return (
        block_out[None],
        grad_in[None],
        g_m[:, EXPERTS],
        g_q,
        g_k,
        g_v,
        g_o,
        g_m[:, EXPERTS + 1],
        g_m[:, 0:EXPERTS],
        g_gate,
        g_up,
        g_down,
    )


def solution(mesh):
    tokens, owned, experts = P("seq", "ctx", None), P(("seq", "ctx"), None), P("ctx", "seq", None)
    vector = P(("seq", "ctx"))
    return jax.shard_map(
        body,
        mesh=mesh,
        in_specs=(
            tokens, tokens, tokens, vector, owned, owned, owned, owned, vector, owned,
            experts, experts, experts,
        ),
        out_specs=(
            tokens, tokens, vector, owned, owned, owned, owned, vector, owned,
            experts, experts, experts,
        ),
        check_vma=False,
    )
```

```python
import functools
import math

import jax
import jax.numpy as jnp
import numpy as np
from jax import lax
from jax.experimental import pallas as pl
from jax.experimental.pallas import tpu as pltpu
from jax.sharding import PartitionSpec as P

WIDTH = 1536
HEADS = 24
KV_HEADS = 8
HEAD = 64
TOPK = 8
ROWS = 128
LENGTH = 2048
EXPERTS = 32
FF = 512
CAP = 48
EPSILON = 1e-06

BF = jnp.bfloat16
F32 = jnp.float32
MESH = pl.DeviceIdType.MESH
VMEM_BYTES = 60 << 20

IN_Q, OUT_Q = 768, 384
IN_H, OUT_H = 2 * IN_Q, 2 * OUT_Q
STAGE = IN_Q + OUT_Q
COL_K, COL_V, COL_M, COL_END = 768, 1024, 1280, 1408
TALL = WIDTH + 128


def vm():
    return pl.BlockSpec(memory_space=pltpu.VMEM)


def hbm():
    return pl.BlockSpec(memory_space=pl.ANY)


def shape(dims, dtype=BF):
    return jax.ShapeDtypeStruct(dims, dtype)


def place():
    seq, ctx = lax.axis_index("seq"), lax.axis_index("ctx")
    return (ctx // 2 % 2 * 2 + seq // 4, ctx // 4, seq % 4, ctx % 2)


def device(x, y, z, core):
    return (x % 2 * 4 + z, (y * 2 + x // 2) * 2 + core)


def ring(at, dim, step):
    x, y, z, core = at
    if dim == 0:
        return ((x + step) % 4, y, z, core)
    if dim == 1:
        return (x, (y + step) % 4, z, core)
    return (x, y, (z + step) % 4, core)


def sibling(at):
    return (at[0], at[1], at[2], 1 - at[3])


def greet(peers):
    barrier = pltpu.get_barrier_semaphore()
    for peer in peers:
        pl.semaphore_signal(barrier, inc=1, device_id=device(*peer), device_id_type=MESH)
    pl.semaphore_wait(barrier, len(peers))


class Wires:
    def __init__(self, send, recv):
        self.send, self.recv, self.used, self.open = send, recv, 0, []

    def go(self, src, dst, peer):
        n = self.used
        self.used += 1
        copy = pltpu.make_async_remote_copy(
            src_ref=src,
            dst_ref=dst,
            send_sem=self.send.at[n],
            recv_sem=self.recv.at[n],
            device_id=device(*peer),
            device_id_type=MESH,
        )
        copy.start()
        self.open.append(copy)
        return copy

    def close(self):
        for copy in self.open:
            copy.wait_send()


def wire_sems(n):
    return [pltpu.SemaphoreType.DMA((n,)), pltpu.SemaphoreType.DMA((n,))]


def got(copies):
    for copy in copies:
        copy.wait_recv()


def dot(a, b):
    return jnp.dot(a, b, preferred_element_type=F32)


def dot_t(a, b):
    return lax.dot_general(a, b, (((1,), (1,)), ((), ())), preferred_element_type=F32)


def t_dot(a, b):
    return lax.dot_general(a, b, (((0,), (0,)), ((), ())), preferred_element_type=F32)


def iota(dims, axis):
    return lax.broadcasted_iota(jnp.int32, dims, axis)


def turn(block, cosine, sine):
    low = iota((block.shape[0], 128), 1) % HEAD < HEAD // 2
    parts = []
    for i in range(block.shape[1] // 128):
        unit = block[:, 128 * i : 128 * i + 128]
        other = jnp.where(low, pltpu.roll(unit, 96, 1), pltpu.roll(unit, 32, 1))
        parts.append(unit * cosine + other * sine)
    return jnp.concatenate(parts, 1)


def regroup():
    r, c = iota((48, 64), 0), iota((48, 64), 1)
    owner = c // 16 % 2 * 2 + c // 32
    hit = (r == owner * 12 + c % 16) & (c % 16 < 12)
    return hit.astype(F32).astype(BF)


def regroup_back():
    r, c = iota((64, 48), 0), iota((64, 48), 1)
    hit = (c == r // 16 * 12 + r % 16) & (r % 16 < 12)
    return hit.astype(F32).astype(BF)


ORDERS = ((0, 1, 2), (1, 2, 0), (2, 0, 1))


def block_of(quarter, part, fixed, at, half=None):
    x, y, z, _ = at
    whole = slice(None)
    columns = (
        pl.ds(pl.multiple_of(x // 2 * quarter, 128), quarter)
        if 0 in fixed
        else pl.ds(0, 2 * quarter)
    )
    spans = {dim: whole for dim in (1, 2)}
    if half is not None:
        spans[1 if 2 in fixed else 2] = pl.ds(2 * half, 2)
    return (
        x % 2 if 0 in fixed else whole,
        z if 2 in fixed else spans[2],
        y if 1 in fixed else spans[1],
        part,
        whole,
        columns,
    )


def spread(ref, quarter, wires, at):
    waits = [[], [], []]

    def send(part, fixed, where, peer, half=None):
        spot = ref.at[block_of(quarter, part, fixed, where, half)]
        waits[part].append(wires.go(spot, spot, peer))

    for phase in range(2):
        for part in range(3):
            got(waits[part])
            waits[part] = []
            fixed = ORDERS[part][phase:]
            for step in (1, 2, 3):
                send(part, fixed, at, ring(at, fixed[0], step))
        yield
    for part in range(3):
        got(waits[part])
        waits[part] = []
        fixed = ORDERS[part][2:]
        for step in (1, 3):
            send(part, fixed, at, ring(at, fixed[0], step))
    yield
    for part in range(3):
        first, waits[part] = waits[part], []
        fixed = ORDERS[part][2:]
        for half, step in ((0, 1), (1, 3)):
            got([first[half]])
            send(part, fixed, ring(at, fixed[0], 4 - step), ring(at, fixed[0], step), half)
    yield
    for part in range(3):
        got(waits[part])


def spread_direct(ref, quarter, wires, at):
    waits = [[], [], []]
    for phase in range(3):
        for part in range(3):
            got(waits[part])
            waits[part] = []
            fixed = ORDERS[part][phase:]
            spot = ref.at[block_of(quarter, part, fixed, at)]
            for step in (1, 2, 3):
                waits[part].append(wires.go(spot, spot, ring(at, fixed[0], step)))
        yield
    for part in range(3):
        got(waits[part])


def finish(*tasks):
    for task in tasks:
        for _ in task:
            pass


def partner(at):
    return (at[0] + 1 - 2 * (at[0] % 2), at[1], at[2], at[3])


def expert_spread(shard, full, wires, at, sem):
    x, _, z, _ = at
    left, right = ring(at, 2, 3), ring(at, 2, 1)
    spot = full.at[:, x % 2, z]
    local = pltpu.make_async_copy(shard, spot, sem)
    local.start()
    pair = wires.go(shard, spot, partner(at))
    yield
    local.wait()
    got([pair])
    spot = full.at[:, :, z]
    a = wires.go(spot, spot, right)
    b = wires.go(spot, spot, left)
    yield
    got([a])
    spot = full.at[0, :, (z + 3) % 4]
    a = wires.go(spot, spot, right)
    got([b])
    spot = full.at[1, :, (z + 1) % 4]
    b = wires.go(spot, spot, left)
    yield
    got([a, b])


def expert_sum_scratch(rows, columns):
    return [
        pltpu.VMEM((2, 2, rows, columns), BF),
        pltpu.VMEM((2, 2, rows, columns), BF),
        pltpu.VMEM((2, 2, rows, columns), BF),
        pltpu.VMEM((2, 2, 2, rows, columns), BF),
        pltpu.VMEM((2, rows, columns), BF),
        pltpu.SemaphoreType.DMA((3,)),
    ]


def expert_sum(grads, result, scratch, wires, at):
    passing, own, halves, pairs, last, lsem = scratch
    z, x_lo = at[2], at[0] % 2
    up, down = ring(at, 2, 1), ring(at, 2, 3)
    above, below, across = (z + 1) % 4, (z + 3) % 4, (z + 2) % 4
    loads = [
        pltpu.make_async_copy(src, dst, lsem.at[i])
        for i, (src, dst) in enumerate(
            (
                (grads.at[0, :, above], passing.at[0]),
                (grads.at[1, :, below], passing.at[1]),
                (grads.at[:, :, z], own),
            )
        )
    ]
    for copy in loads:
        copy.start()
    a = wires.go(grads.at[0, :, across], halves.at[0], up)
    b = wires.go(grads.at[1, :, across], halves.at[1], down)
    direct = [
        wires.go(grads.at[1, :, above], pairs.at[0, 1], up),
        wires.go(grads.at[0, :, below], pairs.at[1, 0], down),
    ]
    yield
    for copy in loads:
        copy.wait()
    got([a])
    for i in range(2):
        passing[0, i] = (passing[0, i].astype(F32) + halves[0, i].astype(F32)).astype(BF)
    a = wires.go(passing.at[0], pairs.at[0, 0], up)
    got([b])
    for i in range(2):
        passing[1, i] = (passing[1, i].astype(F32) + halves[1, i].astype(F32)).astype(BF)
    b = wires.go(passing.at[1], pairs.at[1, 1], down)
    yield
    got([*direct, a, b])
    for e in range(2):
        for i in range(2):
            own[e, i] = (
                own[e, i].astype(F32) + pairs[0, e, i].astype(F32) + pairs[1, e, i].astype(F32)
            ).astype(BF)
    a = wires.go(own.at[:, 1 - x_lo], last, partner(at))
    yield
    got([a])
    for e in range(2):
        result[e] = own[e, x_lo].astype(F32) + last[e].astype(F32)


def ctx_peers(at):
    return [ring(at, 1, 1), ring(at, 1, 2), ring(at, 1, 3), ring(at, 0, 2)]


def all_peers(at):
    return [ring(at, d, s) for d in range(3) for s in (1, 2, 3)]


def share(spot, wires, at, inner=True):
    x, y, _, _ = at
    xh = x // 2
    near, far, up, down = sibling(at), ring(at, 0, 2), ring(at, 1, 1), ring(at, 1, 3)
    above, below, across = (y + 1) % 4, (y + 3) % 4, (y + 2) % 4
    kept = []

    def send(where, peer):
        return wires.go(spot(*where), spot(*where), peer)

    def pass_on(*where):
        if inner:
            kept.append(send(where, near))

    a, b = send((y, xh), up), send((y, xh), down)
    c = send((y, xh), far)
    pass_on(y, xh)
    yield
    got([a])
    a1 = send((below, xh, 0), up)
    got([b])
    b1 = send((above, xh, 1), down)
    pass_on(below, xh)
    pass_on(above, xh)
    got([c])
    a2, b2 = send((y, 1 - xh), up), send((y, 1 - xh), down)
    pass_on(y, 1 - xh)
    yield
    got([a1, b1])
    pass_on(across, xh)
    got([a2])
    a3 = send((below, 1 - xh, 0), up)
    got([b2])
    b3 = send((above, 1 - xh, 1), down)
    pass_on(below, 1 - xh)
    pass_on(above, 1 - xh)
    yield
    got([a3, b3])
    pass_on(across, 1 - xh)
    yield
    got(kept)


def share_rows(ref, wires, at):
    core = at[3]
    return share(lambda y, xh, *half: ref.at[(y, xh, core, *half)], wires, at)


def share_rows_two(ref, wires, at):
    x, y, _, core = at
    xh = x // 2
    near, far = sibling(at), ring(at, 0, 2)

    def pass_on(spot, peer):
        return wires.go(spot, spot, peer)

    inner = [pass_on(ref.at[y, xh, core], near)]
    a = [pass_on(ref.at[y, xh, core, 0], ring(at, 1, s)) for s in (1, 2, 3)]
    b = [pass_on(ref.at[y, xh, core, 1], far)]
    yield
    got(b)
    b = [pass_on(ref.at[y, :, core, 1], ring(at, 1, s)) for s in (1, 2, 3)]
    got(a)
    a = [pass_on(ref.at[:, xh, core, 0], far)]
    inner.append(pass_on(ref.at[y, 1 - xh, core, 1], near))
    for s in (1, 2, 3):
        inner.append(pass_on(ref.at[(y + s) % 4, xh, core, 0], near))
    yield
    got(a)
    inner.append(pass_on(ref.at[:, 1 - xh, core, 0], near))
    got(b)
    for s in (1, 2, 3):
        inner.append(pass_on(ref.at[(y + s) % 4, :, core, 1], near))
    yield
    got(inner)


def ctx_and_sibling(at):
    return ctx_peers(at) + [sibling(at)]


def sum_scratch(rows, columns):
    return [
        pltpu.VMEM((4, rows, columns), BF),
        pltpu.VMEM((3, 2, rows, columns), BF),
        pltpu.VMEM((4, rows, columns), BF),
        pltpu.VMEM((2, rows, columns), BF),
        pltpu.VMEM((3, rows, columns), BF),
        pltpu.VMEM((1, rows, columns), BF),
    ]


def sum_chips(source, scratch, wires, at):
    e0, e1, t0, t1, f0, f1 = scratch
    x, y, _, _ = at
    xh = x // 2
    far = ring(at, 0, 2)
    a = [wires.go(source.at[:, 1 - xh, 0], e0, far)]
    b = [
        wires.go(source.at[(y + s) % 4, :, 1], e1.at[s - 1], ring(at, 1, s)) for s in (1, 2, 3)
    ]
    yield None
    got(a)
    for i in range(4):
        t0[i] = (source[i, xh, 0].astype(F32) + e0[i].astype(F32)).astype(BF)
    a = [wires.go(t0.at[(y + s) % 4], f0.at[s - 1], ring(at, 1, s)) for s in (1, 2, 3)]
    got(b)
    for i in range(2):
        total = source[y, i, 1].astype(F32)
        for s in range(3):
            total += e1[s, i].astype(F32)
        t1[i] = total.astype(BF)
    b = [wires.go(t1.at[1 - xh], f1.at[0], far)]
    yield None
    got(a)
    first = t0[y].astype(F32)
    for s in range(3):
        first += f0[s].astype(F32)
    got(b)
    yield first, t1[xh].astype(F32) + f1[0].astype(F32)


def sum_rows_scratch(columns):
    return [
        pltpu.VMEM((4, 2, 2, 64, columns), BF),
        pltpu.VMEM((4, 2, 2, 64, columns), BF),
        *sum_scratch(64, columns),
        pltpu.SemaphoreType.DMA((2,)),
    ]


def sum_rows(rows, scratch, wires, at):
    landed, own, lsem = scratch[0], scratch[1], scratch[-1]
    core = at[3]
    copies = [
        wires.go(rows.at[:, :, 1 - core, part], landed.at[:, :, part], sibling(at)) for part in range(2)
    ]
    loads = [
        pltpu.make_async_copy(rows.at[:, :, core, part], own.at[:, :, part], lsem.at[part])
        for part in range(2)
    ]
    for copy in loads:
        copy.start()
    yield None
    for part in range(2):
        loads[part].wait()
        got([copies[part]])
        for i in range(4):
            for h in range(2):
                own[i, h, part] = (
                    own[i, h, part].astype(F32) + landed[i, h, part].astype(F32)
                ).astype(BF)
    for result in sum_chips(own, scratch[2:-1], wires, at):
        yield result


def final(steps):
    result = None
    for result in steps:
        pass
    return result


def gather_sums(ref, quarter, landings, wires, at):
    orders = tuple(order[::-1] for order in ORDERS)
    waits = [[], [], []]

    def half_of(part, slot, half):
        span = pl.ds(2 * half, 2)
        where = landings[part][0].at[slot]
        return where.at[span] if orders[part][0] == 0 else where.at[:, span]

    def first(part):
        fixed = orders[part][:1]
        up, across, down = (ring(at, fixed[0], step) for step in (1, 2, 3))
        for half, peer, slot in ((0, up, 0), (1, down, 1)):
            spot = ref.at[block_of(quarter, part, fixed, across, half)]
            waits[part].append(wires.go(spot, half_of(part, 2, half), peer))
        for half, peer, slot in ((1, up, 0), (0, down, 1)):
            spot = ref.at[block_of(quarter, part, fixed, peer, half)]
            waits[part].append(wires.go(spot, half_of(part, slot, half), peer))

    def forward(part):
        fixed = orders[part][:1]
        passing, waits[part] = waits[part][:2], waits[part][2:]
        for half, step in ((0, 1), (1, 3)):
            peer = ring(at, fixed[0], step)
            got([passing[half]])
            index = block_of(quarter, part, fixed, peer, half)
            ref[index] = (
                ref[index].astype(F32) + half_of(part, 2, half)[...].astype(F32)
            ).astype(BF)
            waits[part].append(wires.go(ref.at[index], half_of(part, half, half), peer))

    def send(part, phase):
        fixed = orders[part][: phase + 1]
        for step in (1, 2, 3):
            peer = ring(at, fixed[-1], step)
            spot = ref.at[block_of(quarter, part, fixed, peer)]
            waits[part].append(wires.go(spot, landings[part][phase].at[step - 1], peer))

    def add(part, phase):
        got(waits[part])
        waits[part] = []
        index = block_of(quarter, part, orders[part][: phase + 1], at)
        total = ref[index].astype(F32)
        for step in range(3 if phase else 2):
            total += landings[part][phase][step].astype(F32)
        ref[index] = total.astype(BF)

    for part in range(3):
        first(part)
    yield
    for part in range(3):
        forward(part)
    yield
    for phase in range(3):
        for part in range(3):
            add(part, phase)
            if phase < 2:
                send(part, phase + 1)
        yield


def landing_shapes(quarter):
    found = []
    for order in ORDERS:
        for phase in range(3):
            fixed = order[::-1][: phase + 1]
            dims = [size for size, dim in ((2, 0), (4, 2), (4, 1)) if dim not in fixed]
            found.append(pltpu.VMEM((3, *dims, 16, quarter if 0 in fixed else 2 * quarter), BF))
    return found


def normed(values):
    inverse = lax.rsqrt(jnp.mean(values * values, -1, keepdims=True) + EPSILON)
    return values * inverse, inverse


def attend(q, kv, o, ot, lse, scratch, chip, beside):
    scores, vt, qt, qz, out_t = scratch
    qt[...] = jnp.transpose(q[...].astype(F32) * 0.125).astype(BF)
    for kb in range(8):
        block = kv[kb // 2, kb % 2, :, :, 256:512].reshape(256, 256)
        vt[kb] = jnp.transpose(block.astype(F32)).astype(BF)
    allowed = iota((256, 768), 0) <= iota((256, 768), 1) % 256
    for j in range(4):
        u, half = j // 2, j % 2
        qz[...] = jnp.zeros_like(qz)
        for g in range(3):
            h = 3 * j + g
            qz[64 * half : 64 * half + 64, 256 * g : 256 * g + 256] = qt[64 * h : 64 * h + 64]

        def score(kb):
            rows = pl.ds(pl.multiple_of(kb * 256, 256), 256)
            keys = kv[kb // 2, kb % 2, :, :, 128 * u : 128 * u + 128].reshape(256, 128)
            return rows, dot(keys, qz[...])

        def top(kb, most):
            rows, s = score(kb)
            scores[rows] = s
            return jnp.maximum(most, jnp.max(s.reshape(32, 8, 768), 0))

        most = lax.fori_loop(0, chip, top, jnp.full((8, 768), -1e30, F32))
        rows, s = score(chip)
        s = jnp.where(allowed, s, -1e30)
        scores[rows] = s
        most = jnp.maximum(most, jnp.max(s.reshape(32, 8, 768), 0))
        most = jnp.max(most, 0, keepdims=True)

        def raise_(kb, total):
            rows = pl.ds(pl.multiple_of(kb * 256, 256), 256)
            e = jnp.exp(scores[rows] - most)
            scores[rows] = e
            return total + jnp.sum(e.reshape(32, 8, 768), 0)

        beside[2 * j]()
        total = lax.fori_loop(0, chip + 1, raise_, jnp.zeros((8, 768), F32))
        total = jnp.sum(total, 0, keepdims=True)
        lse[j] = jnp.broadcast_to(most + jnp.log(total), (8, 768))
        inverse = 1.0 / total

        def mix(kb, acc):
            rows = pl.ds(pl.multiple_of(kb * 256, 256), 256)
            p = (scores[rows] * inverse).astype(BF)
            return acc + dot(vt[kb, 64 * j : 64 * j + 64], p)

        acc = lax.fori_loop(0, chip + 1, mix, jnp.zeros((64, 768), F32))
        for g in range(3):
            h = 3 * j + g
            out_t[64 * h : 64 * h + 64] = acc[:, 256 * g : 256 * g + 256]
        beside[2 * j + 1]()
    ot[...] = out_t[...].astype(BF)
    out = jnp.transpose(out_t[...]).astype(BF)
    o[0], o[1] = out[0:128], out[128:256]


def forward_kernel(
    w_query, w_key, w_value, w_out, w_small, x, routes, cosine, sine, dy, w_gate, w_up, w_down,
    rows, router, q, h1t, ot, lse, middle, gates,
    weights_out, wo_out, kv_out, tall, all_dy, gate_full, up_full, down_full,
    weights, columns, wo, kv, both, slots, cos_v, sin_v, o, tall_own, product, arrived,
    scores, vt, qt, qz, out_t, stage, ssem, rsem, lsem,
):
    at = place()
    xx, y, z, core = at
    xh, chip = xx // 2, y * 2 + xx // 2
    near = sibling(at)
    diagonal = sibling(ring(at, 0, 2))
    greet(all_peers(at) + [near, diagonal])
    wires = Wires(ssem, rsem)

    def local(n, src, dst):
        copy = pltpu.make_async_copy(src, dst, lsem.at[n])
        copy.start()
        return copy

    angle = pl.ds(pl.multiple_of(chip * 256, 256), 256)
    angles = [local(0, cosine.at[angle], cos_v), local(1, sine.at[angle], sin_v)]
    dy_in = local(2, dy, all_dy.at[y, xh, core])
    stage[...] = jnp.zeros_like(stage)
    for i in range(2):
        left, right, cut = stage.at[2 * i], stage.at[2 * i + 1], 768 * i + OUT_Q
        left[0:12, 0:IN_Q] = w_query[:, 768 * i : 768 * i + 768]
        left[0:12, IN_Q:STAGE] = w_out[:, 768 * i : cut]
        right[0:12, 0:256] = w_key[:, 256 * i : 256 * i + 256]
        right[0:12, 256:512] = w_value[:, 256 * i : 256 * i + 256]
        right[0:12, 512:640] = w_small[...]
        right[0:12, IN_Q:STAGE] = w_out[:, cut : cut + OUT_Q]
    mine = core * 2 + xh
    first = [
        wires.go(stage.at[peer[3] * 2 + peer[0] // 2], slots.at[mine], peer)
        for peer in (near, ring(at, 0, 2), diagonal)
    ]
    tokens = wires.go(x, both.at[core], near)
    slots[mine] = stage[mine]
    both[core] = x[...]
    got(first)
    unit = dot(regroup(), slots[...].reshape(64, STAGE)).astype(BF)
    in_lanes = pl.ds(pl.multiple_of(xh * IN_Q, 128), IN_Q)
    out_lanes = pl.ds(pl.multiple_of(xh * OUT_Q, 128), OUT_Q)
    for part in range(3):
        weights[xx % 2, z, y, part, :, in_lanes] = unit[16 * part : 16 * part + 16, 0:IN_Q]
        columns[xx % 2, z, y, part, :, out_lanes] = unit[16 * part : 16 * part + 16, IN_Q:STAGE]
    in_task = spread_direct(weights, IN_Q, wires, at)
    out_task = spread_direct(columns, OUT_Q, wires, at)
    dy_task = share_rows_two(all_dy, wires, at)
    gate_task = expert_spread(w_gate, gate_full, wires, at, lsem.at[3])
    up_task = expert_spread(w_up, up_full, wires, at, lsem.at[4])
    down_task = expert_spread(w_down, down_full, wires, at, lsem.at[5])
    next(in_task)
    next(in_task)
    next(gate_task)
    next(in_task)
    finish(in_task)
    weights_kept = local(6, weights, weights_out)
    next(gate_task)
    next(up_task)
    dy_in.wait()
    next(dy_task)

    small = weights[:, :, :, :, :, COL_M:COL_END].reshape(WIDTH, 128)
    router[...] = small
    turned = jnp.transpose(small.astype(F32))
    rows[...] = turned[32:40]
    got([tokens])
    values = both[...].reshape(256, WIDTH).astype(F32)
    hidden = (normed(values)[0] * turned[32:33]).astype(BF)
    made = dot(hidden, weights[:, :, :, :, :, 0:COL_M].reshape(WIDTH, COL_M))
    for copy in angles:
        copy.wait()
    cos, sin = cos_v[...], sin_v[...]
    key = turn(made[:, COL_K:COL_V], cos, sin).astype(BF)
    value = made[:, COL_V:COL_M].astype(BF)
    for part in range(2):
        kv[y, xh, part, :, 0:256] = key[128 * part : 128 * part + 128]
        kv[y, xh, part, :, 256:512] = value[128 * part : 128 * part + 128]
    own = [kv.at[y, xh, 0], kv.at[y, xh, 1]]
    a = [wires.go(own[0], own[0], ring(at, 1, s)) for s in (1, 2, 3)]
    b = [wires.go(own[1], own[1], ring(at, 0, 2))]
    q[...] = turn(made[:, 0:COL_K], cos, sin).astype(BF)
    got(b)
    pair = kv.at[y, :, 1]
    b = [wires.go(pair, pair, ring(at, 1, s)) for s in (1, 2, 3)]
    got(a)
    column = kv.at[:, xh, 0]
    a = [wires.go(column, column, ring(at, 0, 2))]
    next(out_task)
    h1t[...] = jnp.transpose(hidden.astype(F32)).astype(BF)
    next(up_task)
    next(down_task)
    next(out_task)
    got(a)
    got(b)
    kv_kept = local(7, kv, kv_out)
    next(gate_task)

    half = pl.ds(pl.multiple_of(core * 768, 128), 768)
    swap = []

    def swap_out():
        finish(out_task)
        swap.append(wires.go(columns.at[1 - core], wo.at[:, :, :, :, half], near))
        for i in range(4):
            wo[i, :, :, :, half] = columns[core, i]

    beside = [
        lambda: next(out_task),
        lambda: next(down_task),
        lambda: next(dy_task),
        lambda: next(up_task),
        swap_out,
        lambda: None,
        lambda: None,
        lambda: None,
    ]
    attend(q, kv, o, ot, lse, (scores, vt, qt, qz, out_t), chip, beside)
    got(swap)
    wo_kept = local(8, wo, wo_out)

    full = wo[...].reshape(768, WIDTH)
    product[0] = dot(o[1 - core], full)
    swap = wires.go(product.at[0], arrived, near)
    product[1] = dot(o[core], full)
    lane = iota((ROWS, 128), 1)
    named = routes[:, 0:1] == lane
    for i in range(1, TOPK):
        named = named | (routes[:, i : i + 1] == lane)
    got([swap])
    mid = x[...].astype(F32) + product[1] + arrived[...]
    middle[...] = mid
    hidden = (normed(mid)[0] * rows[1:2]).astype(BF)
    logits = jnp.where(named, dot(hidden, router[...]), -jnp.inf)
    raised = jnp.exp(logits - jnp.max(logits, -1, keepdims=True))
    gate = raised / jnp.sum(raised, -1, keepdims=True)
    gates[...] = gate
    high = gate.astype(BF).astype(F32)
    two = high + pltpu.roll(gate - high, EXPERTS, 1)
    for part in range(2):
        cut = slice(64 * part, 64 * part + 64)
        tall_own[part, :, 0:WIDTH] = hidden[cut]
        tall_own[part, :, WIDTH:TALL] = two[cut].astype(BF)
    tall_in = local(9, tall_own, tall.at[y, xh, core])
    tall_task = share_rows(tall, wires, at)
    tall_in.wait()
    next(tall_task)
    next(down_task)
    next(dy_task)
    next(tall_task)
    next(tall_task)
    finish(dy_task, gate_task, up_task)
    finish(tall_task, down_task)
    for copy in (weights_kept, kv_kept, wo_kept):
        copy.wait()
    wires.close()


def forward_call(
    w_query, w_key, w_value, w_out, w_small, x, routes, cosine, sine, dy, w_gate, w_up, w_down
):
    return pl.pallas_call(
        forward_kernel,
        out_shape=[
            shape((8, WIDTH), F32),
            shape((WIDTH, 128)),
            shape((256, 768)),
            shape((WIDTH, 256)),
            shape((768, 256)),
            shape((4, 8, 768), F32),
            shape((ROWS, WIDTH), F32),
            shape((ROWS, 128), F32),
            shape((2, 4, 4, 3, 16, IN_H)),
            shape((4, 4, 3, 16, WIDTH)),
            shape((4, 2, 2, 128, 512)),
            shape((4, 2, 2, 2, 64, TALL)),
            shape((4, 2, 2, 2, 64, WIDTH)),
            shape((2, 2, 4, 192, FF)),
            shape((2, 2, 4, 192, FF)),
            shape((2, 2, 4, 64, WIDTH)),
        ],
        in_specs=[vm()] * 7 + [hbm()] * 2 + [vm()] * 4,
        out_specs=[vm()] * 8 + [hbm()] * 8,
        scratch_shapes=[
            pltpu.VMEM((2, 4, 4, 3, 16, IN_H), BF),
            pltpu.VMEM((2, 4, 4, 3, 16, OUT_H), BF),
            pltpu.VMEM((4, 4, 3, 16, WIDTH), BF),
            pltpu.VMEM((4, 2, 2, 128, 512), BF),
            pltpu.VMEM((2, 128, WIDTH), BF),
            pltpu.VMEM((4, 16, STAGE), BF),
            pltpu.VMEM((256, 128), F32),
            pltpu.VMEM((256, 128), F32),
            pltpu.VMEM((2, 128, 768), BF),
            pltpu.VMEM((2, 64, TALL), BF),
            pltpu.VMEM((2, ROWS, WIDTH), F32),
            pltpu.VMEM((ROWS, WIDTH), F32),
            pltpu.VMEM((LENGTH, 768), F32),
            pltpu.VMEM((8, 256, 256), BF),
            pltpu.VMEM((768, 256), BF),
            pltpu.VMEM((128, 768), BF),
            pltpu.VMEM((768, 256), F32),
            pltpu.VMEM((4, 16, STAGE), BF),
            *wire_sems(144),
            pltpu.SemaphoreType.DMA((10,)),
        ],
        compiler_params=pltpu.CompilerParams(
            collective_id=1, has_side_effects=True, vmem_limit_bytes=VMEM_BYTES
        ),
        name="forward",
    )(w_query, w_key, w_value, w_out, w_small, x, routes, cosine, sine, dy, w_gate, w_up, w_down)


def expert_kernel(
    tall, dy, w_gate, w_up, w_down,
    out_rows, d_rows, g_gate, g_up, g_down,
    big, wide, a_rows, y_rows, r_rows, back, wg, wu, wd, gg, gu, gd, m_s, dg_s, du_s, slot_t, sem,
):
    ctx = lax.axis_index("ctx")
    def copy(n, src, dst):
        made = pltpu.make_async_copy(src, dst, sem.at[n])
        made.start()
        return made

    quarters = [pl.ds(512 * i, 512) for i in range(4)]
    loads = [
        (copy(2 * i, tall.at[rows], big.at[rows]), copy(2 * i + 1, dy.at[rows], wide.at[rows]))
        for i, rows in enumerate(quarters)
    ]
    w_loads = [
        copy(8 + i, src, dst) for i, (src, dst) in enumerate(((w_gate, wg), (w_up, wu), (w_down, wd)))
    ]
    lane = iota((128, 128), 1)
    earlier = (iota((128, 128), 1) < iota((128, 128), 0)).astype(F32).astype(BF)
    slots = iota((CAP, 128), 0).astype(F32)

    def collect(b, _):
        rows = pl.ds(pl.multiple_of(b * 128, 128), 128)
        packed = pl.ds(pl.multiple_of(b * CAP, CAP), CAP)
        both = big[rows, WIDTH:TALL].astype(F32)
        gate = both + pltpu.roll(both, 128 - EXPERTS, 1)
        hot = (gate > 0.0) & (lane < EXPERTS)
        rank = dot(earlier, hot.astype(F32).astype(BF))
        slot = jnp.where(hot, rank, -1.0)
        ranks = slot_t.at[b % 4]
        ranks[...] = jnp.transpose(slot)
        picks = [
            (ranks[pl.ds(2 * ctx + i, 1), :] == slots).astype(F32).astype(BF) for i in range(2)
        ]
        pick = jnp.concatenate(picks, 0)
        found = dot(pick, big[rows, :]).astype(BF)
        grads = dot(pick, wide[rows, :]).astype(BF)
        for i in range(2):
            a_rows[i, packed] = found[CAP * i : CAP * i + CAP]
            y_rows[i, packed] = grads[CAP * i : CAP * i + CAP]
        column = [
            jnp.sum(jnp.where(lane == 2 * ctx + i, slot, 0.0), 1, keepdims=True) for i in range(2)
        ]
        spot = lane.astype(F32)
        put = jnp.where(lane < CAP, column[0], column[1] + CAP) == spot
        back[b] = put.astype(F32).astype(BF)
        return 0

    for i in range(4):
        for load in loads[i]:
            load.wait()
        lax.fori_loop(4 * i, 4 * i + 4, collect, 0, unroll=4)
    for load in w_loads:
        load.wait()
    stores = []
    for e in range(2):
        number = 2 * ctx + e

        def forward(c, _):
            rows = pl.ds(pl.multiple_of(c * 384, 384), 384)
            a = a_rows[e, rows, 0:WIDTH]
            ag, au = dot(a, wg[e]), dot(a, wu[e])
            sg = jax.nn.sigmoid(ag)
            act = ag * sg
            m = (act * au).astype(BF)
            r = dot(m, wd[e]).astype(BF).astype(F32)
            lanes = iota((384, 128), 1)
            hits = (lanes == number) | (lanes == number + EXPERTS)
            gate = jnp.sum(
                jnp.where(hits, a_rows[e, rows, WIDTH:TALL].astype(F32), 0.0), 1, keepdims=True
            )
            y = y_rows[e, rows].astype(F32)
            d_gate = jnp.sum(y * r, 1, keepdims=True)
            r_rows[e, rows] = (gate * r).astype(BF)
            gr = (gate * y).astype(BF)
            y_rows[e, rows] = gr
            dm = dot_t(gr, wd[e])
            m_s[rows] = m
            dg_s[rows] = (dm * au * (sg * (1.0 + ag * (1.0 - sg)))).astype(BF)
            du_s[rows] = (dm * act).astype(BF)
            high = d_gate.astype(BF).astype(F32)
            d_both = jnp.where(
                lanes == number, high, jnp.where(lanes == number + EXPERTS, d_gate - high, 0.0)
            )
            a_rows[e, rows, WIDTH:TALL] = d_both.astype(BF)
            return 0

        lax.fori_loop(0, 2, forward, 0)
        gd[e] = t_dot(m_s[...], y_rows[e]).astype(BF)
        gg[e] = t_dot(a_rows[e, :, 0:WIDTH], dg_s[...]).astype(BF)
        gu[e] = t_dot(a_rows[e, :, 0:WIDTH], du_s[...]).astype(BF)
        for i, (src, dst) in enumerate(((gd, g_down), (gg, g_gate), (gu, g_up))):
            stores.append(copy(11 + 3 * e + i, src.at[e], dst.at[e]))

        def to_tokens(c, _):
            rows = pl.ds(pl.multiple_of(c * 384, 384), 384)
            back_rows = dot_t(dg_s[rows], wg[e]) + dot_t(du_s[rows], wu[e])
            a_rows[e, rows, 0:WIDTH] = back_rows.astype(BF)
            return 0

        lax.fori_loop(0, 2, to_tokens, 0)

    def hand_back(b, _):
        rows = pl.ds(pl.multiple_of(b * 128, 128), 128)
        packed = pl.ds(pl.multiple_of(b * CAP, CAP), CAP)
        put = back[b][:, 0 : 2 * CAP]
        big[rows, :] = dot(put, jnp.concatenate([a_rows[0, packed], a_rows[1, packed]], 0)).astype(BF)
        wide[rows, :] = dot(put, jnp.concatenate([r_rows[0, packed], r_rows[1, packed]], 0)).astype(BF)
        return 0

    for i, rows in enumerate(quarters):
        lax.fori_loop(4 * i, 4 * i + 4, hand_back, 0, unroll=4)
        stores.append(copy(2 * i, big.at[rows], d_rows.at[rows]))
        stores.append(copy(2 * i + 1, wide.at[rows], out_rows.at[rows]))
    for store in stores:
        store.wait()


def expert_call(tall, dy, w_gate, w_up, w_down):
    slots = 16 * CAP
    return pl.pallas_call(
        expert_kernel,
        out_shape=[
            shape((LENGTH, WIDTH)),
            shape((LENGTH, TALL)),
            shape((2, WIDTH, FF)),
            shape((2, WIDTH, FF)),
            shape((2, FF, WIDTH)),
        ],
        in_specs=[hbm()] * 5,
        out_specs=[hbm()] * 5,
        scratch_shapes=[
            pltpu.VMEM((LENGTH, TALL), BF),
            pltpu.VMEM((LENGTH, WIDTH), BF),
            pltpu.VMEM((2, slots, TALL), BF),
            pltpu.VMEM((2, slots, WIDTH), BF),
            pltpu.VMEM((2, slots, WIDTH), BF),
            pltpu.VMEM((16, 128, 128), BF),
            pltpu.VMEM((2, WIDTH, FF), BF),
            pltpu.VMEM((2, WIDTH, FF), BF),
            pltpu.VMEM((2, FF, WIDTH), BF),
            pltpu.VMEM((2, WIDTH, FF), BF),
            pltpu.VMEM((2, WIDTH, FF), BF),
            pltpu.VMEM((2, FF, WIDTH), BF),
            pltpu.VMEM((slots, FF), BF),
            pltpu.VMEM((slots, FF), BF),
            pltpu.VMEM((slots, FF), BF),
            pltpu.VMEM((4, 128, 128), F32),
            pltpu.SemaphoreType.DMA((17,)),
        ],
        compiler_params=pltpu.CompilerParams(vmem_limit_bytes=VMEM_BYTES),
        name="experts",
    )(
        tall.reshape(LENGTH, TALL), dy.reshape(LENGTH, WIDTH), w_gate.reshape(2, WIDTH, FF),
        w_up.reshape(2, WIDTH, FF), w_down.reshape(2, FF, WIDTH),
    )


def split_dot(left, right, form):
    high = left.astype(BF)
    low = (left - high.astype(F32)).astype(BF)
    return form(high, right) + form(low, right)


def norm_back(grad, gain, n, inverse):
    scaled = grad * gain
    return inverse * (scaled - n * jnp.mean(scaled * n, -1, keepdims=True))


def token_grad_kernel(
    d_rows, middle, gates, dy, rows, router, wo, ot, g_down,
    d_mid, d_o, small, g_out, down_sum,
    low, product, *rest,
):
    scratch, expert_scratch, (ssem, rsem) = rest[:9], rest[9:15], rest[15:]
    at = place()
    core = at[3]
    near = sibling(at)
    greet(ctx_and_sibling(at) + [ring(at, 2, 1), ring(at, 2, 3), partner(at)])
    wires = Wires(ssem, rsem)
    steps = sum_rows(d_rows, scratch, wires, at)
    next(steps)
    down_task = expert_sum(g_down, down_sum, expert_scratch, wires, at)
    next(down_task)
    next(steps)
    next(down_task)
    n, inverse = normed(middle[...])
    hidden = (n * rows[1:2]).astype(BF)
    parts = final(steps)
    total = jnp.concatenate(parts, 0)
    d_hidden = total[:, 0:WIDTH]
    both = total[:, WIDTH:TALL]
    gate = gates[...]
    lane = iota((ROWS, 128), 1)
    d_gate = jnp.where(lane < EXPERTS, both + pltpu.roll(both, 128 - EXPERTS, 1), 0.0)
    centre = jnp.sum(gate * d_gate, -1, keepdims=True)
    d_logits = gate * (d_gate - centre)
    d_hidden += split_dot(d_logits, router[...], dot_t)
    d_middle = norm_back(d_hidden, rows[1:2], n, inverse) + dy[...].astype(F32)
    d_low = d_middle.astype(BF)
    low[core] = d_low
    swap = wires.go(low.at[core], low.at[core], near)
    d_mid[...] = d_middle
    grads = split_dot(jnp.transpose(d_logits), hidden, dot)
    line = jnp.sum(d_hidden * n, 0, keepdims=True)
    small[...] = (grads + jnp.where(iota((128, WIDTH), 0) == EXPERTS + 1, line, 0.0))[0:40]
    next(down_task)
    got([swap])
    chip_rows = low[...].reshape(256, WIDTH)
    d_o[...] = dot_t(chip_rows, wo[...].reshape(768, WIDTH)).astype(BF)
    product[...] = dot(ot[...], chip_rows).astype(BF).reshape(4, 4, 3, 16, WIDTH)
    lanes = pl.ds(pl.multiple_of((1 - core) * 768, 128), 768)
    mine = pl.ds(pl.multiple_of(core * 768, 128), 768)
    swap = wires.go(product.at[:, :, :, :, lanes], g_out.at[core], near)
    for i in range(4):
        g_out[core, i] = product[i, :, :, :, mine]
    finish(down_task)
    got([swap])
    wires.close()


def token_grad_call(d_rows, middle, gates, dy, rows, router, wo, ot, g_down):
    return pl.pallas_call(
        token_grad_kernel,
        out_shape=[
            shape((ROWS, WIDTH), F32),
            shape((256, 768)),
            shape((40, WIDTH), F32),
            shape((2, 4, 4, 3, 16, 768)),
            shape((2, 64, WIDTH), F32),
        ],
        in_specs=[hbm()] + [vm()] * 7 + [hbm()],
        out_specs=[vm()] * 5,
        scratch_shapes=[
            pltpu.VMEM((2, ROWS, WIDTH), BF),
            pltpu.VMEM((4, 4, 3, 16, WIDTH), BF),
            *sum_rows_scratch(TALL),
            *expert_sum_scratch(64, WIDTH),
            *wire_sems(24),
        ],
        compiler_params=pltpu.CompilerParams(
            collective_id=4, has_side_effects=True, vmem_limit_bytes=VMEM_BYTES
        ),
        name="token_grad",
    )(
        d_rows.reshape(4, 2, 2, 2, 64, TALL), middle, gates, dy, rows, router, wo, ot,
        g_down.reshape(2, 2, 4, 64, WIDTH),
    )


def attend_back(q, kv, d_o, lse, dq, scratch, chip, turned_back, beside):
    probs, acc, kt, qt, dot_, qz, oz, dqt = scratch
    qt[...] = jnp.transpose(q[...].astype(F32) * 0.125).astype(BF)
    dot_[...] = jnp.transpose(d_o[...].astype(F32)).astype(BF)
    for kb in range(8):
        block = kv[kb // 2, kb % 2, :, :, 0:256].reshape(256, 256)
        kt[kb] = jnp.transpose(block.astype(F32)).astype(BF)
    allowed = iota((256, 768), 0) <= iota((256, 768), 1) % 256
    for j in range(4):
        u, half = j // 2, j % 2
        keys, values = slice(128 * u, 128 * u + 128), slice(256 + 128 * u, 384 + 128 * u)
        if half == 0:
            acc[...] = jnp.zeros_like(acc)
        qz[...] = jnp.zeros_like(qz)
        oz[...] = jnp.zeros_like(oz)
        for g in range(3):
            h = 3 * j + g
            qz[64 * half : 64 * half + 64, 256 * g : 256 * g + 256] = qt[64 * h : 64 * h + 64]
            oz[64 * half : 64 * half + 64, 256 * g : 256 * g + 256] = dot_[64 * h : 64 * h + 64]
        level = lse[j, 0:1]

        def d_share(kb):
            return dot(kv[kb // 2, kb % 2, :, :, values].reshape(256, 128), oz[...])

        def share_of(kb, centre, masked):
            rows = pl.ds(pl.multiple_of(kb * 256, 256), 256)
            block = kv[kb // 2, kb % 2, :, :, keys].reshape(256, 128)
            p = jnp.exp(dot(block, qz[...]) - level)
            if masked:
                p = jnp.where(allowed, p, 0.0)
            probs[rows] = p
            acc[rows, 128:256] += dot_t(p.astype(BF), oz[...])
            return centre + jnp.sum((p * d_share(kb)).reshape(32, 8, 768), 0)

        centre = lax.fori_loop(
            0, chip, functools.partial(share_of, masked=False), jnp.zeros((8, 768), F32)
        )
        beside(4 * j)
        centre = share_of(chip, centre, True)
        centre = jnp.sum(centre, 0, keepdims=True)
        beside(4 * j + 1)

        def back(kb, total):
            rows = pl.ds(pl.multiple_of(kb * 256, 256), 256)
            ds = (probs[rows] * (d_share(kb) - centre)).astype(BF)
            acc[rows, 0:128] += dot_t(ds, qz[...])
            return total + dot(kt[kb, 64 * j : 64 * j + 64], ds)

        total = lax.fori_loop(0, chip, back, jnp.zeros((64, 768), F32))
        beside(4 * j + 2)
        total = back(chip, total)
        for g in range(3):
            h = 3 * j + g
            dqt[64 * h : 64 * h + 64] = total[:, 256 * g : 256 * g + 256] * 0.125
        if half == 1:
            for kb in range(8):
                for part in range(2):
                    row = 256 * kb + 128 * part
                    kv[kb // 2, kb % 2, part, :, keys] = acc[row : row + 128, 0:128].astype(BF)
                    kv[kb // 2, kb % 2, part, :, values] = acc[row : row + 128, 128:256].astype(BF)
        beside(4 * j + 3)
    dq[...] = turned_back(jnp.transpose(dqt[...])).astype(BF)


def backward_kernel(
    q, d_o, lse, middle, h1t, small, x, rows,
    kv_in, d_mid, out_rows, g_out, g_gate, g_up, weights, cosine, sine,
    grad_in, block_out, g_q, g_k, g_v, g_o, g_m, gate_sum, up_sum,
    columns, whole, kv, dq, product, arrived, slots, taken, cos_v, sin_v, *rest,
):
    att_scratch, rest = rest[:8], rest[8:]
    row_scratch, rest = rest[:9], rest[9:]
    out_landings, rest = [rest[3 * i : 3 * i + 3] for i in range(3)], rest[9:]
    in_landings, rest = [rest[3 * i : 3 * i + 3] for i in range(3)], rest[9:]
    gate_scratch, up_scratch, chips, (ssem, rsem, lsem) = rest[:6], rest[6:12], rest[12:18], rest[18:]
    at = place()
    xx, y, z, core = at
    xh, chip = xx // 2, y * 2 + xx // 2
    near = sibling(at)
    diagonal = sibling(ring(at, 0, 2))
    greet(all_peers(at) + [near, diagonal])
    wires = Wires(ssem, rsem)

    def local(n, src, dst):
        copy = pltpu.make_async_copy(src, dst, lsem.at[n])
        copy.start()
        return copy

    columns_in = local(2, g_out, columns)
    kv_loaded = local(4, kv_in, kv)
    d_mid_in = local(5, d_mid, grad_in)
    angle = pl.ds(pl.multiple_of(chip * 256, 256), 256)
    angles = [local(0, cosine.at[angle], cos_v), local(1, sine.at[angle], sin_v)]
    row_task = sum_rows(out_rows, row_scratch, wires, at)
    gate_task = expert_sum(g_gate, gate_sum, gate_scratch, wires, at)
    up_task = expert_sum(g_up, up_sum, up_scratch, wires, at)
    out_task = gather_sums(columns, OUT_Q, out_landings, wires, at)
    next(row_task)
    next(gate_task)
    columns_in.wait()
    next(out_task)

    def put_out():
        parts = final(row_task)
        for part in range(2):
            cut = slice(64 * part, 64 * part + 64)
            block_out[cut] = (middle[cut] + parts[part]).astype(BF)

    steps_beside = {
        3: lambda: next(row_task),
        9: lambda: next(gate_task),
        10: lambda: next(out_task),
        12: lambda: next(row_task),
    }

    def beside(n):
        if n in steps_beside:
            steps_beside[n]()

    def turned_back(values):
        for copy in angles:
            copy.wait()
        return turn(values, cos_v[...], -sin_v[...])

    weights_in = local(3, weights, whole)
    kv_loaded.wait()
    attend_back(q, kv, d_o, lse, dq, att_scratch, chip, turned_back, beside)
    steps = sum_chips(kv, chips, wires, at)
    next(steps)
    n, inverse = normed(x[...].astype(F32))
    next(gate_task)
    next(up_task)
    next(out_task)
    next(steps)
    next(out_task)
    parts = final(steps)
    next(out_task)
    next(up_task)
    total = jnp.concatenate(parts, 0)
    dk = turn(total[:, 0:256], cos_v[...], -sin_v[...]).astype(BF)
    grads = jnp.concatenate([dq[...], dk, total[:, 256:512].astype(BF)], 1)
    weights_in.wait()
    back = dot_t(grads, whole[:, :, :, :, :, 0:COL_M].reshape(WIDTH, COL_M))
    product[0] = back[0:128]
    product[1] = back[128:256]
    swap = wires.go(product.at[1 - core], arrived, near)
    for i in range(8):
        made = dot(h1t[192 * i : 192 * i + 192], grads).astype(BF)
        whole[i // 4, i % 4, :, :, :, 0:COL_M] = made.reshape(4, 3, 16, COL_M)
    whole[:, :, :, :, :, COL_END:IN_H] = jnp.zeros((2, 4, 4, 3, 16, IN_H - COL_END), BF)
    put_out()
    got([swap])
    d_hidden = product[core] + arrived[...]
    line = jnp.sum(d_hidden * n, 0, keepdims=True)
    tiny = small[...] + jnp.where(iota((40, WIDTH), 0) == EXPERTS, line, 0.0)
    tiny = jnp.concatenate([tiny, jnp.zeros((88, WIDTH), F32)], 0)
    whole[:, :, :, :, :, COL_M:COL_END] = (
        jnp.transpose(tiny).astype(BF).reshape(2, 4, 4, 3, 16, 128)
    )
    sums = gather_sums(whole, IN_Q, in_landings, wires, at)
    next(sums)
    d_mid_in.wait()
    grad_in[...] += norm_back(d_hidden, rows[0:1], n, inverse)
    next(up_task)
    finish(gate_task, out_task)
    finish(sums, up_task)
    in_lanes = pl.ds(pl.multiple_of(xh * IN_Q, 128), IN_Q)
    out_lanes = pl.ds(pl.multiple_of(xh * OUT_Q, 128), OUT_Q)
    unit = jnp.concatenate([whole[xx % 2, z, y, part, :, in_lanes] for part in range(3)], 0)
    out_unit = jnp.concatenate([columns[xx % 2, z, y, part, :, out_lanes] for part in range(3)], 0)
    unit = jnp.concatenate([unit, out_unit], 1)
    slots[...] = dot(regroup_back(), unit).astype(BF).reshape(4, 16, STAGE)
    mine = core * 2 + xh
    copies = [
        wires.go(slots.at[peer[0] // 2 * 2 + peer[3]], taken.at[mine], peer)
        for peer in (near, ring(at, 0, 2), diagonal)
    ]
    taken[mine] = slots[xh * 2 + core]
    got(copies)
    tiny = jnp.zeros((12, 128), F32)
    for i in range(2):
        left, right = taken[2 * i].astype(F32)[0:12], taken[2 * i + 1].astype(F32)[0:12]
        g_q[:, 768 * i : 768 * i + 768] = left[:, 0:IN_Q]
        g_k[:, 256 * i : 256 * i + 256] = right[:, 0:256]
        g_v[:, 256 * i : 256 * i + 256] = right[:, 256:512]
        g_o[:, 768 * i : 768 * i + OUT_Q] = left[:, IN_Q:STAGE]
        g_o[:, 768 * i + OUT_Q : 768 * i + 768] = right[:, IN_Q:STAGE]
        tiny += right[:, 512:640]
    g_m[...] = tiny
    wires.close()


def backward_call(
    q, d_o, lse, middle, h1t, small, x, rows, kv, d_mid,
    out_rows, g_out, g_gate, g_up, weights, cosine, sine,
):
    return pl.pallas_call(
        backward_kernel,
        out_shape=[
            shape((ROWS, WIDTH), F32),
            shape((ROWS, WIDTH)),
            shape((12, WIDTH), F32),
            shape((12, 512), F32),
            shape((12, 512), F32),
            shape((12, WIDTH), F32),
            shape((12, 128), F32),
            shape((2, 192, FF), F32),
            shape((2, 192, FF), F32),
        ],
        in_specs=[vm()] * 8 + [hbm()] * 9,
        out_specs=[vm()] * 9,
        scratch_shapes=[
            pltpu.VMEM((2, 4, 4, 3, 16, OUT_H), BF),
            pltpu.VMEM((2, 4, 4, 3, 16, IN_H), BF),
            pltpu.VMEM((4, 2, 2, 128, 512), BF),
            pltpu.VMEM((256, 768), BF),
            pltpu.VMEM((2, ROWS, WIDTH), F32),
            pltpu.VMEM((ROWS, WIDTH), F32),
            pltpu.VMEM((4, 16, STAGE), BF),
            pltpu.VMEM((4, 16, STAGE), BF),
            pltpu.VMEM((256, 128), F32),
            pltpu.VMEM((256, 128), F32),
            pltpu.VMEM((LENGTH, 768), F32),
            pltpu.VMEM((LENGTH, 256), F32),
            pltpu.VMEM((8, 256, 256), BF),
            pltpu.VMEM((768, 256), BF),
            pltpu.VMEM((768, 256), BF),
            pltpu.VMEM((128, 768), BF),
            pltpu.VMEM((128, 768), BF),
            pltpu.VMEM((768, 256), F32),
            *sum_rows_scratch(WIDTH),
            *landing_shapes(OUT_Q),
            *landing_shapes(IN_Q),
            *expert_sum_scratch(192, FF),
            *expert_sum_scratch(192, FF),
            *sum_scratch(128, 512),
            *wire_sems(112),
            pltpu.SemaphoreType.DMA((6,)),
        ],
        compiler_params=pltpu.CompilerParams(
            collective_id=5, has_side_effects=True, vmem_limit_bytes=VMEM_BYTES
        ),
        name="backward",
    )(
        q, d_o, lse, middle, h1t, small, x, rows, kv, d_mid,
        out_rows.reshape(4, 2, 2, 2, 64, WIDTH), g_out, g_gate.reshape(2, 2, 4, 192, FF),
        g_up.reshape(2, 2, 4, 192, FF), weights, cosine, sine,
    )


def results_kernel(*refs):
    half = len(refs) // 2
    for src, dst in zip(refs[:half], refs[half:]):
        dst[...] = src[...]


def results_call(*arrays):
    return pl.pallas_call(
        results_kernel,
        out_shape=[shape(a.shape, a.dtype) for a in arrays],
        in_specs=[vm()] * len(arrays),
        out_specs=[vm()] * len(arrays),
        compiler_params=pltpu.CompilerParams(vmem_limit_bytes=VMEM_BYTES),
        name="results",
    )(*arrays)


def tables():
    frequency = np.exp(
        np.arange(HEAD // 2, dtype=np.float32) * np.float32(-2.0 * math.log(10000.0) / HEAD)
    )
    angles = np.arange(LENGTH, dtype=np.float32)[:, None] * frequency[None, :]
    cosine, sine = np.cos(angles), np.sin(angles)
    return (
        np.concatenate([cosine] * 4, 1).astype(np.float32),
        np.concatenate([-sine, sine] * 2, 1).astype(np.float32),
    )


def body(
    block_in, routes, cotangent, gain_attn, w_query, key_weight, value_weight, w_out,
    gain_ffn, w_router, w_gate, w_up, w_down,
):
    cosine, sine = (jnp.asarray(table) for table in tables())
    x, dy = block_in[0], cotangent[0]
    small = jnp.concatenate([w_router, gain_attn[:, None], gain_ffn[:, None]], 1)
    small = jnp.pad(small, ((0, 0), (0, 128 - EXPERTS - 2)))
    (
        rows, router, q, h1t, ot, lse, middle, gates,
        weights, wo, kv, tall, all_dy, gate_full, up_full, down_full,
    ) = forward_call(
        w_query, key_weight, value_weight, w_out, small, x, routes[0], cosine, sine,
        dy.reshape(2, 64, WIDTH), w_gate, w_up, w_down,
    )
    out_rows, d_rows, g_gate, g_up, g_down = expert_call(tall, all_dy, gate_full, up_full, down_full)
    d_mid, d_o, small, g_out, g_down = token_grad_call(
        d_rows, middle, gates, dy, rows, router, wo, ot, g_down
    )
    grad_in, block_out, g_q, g_k, g_v, g_o, g_m, g_gate, g_up = backward_call(
        q, d_o, lse, middle, h1t, small, x, rows, kv, d_mid,
        out_rows, g_out, g_gate, g_up, weights, cosine, sine,
    )
    block_out, grad_in, g_q, g_k, g_v, g_o, g_gate, g_up, g_down = results_call(
        block_out, grad_in, g_q, g_k, g_v, g_o, g_gate, g_up, g_down
    )
    return (
        block_out[None],
        grad_in[None],
        g_m[:, EXPERTS],
        g_q,
        g_k,
        g_v,
        g_o,
        g_m[:, EXPERTS + 1],
        g_m[:, 0:EXPERTS],
        g_gate,
        g_up,
        g_down,
    )


def solution(mesh):
    tokens, owned, experts = P("seq", "ctx", None), P(("seq", "ctx"), None), P("ctx", "seq", None)
    vector = P(("seq", "ctx"))
    return jax.shard_map(
        body,
        mesh=mesh,
        in_specs=(
            tokens, tokens, tokens, vector, owned, owned, owned, owned, vector, owned,
            experts, experts, experts,
        ),
        out_specs=(
            tokens, tokens, vector, owned, owned, owned, owned, vector, owned,
            experts, experts, experts,
        ),
        check_vma=False,
    )
```

```python
import functools
import math

import jax
import jax.numpy as jnp
import numpy as np
from jax import lax
from jax.experimental import pallas as pl
from jax.experimental.pallas import tpu as pltpu
from jax.sharding import PartitionSpec as P

WIDTH = 1536
HEADS = 24
KV_HEADS = 8
HEAD = 64
TOPK = 8
ROWS = 128
LENGTH = 2048
EXPERTS = 32
FF = 512
CAP = 48
EPSILON = 1e-06

BF = jnp.bfloat16
F32 = jnp.float32
MESH = pl.DeviceIdType.MESH
VMEM_BYTES = 60 << 20

IN_Q, OUT_Q = 768, 384
IN_H, OUT_H = 2 * IN_Q, 2 * OUT_Q
STAGE = IN_Q + OUT_Q
COL_K, COL_V, COL_M, COL_END = 768, 1024, 1280, 1408
TALL = WIDTH + 128


def vm():
    return pl.BlockSpec(memory_space=pltpu.VMEM)


def hbm():
    return pl.BlockSpec(memory_space=pl.ANY)


def shape(dims, dtype=BF):
    return jax.ShapeDtypeStruct(dims, dtype)


def place():
    seq, ctx = lax.axis_index("seq"), lax.axis_index("ctx")
    return (ctx // 2 % 2 * 2 + seq // 4, ctx // 4, seq % 4, ctx % 2)


def device(x, y, z, core):
    return (x % 2 * 4 + z, (y * 2 + x // 2) * 2 + core)


def ring(at, dim, step):
    x, y, z, core = at
    if dim == 0:
        return ((x + step) % 4, y, z, core)
    if dim == 1:
        return (x, (y + step) % 4, z, core)
    return (x, y, (z + step) % 4, core)


def sibling(at):
    return (at[0], at[1], at[2], 1 - at[3])


def greet(peers):
    barrier = pltpu.get_barrier_semaphore()
    for peer in peers:
        pl.semaphore_signal(barrier, inc=1, device_id=device(*peer), device_id_type=MESH)
    pl.semaphore_wait(barrier, len(peers))


class Wires:
    def __init__(self, send, recv):
        self.send, self.recv, self.used, self.open = send, recv, 0, []

    def go(self, src, dst, peer):
        n = self.used
        self.used += 1
        copy = pltpu.make_async_remote_copy(
            src_ref=src,
            dst_ref=dst,
            send_sem=self.send.at[n],
            recv_sem=self.recv.at[n],
            device_id=device(*peer),
            device_id_type=MESH,
        )
        copy.start()
        self.open.append(copy)
        return copy

    def close(self):
        for copy in self.open:
            copy.wait_send()


def wire_sems(n):
    return [pltpu.SemaphoreType.DMA((n,)), pltpu.SemaphoreType.DMA((n,))]


def got(copies):
    for copy in copies:
        copy.wait_recv()


def dot(a, b):
    return jnp.dot(a, b, preferred_element_type=F32)


def dot_t(a, b):
    return lax.dot_general(a, b, (((1,), (1,)), ((), ())), preferred_element_type=F32)


def t_dot(a, b):
    return lax.dot_general(a, b, (((0,), (0,)), ((), ())), preferred_element_type=F32)


def iota(dims, axis):
    return lax.broadcasted_iota(jnp.int32, dims, axis)


def turn(block, cosine, sine):
    low = iota((block.shape[0], 128), 1) % HEAD < HEAD // 2
    parts = []
    for i in range(block.shape[1] // 128):
        unit = block[:, 128 * i : 128 * i + 128]
        other = jnp.where(low, pltpu.roll(unit, 96, 1), pltpu.roll(unit, 32, 1))
        parts.append(unit * cosine + other * sine)
    return jnp.concatenate(parts, 1)


def regroup():
    r, c = iota((48, 64), 0), iota((48, 64), 1)
    owner = c // 16 % 2 * 2 + c // 32
    hit = (r == owner * 12 + c % 16) & (c % 16 < 12)
    return hit.astype(F32).astype(BF)


def regroup_back():
    r, c = iota((64, 48), 0), iota((64, 48), 1)
    hit = (c == r // 16 * 12 + r % 16) & (r % 16 < 12)
    return hit.astype(F32).astype(BF)


ORDERS = ((0, 1, 2), (1, 2, 0), (2, 0, 1))


def block_of(quarter, part, fixed, at, half=None):
    x, y, z, _ = at
    whole = slice(None)
    columns = (
        pl.ds(pl.multiple_of(x // 2 * quarter, 128), quarter)
        if 0 in fixed
        else pl.ds(0, 2 * quarter)
    )
    spans = {dim: whole for dim in (1, 2)}
    if half is not None:
        spans[1 if 2 in fixed else 2] = pl.ds(2 * half, 2)
    return (
        x % 2 if 0 in fixed else whole,
        z if 2 in fixed else spans[2],
        y if 1 in fixed else spans[1],
        part,
        whole,
        columns,
    )


def spread(ref, quarter, wires, at):
    waits = [[], [], []]

    def send(part, fixed, where, peer, half=None):
        spot = ref.at[block_of(quarter, part, fixed, where, half)]
        waits[part].append(wires.go(spot, spot, peer))

    for phase in range(2):
        for part in range(3):
            got(waits[part])
            waits[part] = []
            fixed = ORDERS[part][phase:]
            for step in (1, 2, 3):
                send(part, fixed, at, ring(at, fixed[0], step))
        yield
    for part in range(3):
        got(waits[part])
        waits[part] = []
        fixed = ORDERS[part][2:]
        for step in (1, 3):
            send(part, fixed, at, ring(at, fixed[0], step))
    yield
    for part in range(3):
        first, waits[part] = waits[part], []
        fixed = ORDERS[part][2:]
        for half, step in ((0, 1), (1, 3)):
            got([first[half]])
            send(part, fixed, ring(at, fixed[0], 4 - step), ring(at, fixed[0], step), half)
    yield
    for part in range(3):
        got(waits[part])


def spread_direct(ref, quarter, wires, at):
    waits = [[], [], []]
    for phase in range(3):
        for part in range(3):
            got(waits[part])
            waits[part] = []
            fixed = ORDERS[part][phase:]
            spot = ref.at[block_of(quarter, part, fixed, at)]
            for step in (1, 2, 3):
                waits[part].append(wires.go(spot, spot, ring(at, fixed[0], step)))
        yield
    for part in range(3):
        got(waits[part])


def finish(*tasks):
    for task in tasks:
        for _ in task:
            pass


def partner(at):
    return (at[0] + 1 - 2 * (at[0] % 2), at[1], at[2], at[3])


def expert_spread(shard, full, wires, at, sem):
    x, _, z, _ = at
    left, right = ring(at, 2, 3), ring(at, 2, 1)
    spot = full.at[:, x % 2, z]
    local = pltpu.make_async_copy(shard, spot, sem)
    local.start()
    pair = wires.go(shard, spot, partner(at))
    yield
    local.wait()
    got([pair])
    spot = full.at[:, :, z]
    a = wires.go(spot, spot, right)
    b = wires.go(spot, spot, left)
    yield
    got([a])
    spot = full.at[0, :, (z + 3) % 4]
    a = wires.go(spot, spot, right)
    got([b])
    spot = full.at[1, :, (z + 1) % 4]
    b = wires.go(spot, spot, left)
    yield
    got([a, b])


def expert_sum_scratch(rows, columns):
    return [
        pltpu.VMEM((2, 2, rows, columns), BF),
        pltpu.VMEM((2, 2, rows, columns), BF),
        pltpu.VMEM((2, 2, rows, columns), BF),
        pltpu.VMEM((2, 2, 2, rows, columns), BF),
        pltpu.VMEM((2, rows, columns), BF),
        pltpu.SemaphoreType.DMA((3,)),
    ]


def expert_sum(grads, result, scratch, wires, at):
    passing, own, halves, pairs, last, lsem = scratch
    z, x_lo = at[2], at[0] % 2
    up, down = ring(at, 2, 1), ring(at, 2, 3)
    above, below, across = (z + 1) % 4, (z + 3) % 4, (z + 2) % 4
    loads = [
        pltpu.make_async_copy(src, dst, lsem.at[i])
        for i, (src, dst) in enumerate(
            (
                (grads.at[0, :, above], passing.at[0]),
                (grads.at[1, :, below], passing.at[1]),
                (grads.at[:, :, z], own),
            )
        )
    ]
    for copy in loads:
        copy.start()
    a = wires.go(grads.at[0, :, across], halves.at[0], up)
    b = wires.go(grads.at[1, :, across], halves.at[1], down)
    direct = [
        wires.go(grads.at[1, :, above], pairs.at[0, 1], up),
        wires.go(grads.at[0, :, below], pairs.at[1, 0], down),
    ]
    yield
    for copy in loads:
        copy.wait()
    got([a])
    for i in range(2):
        passing[0, i] = (passing[0, i].astype(F32) + halves[0, i].astype(F32)).astype(BF)
    a = wires.go(passing.at[0], pairs.at[0, 0], up)
    got([b])
    for i in range(2):
        passing[1, i] = (passing[1, i].astype(F32) + halves[1, i].astype(F32)).astype(BF)
    b = wires.go(passing.at[1], pairs.at[1, 1], down)
    yield
    got([*direct, a, b])
    for e in range(2):
        for i in range(2):
            own[e, i] = (
                own[e, i].astype(F32) + pairs[0, e, i].astype(F32) + pairs[1, e, i].astype(F32)
            ).astype(BF)
    a = wires.go(own.at[:, 1 - x_lo], last, partner(at))
    yield
    got([a])
    for e in range(2):
        result[e] = own[e, x_lo].astype(F32) + last[e].astype(F32)


def ctx_peers(at):
    return [ring(at, 1, 1), ring(at, 1, 2), ring(at, 1, 3), ring(at, 0, 2)]


def all_peers(at):
    return [ring(at, d, s) for d in range(3) for s in (1, 2, 3)]


def share(spot, wires, at, inner=True):
    x, y, _, _ = at
    xh = x // 2
    near, far, up, down = sibling(at), ring(at, 0, 2), ring(at, 1, 1), ring(at, 1, 3)
    above, below, across = (y + 1) % 4, (y + 3) % 4, (y + 2) % 4
    kept = []

    def send(where, peer):
        return wires.go(spot(*where), spot(*where), peer)

    def pass_on(*where):
        if inner:
            kept.append(send(where, near))

    a, b = send((y, xh), up), send((y, xh), down)
    c = send((y, xh), far)
    pass_on(y, xh)
    yield
    got([a])
    a1 = send((below, xh, 0), up)
    got([b])
    b1 = send((above, xh, 1), down)
    pass_on(below, xh)
    pass_on(above, xh)
    got([c])
    a2, b2 = send((y, 1 - xh), up), send((y, 1 - xh), down)
    pass_on(y, 1 - xh)
    yield
    got([a1, b1])
    pass_on(across, xh)
    got([a2])
    a3 = send((below, 1 - xh, 0), up)
    got([b2])
    b3 = send((above, 1 - xh, 1), down)
    pass_on(below, 1 - xh)
    pass_on(above, 1 - xh)
    yield
    got([a3, b3])
    pass_on(across, 1 - xh)
    yield
    got(kept)


def share_rows(ref, wires, at):
    core = at[3]
    return share(lambda y, xh, *half: ref.at[(y, xh, core, *half)], wires, at)


def share_rows_two(ref, wires, at):
    x, y, _, core = at
    xh = x // 2
    near, far = sibling(at), ring(at, 0, 2)

    def pass_on(spot, peer):
        return wires.go(spot, spot, peer)

    inner = [pass_on(ref.at[y, xh, core], near)]
    a = [pass_on(ref.at[y, xh, core, 0], ring(at, 1, s)) for s in (1, 2, 3)]
    b = [pass_on(ref.at[y, xh, core, 1], far)]
    yield
    got(b)
    b = [pass_on(ref.at[y, :, core, 1], ring(at, 1, s)) for s in (1, 2, 3)]
    got(a)
    a = [pass_on(ref.at[:, xh, core, 0], far)]
    inner.append(pass_on(ref.at[y, 1 - xh, core, 1], near))
    for s in (1, 2, 3):
        inner.append(pass_on(ref.at[(y + s) % 4, xh, core, 0], near))
    yield
    got(a)
    inner.append(pass_on(ref.at[:, 1 - xh, core, 0], near))
    got(b)
    for s in (1, 2, 3):
        inner.append(pass_on(ref.at[(y + s) % 4, :, core, 1], near))
    yield
    got(inner)


def ctx_and_sibling(at):
    return ctx_peers(at) + [sibling(at)]


def sum_scratch(rows, columns):
    return [
        pltpu.VMEM((4, rows, columns), BF),
        pltpu.VMEM((3, 2, rows, columns), BF),
        pltpu.VMEM((4, rows, columns), BF),
        pltpu.VMEM((2, rows, columns), BF),
        pltpu.VMEM((3, rows, columns), BF),
        pltpu.VMEM((1, rows, columns), BF),
    ]


def sum_chips(source, scratch, wires, at):
    e0, e1, t0, t1, f0, f1 = scratch
    x, y, _, _ = at
    xh = x // 2
    far = ring(at, 0, 2)
    a = [wires.go(source.at[:, 1 - xh, 0], e0, far)]
    b = [
        wires.go(source.at[(y + s) % 4, :, 1], e1.at[s - 1], ring(at, 1, s)) for s in (1, 2, 3)
    ]
    yield None
    got(a)
    for i in range(4):
        t0[i] = (source[i, xh, 0].astype(F32) + e0[i].astype(F32)).astype(BF)
    a = [wires.go(t0.at[(y + s) % 4], f0.at[s - 1], ring(at, 1, s)) for s in (1, 2, 3)]
    got(b)
    for i in range(2):
        total = source[y, i, 1].astype(F32)
        for s in range(3):
            total += e1[s, i].astype(F32)
        t1[i] = total.astype(BF)
    b = [wires.go(t1.at[1 - xh], f1.at[0], far)]
    yield None
    got(a)
    first = t0[y].astype(F32)
    for s in range(3):
        first += f0[s].astype(F32)
    got(b)
    yield first, t1[xh].astype(F32) + f1[0].astype(F32)


def sum_rows_scratch(columns):
    return [
        pltpu.VMEM((4, 2, 2, 64, columns), BF),
        pltpu.VMEM((4, 2, 2, 64, columns), BF),
        *sum_scratch(64, columns),
        pltpu.SemaphoreType.DMA((2,)),
    ]


def sum_rows(rows, scratch, wires, at):
    landed, own, lsem = scratch[0], scratch[1], scratch[-1]
    core = at[3]
    copies = [
        wires.go(rows.at[:, :, 1 - core, part], landed.at[:, :, part], sibling(at)) for part in range(2)
    ]
    loads = [
        pltpu.make_async_copy(rows.at[:, :, core, part], own.at[:, :, part], lsem.at[part])
        for part in range(2)
    ]
    for copy in loads:
        copy.start()
    yield None
    for part in range(2):
        loads[part].wait()
        got([copies[part]])
        for i in range(4):
            for h in range(2):
                own[i, h, part] = (
                    own[i, h, part].astype(F32) + landed[i, h, part].astype(F32)
                ).astype(BF)
    for result in sum_chips(own, scratch[2:-1], wires, at):
        yield result


def final(steps):
    result = None
    for result in steps:
        pass
    return result


def gather_sums(ref, quarter, landings, wires, at):
    orders = tuple(order[::-1] for order in ORDERS)
    waits = [[], [], []]

    def half_of(part, slot, half):
        span = pl.ds(2 * half, 2)
        where = landings[part][0].at[slot]
        return where.at[span] if orders[part][0] == 0 else where.at[:, span]

    def first(part):
        fixed = orders[part][:1]
        up, across, down = (ring(at, fixed[0], step) for step in (1, 2, 3))
        for half, peer, slot in ((0, up, 0), (1, down, 1)):
            spot = ref.at[block_of(quarter, part, fixed, across, half)]
            waits[part].append(wires.go(spot, half_of(part, 2, half), peer))
        for half, peer, slot in ((1, up, 0), (0, down, 1)):
            spot = ref.at[block_of(quarter, part, fixed, peer, half)]
            waits[part].append(wires.go(spot, half_of(part, slot, half), peer))

    def forward(part):
        fixed = orders[part][:1]
        passing, waits[part] = waits[part][:2], waits[part][2:]
        for half, step in ((0, 1), (1, 3)):
            peer = ring(at, fixed[0], step)
            got([passing[half]])
            index = block_of(quarter, part, fixed, peer, half)
            ref[index] = (
                ref[index].astype(F32) + half_of(part, 2, half)[...].astype(F32)
            ).astype(BF)
            waits[part].append(wires.go(ref.at[index], half_of(part, half, half), peer))

    def send(part, phase):
        fixed = orders[part][: phase + 1]
        for step in (1, 2, 3):
            peer = ring(at, fixed[-1], step)
            spot = ref.at[block_of(quarter, part, fixed, peer)]
            waits[part].append(wires.go(spot, landings[part][phase].at[step - 1], peer))

    def add(part, phase):
        got(waits[part])
        waits[part] = []
        index = block_of(quarter, part, orders[part][: phase + 1], at)
        total = ref[index].astype(F32)
        for step in range(3 if phase else 2):
            total += landings[part][phase][step].astype(F32)
        ref[index] = total.astype(BF)

    for part in range(3):
        first(part)
    yield
    for part in range(3):
        forward(part)
    yield
    for phase in range(3):
        for part in range(3):
            add(part, phase)
            if phase < 2:
                send(part, phase + 1)
        yield


def landing_shapes(quarter):
    found = []
    for order in ORDERS:
        for phase in range(3):
            fixed = order[::-1][: phase + 1]
            dims = [size for size, dim in ((2, 0), (4, 2), (4, 1)) if dim not in fixed]
            found.append(pltpu.VMEM((3, *dims, 16, quarter if 0 in fixed else 2 * quarter), BF))
    return found


def normed(values):
    inverse = lax.rsqrt(jnp.mean(values * values, -1, keepdims=True) + EPSILON)
    return values * inverse, inverse


def allowed_last(xh):
    return iota((512, 768), 0) <= iota((512, 768), 1) % 256 + 256 * xh


def attend(q, kv, o, ot, lse, scratch, place_of, beside):
    scores, vt, qt, qz, out_t = scratch
    y, xh = place_of
    qt[...] = jnp.transpose(q[...].astype(F32) * 0.125).astype(BF)
    for kb in range(4):
        block = kv[kb, :, :, :, 256:512].reshape(512, 256)
        vt[kb] = jnp.transpose(block.astype(F32)).astype(BF)
    for j in range(4):
        u, half = j // 2, j % 2
        qz[...] = jnp.zeros_like(qz)
        for g in range(3):
            h = 3 * j + g
            qz[64 * half : 64 * half + 64, 256 * g : 256 * g + 256] = qt[64 * h : 64 * h + 64]

        def score(kb):
            rows = pl.ds(pl.multiple_of(kb * 512, 512), 512)
            keys = kv[kb, :, :, :, 128 * u : 128 * u + 128].reshape(512, 128)
            return rows, dot(keys, qz[...])

        def top(kb, most):
            rows, s = score(kb)
            scores[rows] = s
            return jnp.maximum(most, jnp.max(s.reshape(64, 8, 768), 0))

        most = lax.fori_loop(0, y, top, jnp.full((8, 768), -1e30, F32))
        rows, s = score(y)
        s = jnp.where(allowed_last(xh), s, -1e30)
        scores[rows] = s
        most = jnp.maximum(most, jnp.max(s.reshape(64, 8, 768), 0))
        most = jnp.max(most, 0, keepdims=True)

        def raise_(kb, total):
            rows = pl.ds(pl.multiple_of(kb * 512, 512), 512)
            e = jnp.exp(scores[rows] - most)
            scores[rows] = e
            return total + jnp.sum(e.reshape(64, 8, 768), 0)

        beside[2 * j]()
        total = lax.fori_loop(0, y + 1, raise_, jnp.zeros((8, 768), F32))
        total = jnp.sum(total, 0, keepdims=True)
        lse[j] = jnp.broadcast_to(most + jnp.log(total), (8, 768))
        inverse = 1.0 / total

        def mix(kb, acc):
            rows = pl.ds(pl.multiple_of(kb * 512, 512), 512)
            p = (scores[rows] * inverse).astype(BF)
            return acc + dot(vt[kb, 64 * j : 64 * j + 64], p)

        acc = lax.fori_loop(0, y + 1, mix, jnp.zeros((64, 768), F32))
        for g in range(3):
            h = 3 * j + g
            out_t[64 * h : 64 * h + 64] = acc[:, 256 * g : 256 * g + 256]
        beside[2 * j + 1]()
    ot[...] = out_t[...].astype(BF)
    out = jnp.transpose(out_t[...]).astype(BF)
    o[0], o[1] = out[0:128], out[128:256]


def forward_kernel(
    w_query, w_key, w_value, w_out, w_small, x, routes, cosine, sine, dy, w_gate, w_up, w_down,
    rows, router, q, h1t, ot, lse, middle, gates,
    weights_out, wo_out, kv_out, tall, all_dy, gate_full, up_full, down_full,
    weights, columns, wo, kv, both, slots, cos_v, sin_v, o, tall_own, product, arrived,
    scores, vt, qt, qz, out_t, stage, ssem, rsem, lsem,
):
    at = place()
    xx, y, z, core = at
    xh, chip = xx // 2, y * 2 + xx // 2
    near = sibling(at)
    diagonal = sibling(ring(at, 0, 2))
    greet(all_peers(at) + [near, diagonal])
    wires = Wires(ssem, rsem)

    def local(n, src, dst):
        copy = pltpu.make_async_copy(src, dst, lsem.at[n])
        copy.start()
        return copy

    angle = pl.ds(pl.multiple_of(chip * 256, 256), 256)
    angles = [local(0, cosine.at[angle], cos_v), local(1, sine.at[angle], sin_v)]
    dy_in = local(2, dy, all_dy.at[y, xh, core])
    stage[...] = jnp.zeros_like(stage)
    for i in range(2):
        left, right, cut = stage.at[2 * i], stage.at[2 * i + 1], 768 * i + OUT_Q
        left[0:12, 0:IN_Q] = w_query[:, 768 * i : 768 * i + 768]
        left[0:12, IN_Q:STAGE] = w_out[:, 768 * i : cut]
        right[0:12, 0:256] = w_key[:, 256 * i : 256 * i + 256]
        right[0:12, 256:512] = w_value[:, 256 * i : 256 * i + 256]
        right[0:12, 512:640] = w_small[...]
        right[0:12, IN_Q:STAGE] = w_out[:, cut : cut + OUT_Q]
    mine = core * 2 + xh
    first = [
        wires.go(stage.at[peer[3] * 2 + peer[0] // 2], slots.at[mine], peer)
        for peer in (near, ring(at, 0, 2), diagonal)
    ]
    tokens = wires.go(x, both.at[core], near)
    slots[mine] = stage[mine]
    both[core] = x[...]
    got(first)
    unit = dot(regroup(), slots[...].reshape(64, STAGE)).astype(BF)
    in_lanes = pl.ds(pl.multiple_of(xh * IN_Q, 128), IN_Q)
    out_lanes = pl.ds(pl.multiple_of(xh * OUT_Q, 128), OUT_Q)
    for part in range(3):
        weights[xx % 2, z, y, part, :, in_lanes] = unit[16 * part : 16 * part + 16, 0:IN_Q]
        columns[xx % 2, z, y, part, :, out_lanes] = unit[16 * part : 16 * part + 16, IN_Q:STAGE]
    in_task = spread_direct(weights, IN_Q, wires, at)
    out_task = spread_direct(columns, OUT_Q, wires, at)
    dy_task = share_rows_two(all_dy, wires, at)
    gate_task = expert_spread(w_gate, gate_full, wires, at, lsem.at[3])
    up_task = expert_spread(w_up, up_full, wires, at, lsem.at[4])
    down_task = expert_spread(w_down, down_full, wires, at, lsem.at[5])
    next(in_task)
    next(in_task)
    next(gate_task)
    next(in_task)
    finish(in_task)
    weights_kept = local(6, weights, weights_out)
    next(gate_task)
    next(up_task)
    dy_in.wait()
    next(dy_task)

    small = weights[:, :, :, :, :, COL_M:COL_END].reshape(WIDTH, 128)
    router[...] = small
    turned = jnp.transpose(small.astype(F32))
    rows[...] = turned[32:40]
    got([tokens])
    values = both[...].reshape(256, WIDTH).astype(F32)
    hidden = (normed(values)[0] * turned[32:33]).astype(BF)
    made = dot(hidden, weights[:, :, :, :, :, 0:COL_M].reshape(WIDTH, COL_M))
    for copy in angles:
        copy.wait()
    cos, sin = cos_v[...], sin_v[...]
    key = turn(made[:, COL_K:COL_V], cos, sin).astype(BF)
    value = made[:, COL_V:COL_M].astype(BF)
    for part in range(2):
        kv[y, xh, part, :, 0:256] = key[128 * part : 128 * part + 128]
        kv[y, xh, part, :, 256:512] = value[128 * part : 128 * part + 128]
    own = [kv.at[y, xh, 0], kv.at[y, xh, 1]]
    a = [wires.go(own[0], own[0], ring(at, 1, s)) for s in (1, 2, 3)]
    b = [wires.go(own[1], own[1], ring(at, 0, 2))]
    q[...] = turn(made[:, 0:COL_K], cos, sin).astype(BF)
    got(b)
    pair = kv.at[y, :, 1]
    b = [wires.go(pair, pair, ring(at, 1, s)) for s in (1, 2, 3)]
    got(a)
    column = kv.at[:, xh, 0]
    a = [wires.go(column, column, ring(at, 0, 2))]
    next(out_task)
    h1t[...] = jnp.transpose(hidden.astype(F32)).astype(BF)
    chosen = jnp.transpose(routes[...].astype(F32))
    next(up_task)
    next(down_task)
    next(out_task)
    got(a)
    got(b)
    kv_kept = local(7, kv, kv_out)
    next(gate_task)

    half = pl.ds(pl.multiple_of(core * 768, 128), 768)
    swap = []

    def swap_out():
        finish(out_task)
        swap.append(wires.go(columns.at[1 - core], wo.at[:, :, :, :, half], near))
        for i in range(4):
            wo[i, :, :, :, half] = columns[core, i]

    beside = [
        lambda: next(out_task),
        lambda: next(down_task),
        lambda: next(dy_task),
        lambda: next(up_task),
        swap_out,
        lambda: None,
        lambda: None,
        lambda: None,
    ]
    attend(q, kv, o, ot, lse, (scores, vt, qt, qz, out_t), (y, xh), beside)
    got(swap)
    wo_kept = local(8, wo, wo_out)

    full = wo[...].reshape(768, WIDTH)
    product[0] = dot(o[1 - core], full)
    swap = wires.go(product.at[0], arrived, near)
    product[1] = dot(o[core], full)
    lane = iota((ROWS, 128), 1)
    spots = lane.astype(F32)
    named = chosen[:, 0:1] == spots
    for i in range(1, TOPK):
        named = named | (chosen[:, i : i + 1] == spots)
    got([swap])
    mid = x[...].astype(F32) + product[1] + arrived[...]
    middle[...] = mid
    hidden = (normed(mid)[0] * rows[1:2]).astype(BF)
    logits = jnp.where(named, dot(hidden, router[...]), -jnp.inf)
    raised = jnp.exp(logits - jnp.max(logits, -1, keepdims=True))
    gate = raised / jnp.sum(raised, -1, keepdims=True)
    gates[...] = gate
    high = gate.astype(BF).astype(F32)
    two = high + pltpu.roll(gate - high, EXPERTS, 1)
    for part in range(2):
        cut = slice(64 * part, 64 * part + 64)
        tall_own[part, :, 0:WIDTH] = hidden[cut]
        tall_own[part, :, WIDTH:TALL] = two[cut].astype(BF)
    tall_in = local(9, tall_own, tall.at[y, xh, core])
    tall_task = share_rows(tall, wires, at)
    tall_in.wait()
    next(tall_task)
    next(down_task)
    next(dy_task)
    next(tall_task)
    next(tall_task)
    finish(dy_task, gate_task, up_task)
    finish(tall_task, down_task)
    for copy in (weights_kept, kv_kept, wo_kept):
        copy.wait()
    wires.close()


def forward_call(
    w_query, w_key, w_value, w_out, w_small, x, routes, cosine, sine, dy, w_gate, w_up, w_down
):
    return pl.pallas_call(
        forward_kernel,
        out_shape=[
            shape((8, WIDTH), F32),
            shape((WIDTH, 128)),
            shape((256, 768)),
            shape((WIDTH, 256)),
            shape((768, 256)),
            shape((4, 8, 768), F32),
            shape((ROWS, WIDTH), F32),
            shape((ROWS, 128), F32),
            shape((2, 4, 4, 3, 16, IN_H)),
            shape((4, 4, 3, 16, WIDTH)),
            shape((4, 2, 2, 128, 512)),
            shape((4, 2, 2, 2, 64, TALL)),
            shape((4, 2, 2, 2, 64, WIDTH)),
            shape((2, 2, 4, 192, FF)),
            shape((2, 2, 4, 192, FF)),
            shape((2, 2, 4, 64, WIDTH)),
        ],
        in_specs=[vm()] * 7 + [hbm()] * 2 + [vm()] * 4,
        out_specs=[vm()] * 8 + [hbm()] * 8,
        scratch_shapes=[
            pltpu.VMEM((2, 4, 4, 3, 16, IN_H), BF),
            pltpu.VMEM((2, 4, 4, 3, 16, OUT_H), BF),
            pltpu.VMEM((4, 4, 3, 16, WIDTH), BF),
            pltpu.VMEM((4, 2, 2, 128, 512), BF),
            pltpu.VMEM((2, 128, WIDTH), BF),
            pltpu.VMEM((4, 16, STAGE), BF),
            pltpu.VMEM((256, 128), F32),
            pltpu.VMEM((256, 128), F32),
            pltpu.VMEM((2, 128, 768), BF),
            pltpu.VMEM((2, 64, TALL), BF),
            pltpu.VMEM((2, ROWS, WIDTH), F32),
            pltpu.VMEM((ROWS, WIDTH), F32),
            pltpu.VMEM((LENGTH, 768), F32),
            pltpu.VMEM((4, 256, 512), BF),
            pltpu.VMEM((768, 256), BF),
            pltpu.VMEM((128, 768), BF),
            pltpu.VMEM((768, 256), F32),
            pltpu.VMEM((4, 16, STAGE), BF),
            *wire_sems(144),
            pltpu.SemaphoreType.DMA((10,)),
        ],
        compiler_params=pltpu.CompilerParams(
            collective_id=1, has_side_effects=True, vmem_limit_bytes=VMEM_BYTES
        ),
        name="forward",
    )(w_query, w_key, w_value, w_out, w_small, x, routes, cosine, sine, dy, w_gate, w_up, w_down)


def expert_kernel(
    tall, dy, w_gate, w_up, w_down,
    out_rows, d_rows, g_gate, g_up, g_down,
    big, wide, a_rows, y_rows, r_rows, back, wg, wu, wd, gg, gu, gd, m_s, dg_s, du_s, slot_t, sem,
):
    ctx = lax.axis_index("ctx")
    def copy(n, src, dst):
        made = pltpu.make_async_copy(src, dst, sem.at[n])
        made.start()
        return made

    quarters = [pl.ds(512 * i, 512) for i in range(4)]
    loads = [
        (copy(2 * i, tall.at[rows], big.at[rows]), copy(2 * i + 1, dy.at[rows], wide.at[rows]))
        for i, rows in enumerate(quarters)
    ]
    w_loads = [
        copy(8 + i, src, dst) for i, (src, dst) in enumerate(((w_gate, wg), (w_up, wu), (w_down, wd)))
    ]
    lane = iota((128, 128), 1)
    earlier = (iota((128, 128), 1) < iota((128, 128), 0)).astype(F32).astype(BF)
    slots = iota((CAP, 128), 0).astype(F32)

    def collect(b, _):
        rows = pl.ds(pl.multiple_of(b * 128, 128), 128)
        packed = pl.ds(pl.multiple_of(b * CAP, CAP), CAP)
        both = big[rows, WIDTH:TALL].astype(F32)
        gate = both + pltpu.roll(both, 128 - EXPERTS, 1)
        hot = (gate > 0.0) & (lane < EXPERTS)
        rank = dot(earlier, hot.astype(F32).astype(BF))
        slot = jnp.where(hot, rank, -1.0)
        ranks = slot_t.at[b % 4]
        ranks[...] = jnp.transpose(slot)
        picks = [
            (ranks[pl.ds(2 * ctx + i, 1), :] == slots).astype(F32).astype(BF) for i in range(2)
        ]
        pick = jnp.concatenate(picks, 0)
        found = dot(pick, big[rows, :]).astype(BF)
        grads = dot(pick, wide[rows, :]).astype(BF)
        for i in range(2):
            a_rows[i, packed] = found[CAP * i : CAP * i + CAP]
            y_rows[i, packed] = grads[CAP * i : CAP * i + CAP]
        column = [
            jnp.sum(jnp.where(lane == 2 * ctx + i, slot, 0.0), 1, keepdims=True) for i in range(2)
        ]
        spot = lane.astype(F32)
        put = jnp.where(lane < CAP, column[0], column[1] + CAP) == spot
        back[b] = put.astype(F32).astype(BF)
        return 0

    for i in range(4):
        for load in loads[i]:
            load.wait()
        lax.fori_loop(4 * i, 4 * i + 4, collect, 0, unroll=4)
    for load in w_loads:
        load.wait()
    stores = []
    for e in range(2):
        number = 2 * ctx + e

        def forward(c, _):
            rows = pl.ds(pl.multiple_of(c * 384, 384), 384)
            a = a_rows[e, rows, 0:WIDTH]
            ag, au = dot(a, wg[e]), dot(a, wu[e])
            sg = jax.nn.sigmoid(ag)
            act = ag * sg
            m = (act * au).astype(BF)
            r = dot(m, wd[e]).astype(BF).astype(F32)
            lanes = iota((384, 128), 1)
            hits = (lanes == number) | (lanes == number + EXPERTS)
            gate = jnp.sum(
                jnp.where(hits, a_rows[e, rows, WIDTH:TALL].astype(F32), 0.0), 1, keepdims=True
            )
            y = y_rows[e, rows].astype(F32)
            d_gate = jnp.sum(y * r, 1, keepdims=True)
            r_rows[e, rows] = (gate * r).astype(BF)
            gr = (gate * y).astype(BF)
            y_rows[e, rows] = gr
            dm = dot_t(gr, wd[e])
            m_s[rows] = m
            dg_s[rows] = (dm * au * (sg * (1.0 + ag * (1.0 - sg)))).astype(BF)
            du_s[rows] = (dm * act).astype(BF)
            high = d_gate.astype(BF).astype(F32)
            d_both = jnp.where(
                lanes == number, high, jnp.where(lanes == number + EXPERTS, d_gate - high, 0.0)
            )
            a_rows[e, rows, WIDTH:TALL] = d_both.astype(BF)
            return 0

        lax.fori_loop(0, 2, forward, 0)
        gd[e] = t_dot(m_s[...], y_rows[e]).astype(BF)
        gg[e] = t_dot(a_rows[e, :, 0:WIDTH], dg_s[...]).astype(BF)
        gu[e] = t_dot(a_rows[e, :, 0:WIDTH], du_s[...]).astype(BF)
        for i, (src, dst) in enumerate(((gd, g_down), (gg, g_gate), (gu, g_up))):
            stores.append(copy(11 + 3 * e + i, src.at[e], dst.at[e]))

        def to_tokens(c, _):
            rows = pl.ds(pl.multiple_of(c * 384, 384), 384)
            back_rows = dot_t(dg_s[rows], wg[e]) + dot_t(du_s[rows], wu[e])
            a_rows[e, rows, 0:WIDTH] = back_rows.astype(BF)
            return 0

        lax.fori_loop(0, 2, to_tokens, 0)

    def hand_back(b, _):
        rows = pl.ds(pl.multiple_of(b * 128, 128), 128)
        packed = pl.ds(pl.multiple_of(b * CAP, CAP), CAP)
        put = back[b][:, 0 : 2 * CAP]
        big[rows, :] = dot(put, jnp.concatenate([a_rows[0, packed], a_rows[1, packed]], 0)).astype(BF)
        wide[rows, :] = dot(put, jnp.concatenate([r_rows[0, packed], r_rows[1, packed]], 0)).astype(BF)
        return 0

    for i, rows in enumerate(quarters):
        lax.fori_loop(4 * i, 4 * i + 4, hand_back, 0, unroll=4)
        stores.append(copy(2 * i, big.at[rows], d_rows.at[rows]))
        stores.append(copy(2 * i + 1, wide.at[rows], out_rows.at[rows]))
    for store in stores:
        store.wait()


def expert_call(tall, dy, w_gate, w_up, w_down):
    slots = 16 * CAP
    return pl.pallas_call(
        expert_kernel,
        out_shape=[
            shape((LENGTH, WIDTH)),
            shape((LENGTH, TALL)),
            shape((2, WIDTH, FF)),
            shape((2, WIDTH, FF)),
            shape((2, FF, WIDTH)),
        ],
        in_specs=[hbm()] * 5,
        out_specs=[hbm()] * 5,
        scratch_shapes=[
            pltpu.VMEM((LENGTH, TALL), BF),
            pltpu.VMEM((LENGTH, WIDTH), BF),
            pltpu.VMEM((2, slots, TALL), BF),
            pltpu.VMEM((2, slots, WIDTH), BF),
            pltpu.VMEM((2, slots, WIDTH), BF),
            pltpu.VMEM((16, 128, 128), BF),
            pltpu.VMEM((2, WIDTH, FF), BF),
            pltpu.VMEM((2, WIDTH, FF), BF),
            pltpu.VMEM((2, FF, WIDTH), BF),
            pltpu.VMEM((2, WIDTH, FF), BF),
            pltpu.VMEM((2, WIDTH, FF), BF),
            pltpu.VMEM((2, FF, WIDTH), BF),
            pltpu.VMEM((slots, FF), BF),
            pltpu.VMEM((slots, FF), BF),
            pltpu.VMEM((slots, FF), BF),
            pltpu.VMEM((4, 128, 128), F32),
            pltpu.SemaphoreType.DMA((17,)),
        ],
        compiler_params=pltpu.CompilerParams(vmem_limit_bytes=VMEM_BYTES),
        name="experts",
    )(
        tall.reshape(LENGTH, TALL), dy.reshape(LENGTH, WIDTH), w_gate.reshape(2, WIDTH, FF),
        w_up.reshape(2, WIDTH, FF), w_down.reshape(2, FF, WIDTH),
    )


def split_dot(left, right, form):
    high = left.astype(BF)
    low = (left - high.astype(F32)).astype(BF)
    return form(high, right) + form(low, right)


def norm_back(grad, gain, n, inverse):
    scaled = grad * gain
    return inverse * (scaled - n * jnp.mean(scaled * n, -1, keepdims=True))


def token_grad_kernel(
    d_rows, middle, gates, dy, rows, router, wo, ot, g_down,
    d_mid, d_o, small, g_out, down_sum,
    low, *rest,
):
    scratch, expert_scratch, (ssem, rsem) = rest[:9], rest[9:15], rest[15:]
    at = place()
    core = at[3]
    near = sibling(at)
    greet(ctx_and_sibling(at) + [ring(at, 2, 1), ring(at, 2, 3), partner(at)])
    wires = Wires(ssem, rsem)
    steps = sum_rows(d_rows, scratch, wires, at)
    next(steps)
    down_task = expert_sum(g_down, down_sum, expert_scratch, wires, at)
    next(down_task)
    next(steps)
    n, inverse = normed(middle[...])
    hidden = (n * rows[1:2]).astype(BF)
    next(steps)
    next(down_task)
    parts = final(steps)
    total = jnp.concatenate(parts, 0)
    d_hidden = total[:, 0:WIDTH]
    both = total[:, WIDTH:TALL]
    gate = gates[...]
    lane = iota((ROWS, 128), 1)
    d_gate = jnp.where(lane < EXPERTS, both + pltpu.roll(both, 128 - EXPERTS, 1), 0.0)
    centre = jnp.sum(gate * d_gate, -1, keepdims=True)
    d_logits = gate * (d_gate - centre)
    d_hidden += split_dot(d_logits, router[...], dot_t)
    d_middle = norm_back(d_hidden, rows[1:2], n, inverse) + dy[...].astype(F32)
    d_low = d_middle.astype(BF)
    low[core] = d_low
    swap = wires.go(low.at[core], low.at[core], near)
    d_mid[...] = d_middle
    grads = split_dot(jnp.transpose(d_logits), hidden, dot)
    line = jnp.sum(d_hidden * n, 0, keepdims=True)
    small[...] = (grads + jnp.where(iota((128, WIDTH), 0) == EXPERTS + 1, line, 0.0))[0:40]
    next(down_task)
    got([swap])
    chip_rows = low[...].reshape(256, WIDTH)
    d_o[...] = dot_t(chip_rows, wo[...].reshape(768, WIDTH)).astype(BF)
    g_out[...] = dot(ot[...], chip_rows).astype(BF).reshape(4, 4, 3, 16, WIDTH)
    finish(down_task)
    wires.close()


def token_grad_call(d_rows, middle, gates, dy, rows, router, wo, ot, g_down):
    return pl.pallas_call(
        token_grad_kernel,
        out_shape=[
            shape((ROWS, WIDTH), F32),
            shape((256, 768)),
            shape((40, WIDTH), F32),
            shape((4, 4, 3, 16, WIDTH)),
            shape((2, 64, WIDTH), F32),
        ],
        in_specs=[hbm()] + [vm()] * 7 + [hbm()],
        out_specs=[vm()] * 5,
        scratch_shapes=[
            pltpu.VMEM((2, ROWS, WIDTH), BF),
            *sum_rows_scratch(TALL),
            *expert_sum_scratch(64, WIDTH),
            *wire_sems(24),
        ],
        compiler_params=pltpu.CompilerParams(
            collective_id=4, has_side_effects=True, vmem_limit_bytes=VMEM_BYTES
        ),
        name="token_grad",
    )(
        d_rows.reshape(4, 2, 2, 2, 64, TALL), middle, gates, dy, rows, router, wo, ot,
        g_down.reshape(2, 2, 4, 64, WIDTH),
    )


def attend_back(q, kv, lse, dq, scratch, place_of, turned_back, beside):
    probs, acc, kt, qt, dot_, qz, oz, dqt = scratch
    y, xh = place_of
    qt[...] = jnp.transpose(q[...].astype(F32) * 0.125).astype(BF)
    dot_[...] = jnp.transpose(dq[...].astype(F32)).astype(BF)
    for kb in range(4):
        block = kv[kb, :, :, :, 0:256].reshape(512, 256)
        kt[kb] = jnp.transpose(block.astype(F32)).astype(BF)
    for j in range(4):
        u, half = j // 2, j % 2
        keys, values = slice(128 * u, 128 * u + 128), slice(256 + 128 * u, 384 + 128 * u)
        if half == 0:
            acc[...] = jnp.zeros_like(acc)
        qz[...] = jnp.zeros_like(qz)
        oz[...] = jnp.zeros_like(oz)
        for g in range(3):
            h = 3 * j + g
            qz[64 * half : 64 * half + 64, 256 * g : 256 * g + 256] = qt[64 * h : 64 * h + 64]
            oz[64 * half : 64 * half + 64, 256 * g : 256 * g + 256] = dot_[64 * h : 64 * h + 64]
        level = lse[j, 0:1]

        def d_share(kb):
            return dot(kv[kb, :, :, :, values].reshape(512, 128), oz[...])

        def share_of(kb, centre, masked):
            rows = pl.ds(pl.multiple_of(kb * 512, 512), 512)
            p = jnp.exp(dot(kv[kb, :, :, :, keys].reshape(512, 128), qz[...]) - level)
            if masked:
                p = jnp.where(allowed_last(xh), p, 0.0)
            probs[rows] = p
            acc[rows, 128:256] += dot_t(p.astype(BF), oz[...])
            return centre + jnp.sum((p * d_share(kb)).reshape(64, 8, 768), 0)

        centre = lax.fori_loop(
            0, y, functools.partial(share_of, masked=False), jnp.zeros((8, 768), F32)
        )
        beside(4 * j)
        centre = share_of(y, centre, True)
        centre = jnp.sum(centre, 0, keepdims=True)
        beside(4 * j + 1)

        def back(kb, total):
            rows = pl.ds(pl.multiple_of(kb * 512, 512), 512)
            ds = (probs[rows] * (d_share(kb) - centre)).astype(BF)
            acc[rows, 0:128] += dot_t(ds, qz[...])
            return total + dot(kt[kb, 64 * j : 64 * j + 64], ds)

        total = lax.fori_loop(0, y, back, jnp.zeros((64, 768), F32))
        beside(4 * j + 2)
        total = back(y, total)
        for g in range(3):
            h = 3 * j + g
            dqt[64 * h : 64 * h + 64] = total[:, 256 * g : 256 * g + 256] * 0.125
        if half == 1:
            for kb in range(8):
                for part in range(2):
                    row = 256 * kb + 128 * part
                    kv[kb // 2, kb % 2, part, :, keys] = acc[row : row + 128, 0:128].astype(BF)
                    kv[kb // 2, kb % 2, part, :, values] = acc[row : row + 128, 128:256].astype(BF)
        beside(4 * j + 3)
    dq[...] = turned_back(jnp.transpose(dqt[...])).astype(BF)


def backward_kernel(
    q, lse, h1t, small, x, rows,
    d_o, middle, kv_in, d_mid, out_rows, g_out, g_gate, g_up, weights, cosine, sine,
    grad_in, block_out, g_q, g_k, g_v, g_o, g_m, gate_sum, up_sum,
    columns, whole, kv, dq, product, arrived, slots, taken, cos_v, sin_v, *rest,
):
    att_scratch, rest = rest[:8], rest[8:]
    row_scratch, rest = rest[:9], rest[9:]
    out_landings, rest = [rest[3 * i : 3 * i + 3] for i in range(3)], rest[9:]
    in_landings, rest = [rest[3 * i : 3 * i + 3] for i in range(3)], rest[9:]
    gate_scratch, up_scratch, chips, (ssem, rsem, lsem) = rest[:6], rest[6:12], rest[12:18], rest[18:]
    at = place()
    xx, y, z, core = at
    xh, chip = xx // 2, y * 2 + xx // 2
    near = sibling(at)
    diagonal = sibling(ring(at, 0, 2))
    greet(all_peers(at) + [near, diagonal])
    wires = Wires(ssem, rsem)

    def local(n, src, dst):
        copy = pltpu.make_async_copy(src, dst, lsem.at[n])
        copy.start()
        return copy

    mine = pl.ds(pl.multiple_of(core * 768, 128), 768)
    theirs = pl.ds(pl.multiple_of((1 - core) * 768, 128), 768)
    columns_in = local(2, g_out.at[:, :, :, :, mine], columns.at[core])
    columns_swap = wires.go(g_out.at[:, :, :, :, theirs], columns.at[core], near)
    kv_loaded = local(4, kv_in, kv)
    d_mid_in = local(5, d_mid, grad_in)
    d_o_in = local(6, d_o, dq)
    middle_in = local(7, middle, product.at[0])
    angle = pl.ds(pl.multiple_of(chip * 256, 256), 256)
    angles = [local(0, cosine.at[angle], cos_v), local(1, sine.at[angle], sin_v)]
    row_task = sum_rows(out_rows, row_scratch, wires, at)
    gate_task = expert_sum(g_gate, gate_sum, gate_scratch, wires, at)
    up_task = expert_sum(g_up, up_sum, up_scratch, wires, at)
    out_task = gather_sums(columns, OUT_Q, out_landings, wires, at)
    next(row_task)
    next(gate_task)

    def put_out():
        parts = final(row_task)
        middle_in.wait()
        for part in range(2):
            cut = slice(64 * part, 64 * part + 64)
            block_out[cut] = (product[0, cut] + parts[part]).astype(BF)

    def start_out():
        columns_in.wait()
        got([columns_swap])
        next(out_task)

    steps_beside = {
        1: start_out,
        3: lambda: next(row_task),
        9: lambda: next(gate_task),
        10: lambda: next(out_task),
        12: lambda: next(row_task),
    }

    def beside(n):
        if n in steps_beside:
            steps_beside[n]()

    def turned_back(values):
        for copy in angles:
            copy.wait()
        return turn(values, cos_v[...], -sin_v[...])

    weights_in = local(3, weights, whole)
    kv_loaded.wait()
    d_o_in.wait()
    attend_back(q, kv, lse, dq, att_scratch, (y, xh), turned_back, beside)
    steps = sum_chips(kv, chips, wires, at)
    next(steps)
    n, inverse = normed(x[...].astype(F32))
    next(gate_task)
    next(up_task)
    next(out_task)
    next(steps)
    next(out_task)
    parts = final(steps)
    next(out_task)
    next(up_task)
    total = jnp.concatenate(parts, 0)
    dk = turn(total[:, 0:256], cos_v[...], -sin_v[...]).astype(BF)
    grads = jnp.concatenate([dq[...], dk, total[:, 256:512].astype(BF)], 1)
    put_out()
    weights_in.wait()
    back = dot_t(grads, whole[:, :, :, :, :, 0:COL_M].reshape(WIDTH, COL_M))
    product[0] = back[0:128]
    product[1] = back[128:256]
    swap = wires.go(product.at[1 - core], arrived, near)
    for i in range(8):
        made = dot(h1t[192 * i : 192 * i + 192], grads).astype(BF)
        whole[i // 4, i % 4, :, :, :, 0:COL_M] = made.reshape(4, 3, 16, COL_M)
    whole[:, :, :, :, :, COL_END:IN_H] = jnp.zeros((2, 4, 4, 3, 16, IN_H - COL_END), BF)
    got([swap])
    d_hidden = product[core] + arrived[...]
    line = jnp.sum(d_hidden * n, 0, keepdims=True)
    tiny = small[...] + jnp.where(iota((40, WIDTH), 0) == EXPERTS, line, 0.0)
    tiny = jnp.concatenate([tiny, jnp.zeros((88, WIDTH), F32)], 0)
    whole[:, :, :, :, :, COL_M:COL_END] = (
        jnp.transpose(tiny).astype(BF).reshape(2, 4, 4, 3, 16, 128)
    )
    sums = gather_sums(whole, IN_Q, in_landings, wires, at)
    next(sums)
    d_mid_in.wait()
    grad_in[...] += norm_back(d_hidden, rows[0:1], n, inverse)
    next(up_task)
    finish(gate_task, out_task)
    finish(sums, up_task)
    in_lanes = pl.ds(pl.multiple_of(xh * IN_Q, 128), IN_Q)
    out_lanes = pl.ds(pl.multiple_of(xh * OUT_Q, 128), OUT_Q)
    unit = jnp.concatenate([whole[xx % 2, z, y, part, :, in_lanes] for part in range(3)], 0)
    out_unit = jnp.concatenate([columns[xx % 2, z, y, part, :, out_lanes] for part in range(3)], 0)
    unit = jnp.concatenate([unit, out_unit], 1)
    slots[...] = dot(regroup_back(), unit).astype(BF).reshape(4, 16, STAGE)
    mine = core * 2 + xh
    copies = [
        wires.go(slots.at[peer[0] // 2 * 2 + peer[3]], taken.at[mine], peer)
        for peer in (near, ring(at, 0, 2), diagonal)
    ]
    taken[mine] = slots[xh * 2 + core]
    got(copies)
    tiny = jnp.zeros((12, 128), F32)
    for i in range(2):
        left, right = taken[2 * i].astype(F32)[0:12], taken[2 * i + 1].astype(F32)[0:12]
        g_q[:, 768 * i : 768 * i + 768] = left[:, 0:IN_Q]
        g_k[:, 256 * i : 256 * i + 256] = right[:, 0:256]
        g_v[:, 256 * i : 256 * i + 256] = right[:, 256:512]
        g_o[:, 768 * i : 768 * i + OUT_Q] = left[:, IN_Q:STAGE]
        g_o[:, 768 * i + OUT_Q : 768 * i + 768] = right[:, IN_Q:STAGE]
        tiny += right[:, 512:640]
    g_m[...] = tiny
    wires.close()


def backward_call(
    q, lse, h1t, small, x, rows, d_o, middle, kv, d_mid,
    out_rows, g_out, g_gate, g_up, weights, cosine, sine,
):
    return pl.pallas_call(
        backward_kernel,
        out_shape=[
            shape((ROWS, WIDTH), F32),
            shape((ROWS, WIDTH)),
            shape((12, WIDTH), F32),
            shape((12, 512), F32),
            shape((12, 512), F32),
            shape((12, WIDTH), F32),
            shape((12, 128), F32),
            shape((2, 192, FF), F32),
            shape((2, 192, FF), F32),
        ],
        in_specs=[vm()] * 6 + [hbm()] * 11,
        out_specs=[vm()] * 9,
        scratch_shapes=[
            pltpu.VMEM((2, 4, 4, 3, 16, OUT_H), BF),
            pltpu.VMEM((2, 4, 4, 3, 16, IN_H), BF),
            pltpu.VMEM((4, 2, 2, 128, 512), BF),
            pltpu.VMEM((256, 768), BF),
            pltpu.VMEM((2, ROWS, WIDTH), F32),
            pltpu.VMEM((ROWS, WIDTH), F32),
            pltpu.VMEM((4, 16, STAGE), BF),
            pltpu.VMEM((4, 16, STAGE), BF),
            pltpu.VMEM((256, 128), F32),
            pltpu.VMEM((256, 128), F32),
            pltpu.VMEM((LENGTH, 768), F32),
            pltpu.VMEM((LENGTH, 256), F32),
            pltpu.VMEM((4, 256, 512), BF),
            pltpu.VMEM((768, 256), BF),
            pltpu.VMEM((768, 256), BF),
            pltpu.VMEM((128, 768), BF),
            pltpu.VMEM((128, 768), BF),
            pltpu.VMEM((768, 256), F32),
            *sum_rows_scratch(WIDTH),
            *landing_shapes(OUT_Q),
            *landing_shapes(IN_Q),
            *expert_sum_scratch(192, FF),
            *expert_sum_scratch(192, FF),
            *sum_scratch(128, 512),
            *wire_sems(112),
            pltpu.SemaphoreType.DMA((8,)),
        ],
        compiler_params=pltpu.CompilerParams(
            collective_id=5, has_side_effects=True, vmem_limit_bytes=63 << 20
        ),
        name="backward",
    )(
        q, lse, h1t, small, x, rows, d_o, middle, kv, d_mid,
        out_rows.reshape(4, 2, 2, 2, 64, WIDTH), g_out, g_gate.reshape(2, 2, 4, 192, FF),
        g_up.reshape(2, 2, 4, 192, FF), weights, cosine, sine,
    )


def results_kernel(*refs):
    half = len(refs) // 2
    for src, dst in zip(refs[:half], refs[half:]):
        dst[...] = src[...]


def results_call(*arrays):
    return pl.pallas_call(
        results_kernel,
        out_shape=[shape(a.shape, a.dtype) for a in arrays],
        in_specs=[vm()] * len(arrays),
        out_specs=[vm()] * len(arrays),
        compiler_params=pltpu.CompilerParams(vmem_limit_bytes=VMEM_BYTES),
        name="results",
    )(*arrays)


def tables():
    frequency = np.exp(
        np.arange(HEAD // 2, dtype=np.float32) * np.float32(-2.0 * math.log(10000.0) / HEAD)
    )
    angles = np.arange(LENGTH, dtype=np.float32)[:, None] * frequency[None, :]
    cosine, sine = np.cos(angles), np.sin(angles)
    return (
        np.concatenate([cosine] * 4, 1).astype(np.float32),
        np.concatenate([-sine, sine] * 2, 1).astype(np.float32),
    )


def body(
    block_in, routes, cotangent, gain_attn, w_query, key_weight, value_weight, w_out,
    gain_ffn, w_router, w_gate, w_up, w_down,
):
    cosine, sine = (jnp.asarray(table) for table in tables())
    x, dy = block_in[0], cotangent[0]
    small = jnp.concatenate([w_router, gain_attn[:, None], gain_ffn[:, None]], 1)
    small = jnp.pad(small, ((0, 0), (0, 128 - EXPERTS - 2)))
    (
        rows, router, q, h1t, ot, lse, middle, gates,
        weights, wo, kv, tall, all_dy, gate_full, up_full, down_full,
    ) = forward_call(
        w_query, key_weight, value_weight, w_out, small, x, routes[0].T, cosine, sine,
        dy.reshape(2, 64, WIDTH), w_gate, w_up, w_down,
    )
    out_rows, d_rows, g_gate, g_up, g_down = expert_call(tall, all_dy, gate_full, up_full, down_full)
    d_mid, d_o, small, g_out, g_down = token_grad_call(
        d_rows, middle, gates, dy, rows, router, wo, ot, g_down
    )
    grad_in, block_out, g_q, g_k, g_v, g_o, g_m, g_gate, g_up = backward_call(
        q, lse, h1t, small, x, rows, d_o, middle, kv, d_mid,
        out_rows, g_out, g_gate, g_up, weights, cosine, sine,
    )
    block_out, grad_in, g_q, g_k, g_v, g_o, g_gate, g_up, g_down = results_call(
        block_out, grad_in, g_q, g_k, g_v, g_o, g_gate, g_up, g_down
    )
    return (
        block_out[None],
        grad_in[None],
        g_m[:, EXPERTS],
        g_q,
        g_k,
        g_v,
        g_o,
        g_m[:, EXPERTS + 1],
        g_m[:, 0:EXPERTS],
        g_gate,
        g_up,
        g_down,
    )


def solution(mesh):
    tokens, owned, experts = P("seq", "ctx", None), P(("seq", "ctx"), None), P("ctx", "seq", None)
    vector = P(("seq", "ctx"))
    return jax.shard_map(
        body,
        mesh=mesh,
        in_specs=(
            tokens, tokens, tokens, vector, owned, owned, owned, owned, vector, owned,
            experts, experts, experts,
        ),
        out_specs=(
            tokens, tokens, vector, owned, owned, owned, owned, vector, owned,
            experts, experts, experts,
        ),
        check_vma=False,
    )
```
